256 devices in a mesh: angle: 8 (over y, x_hi), gz: 32 (over x_lo, z, core).
Axes of the slice: x: 4 (x_hi: 2, x_lo: 2; x = x_hi * 2 + x_lo), y: 4, z: 8, core: 2. Of those that a mesh axis runs over, the one named last changes fastest.
Arguments:
- volume: bfloat16 [32, 512, 512], P('gz'), may hold values from -0.3984375 to 0.3984375
- probe: float32 [8, 2, 128, 128], replicated, may hold values from -0.046875 to 0.046875
- measured: float32 [8, 32, 128, 128], P('angle', 'gz'), may hold values from 2 to 40
- angle_index: int32 [8], P('angle'), may hold values from 0 to 7, each once
- row_offset: int32 [8, 32], P('angle', 'gz'), may hold values from -64 to -32, as said below
- col_offset: int32 [8, 32], P('angle', 'gz'), may hold values from 0 to 384, as said below
Outputs:
- volume_update: float32 [32, 512, 512], P('gz', 'angle')
- probe_update: float32 [8, 2, 128, 128], replicated
The draws below stay inside these ranges and needn't reach their ends.
Inputs may be any that keep to these rules, and one draw needn't show every extreme that they name: `row_offset`: windows may reach 64 rows past either end of the projection; both ends are used. `col_offset`: both ends are used. `angle_index`: each angle number once.
All inputs are finite; a program needn't handle non-finite values.
Results may differ from the reference program's by a relative error of at most 0.0005.
Values sent between devices are 32-bit elements; how exact they have to be, the bound alone decides.
No kernel may reach another device: no remote copies, remote signals or barrier semaphores. Data moves between devices by JAX's collectives and lax.ppermute only.
A program may use at most 64 MiB of HBM per device.

```python
import math
import jax
import jax.numpy as jnp
from jax import lax

NX = 512
NY = 512
WIN = 128
MODES = 8
NZ = 32
ANGLES = 8
POS = 32


def draw_row_offset(key, part):
    key = jax.random.fold_in(key, 11)
    half = WIN // 2
    values = jax.random.randint(key, (ANGLES, POS), -half, NZ - half + 1)
    values = values.at[0, 0].set(NZ - half)
    return values.at[ANGLES - 1, POS - 1].set(-half)


def draw_col_offset(key, part):
    key = jax.random.fold_in(key, 23)
    values = jax.random.randint(key, (ANGLES, POS), 0, NY - WIN + 1)
    values = values.at[1, 0].set(NY - WIN)
    return values.at[ANGLES - 2, POS - 1].set(0)


def block_levels(rng, shape, shards, least, largest):
    gain, own = 1.0, jax.random.fold_in(rng, 6)
    for dim, shards_of in shards:
        heights = jnp.exp(jax.random.uniform(jax.random.fold_in(own, dim), (shards_of,), jnp.float32, least / len(shards), largest / len(shards)))
        gain = gain * jnp.repeat(heights, shape[dim] // shards_of).reshape([-1 if axis == dim else 1 for axis in range(len(shape))])
    return gain


def noise(stream_key, extent, scale, reach, shards=(), kind=jnp.bfloat16):
    loudness = block_levels(stream_key, extent, shards, -0.22, 0.18) if shards else 1.0
    drawn = jax.random.normal(stream_key, extent, jnp.float32) * scale * loudness
    return jnp.minimum(jnp.maximum(drawn, -reach), reach).astype(kind)


def setup_inputs(seed: int = 0) -> dict:
    seeds = jax.random.split(jax.random.key(seed), 7)
    volume = noise(seeds[0], (NZ, NX, NY), 0.05, 0.3984375, ((0, 32),))
    probe = noise(seeds[1], (MODES, 2, WIN, WIN), (WIN * WIN) ** -0.5, 0.046875, (), jnp.float32)
    measured = jnp.clip(jnp.exp(math.log(40.0) - 2.9957323 * jax.random.uniform(seeds[2], (ANGLES, POS, WIN, WIN), jnp.float32) ** block_levels(seeds[2], (ANGLES, POS, WIN, WIN), ((0, 8), (1, 32)), -0.2, 0.2)), 2.0, 40.0)
    angle_index = jax.random.permutation(seeds[3], ANGLES).astype(jnp.int32)
    row_offset = draw_row_offset(jax.random.fold_in(seeds[6], 71), 0)
    col_offset = draw_col_offset(jax.random.fold_in(seeds[6], 71), 0)
    return {"volume": volume, "probe": probe, "measured": measured, "angle_index": angle_index, "row_offset": row_offset, "col_offset": col_offset}


def signed_freq(count):
    index = jnp.arange(count, dtype=jnp.int32)
    return jnp.where(index < count // 2, index, index - count).astype(jnp.float32)

def shear_phases(angle_number):
    theta = math.pi * (angle_number.astype(jnp.float32) + 0.5) / ANGLES - math.pi / 2
    shear_x = -jnp.tan(theta / 2)
    shear_y = jnp.sin(theta)
    cells_y = jnp.arange(NY, dtype=jnp.int32).astype(jnp.float32) - NY / 2
    cells_x = jnp.arange(NX, dtype=jnp.int32).astype(jnp.float32) - NX / 2
    phase_one = -2.0 * math.pi * signed_freq(NX)[:, None] * shear_x * cells_y[None, :] / NX
    phase_two = -2.0 * math.pi * signed_freq(NY)[:, None] * shear_y * cells_x[None, :] / NY
    return (phase_one, phase_two)

def project_block(block, phase_one, phase_two):
    spectrum = jnp.fft.fft(block, axis=1) * jnp.exp(1j * phase_one)[None]
    sheared = jnp.real(jnp.fft.ifft(spectrum, axis=1))
    beam = jnp.fft.fft(sheared, axis=2)
    summed = lax.optimization_barrier(jnp.sum(beam * jnp.exp(1j * phase_two).T[None], axis=1))
    return jnp.real(jnp.fft.ifft(summed, axis=-1))

def backproject_block(grad_rows, phase_one, phase_two):
    cbar = jnp.fft.fft(grad_rows, axis=-1) / NY
    spread = cbar[:, None, :] * jnp.exp(-1j * phase_two).T[None]
    sheared = jnp.real(jnp.fft.ifft(spread, axis=2)) * NY
    spectrum = jnp.fft.fft(sheared, axis=1) / NX * jnp.exp(-1j * phase_one)[None]
    return jnp.real(jnp.fft.ifft(spectrum, axis=1)) * NX

def window_terms(proj_rows, probe_modes, measure, rows_here, cols_here):
    half = WIN // 2
    padded = jnp.pad(proj_rows, ((half, half), (0, 0)))

    def cut_patch(row_start, col_start):
        return lax.dynamic_slice(padded, (row_start + half, col_start), (WIN, WIN))
    patches = jax.vmap(cut_patch)(rows_here, cols_here)
    objects = jnp.exp(1j * patches)
    far = jnp.fft.fft2(probe_modes[None] * objects[:, None])
    intensity = lax.optimization_barrier(jnp.sum(jnp.real(far * jnp.conj(far)), axis=1))
    factor = (1.0 - jnp.sqrt(measure + 1.0) / jnp.sqrt(intensity + 1.0)) / WIN
    back = WIN * WIN * jnp.fft.ifft2(factor[:, None] * far)
    probe_grad = lax.optimization_barrier(jnp.sum(jnp.conj(objects)[:, None] * back, axis=0))
    object_grad = lax.optimization_barrier(jnp.sum(jnp.conj(probe_modes)[None] * back, axis=1))
    patch_grad = jnp.imag(object_grad * jnp.conj(objects))

    def add_patch(index, buffer):
        start_row = rows_here[index] + half
        start_col = cols_here[index]
        current = lax.dynamic_slice(buffer, (start_row, start_col), (WIN, WIN))
        return lax.dynamic_update_slice(buffer, current + patch_grad[index], (start_row, start_col))
    buffer = lax.fori_loop(0, POS, add_patch, jnp.zeros(padded.shape, jnp.float32))
    return (buffer[half:half + NZ], jnp.stack([jnp.real(probe_grad), jnp.imag(probe_grad)], axis=1))

def reference(volume, probe, measured, angle_index, row_offset, col_offset):
    field = volume.astype(jnp.float32)
    block_rows = math.gcd(NZ, 16)
    blocks = field.reshape(NZ // block_rows, block_rows, NX, NY)
    probe_modes = probe[:, 0] + 1j * probe[:, 1]

    def per_angle(carry, inputs):
        volume_acc, probe_acc = carry
        angle_number, measure, rows_here, cols_here = inputs
        phase_one, phase_two = shear_phases(angle_number)

        def forward_block(block):
            return project_block(block, phase_one, phase_two)
        proj_rows = lax.map(forward_block, blocks).reshape(NZ, NY)
        grad_rows, probe_grad = window_terms(proj_rows, probe_modes, measure, rows_here, cols_here)

        def adjoint_block(rows_block):
            return backproject_block(rows_block, phase_one, phase_two)
        grad_blocks = grad_rows.reshape(NZ // block_rows, block_rows, NY)
        field_grad = lax.map(adjoint_block, grad_blocks).reshape(NZ, NX, NY)
        return ((volume_acc + field_grad, probe_acc + probe_grad), None)
    start = (jnp.zeros((NZ, NX, NY), jnp.float32), jnp.zeros((MODES, 2, WIN, WIN), jnp.float32))
    (volume_grad, probe_grad), unused = lax.scan(per_angle, start, (angle_index, measured, row_offset, col_offset))
    return (4.0 * volume_grad, probe_grad / 16.0)
```

```python
import math

import jax
import jax.numpy as jnp
import numpy as np
from jax import lax
from jax.experimental import pallas as pl
from jax.experimental.pallas import tpu as pltpu
from jax.sharding import Mesh, PartitionSpec as P

N = 512
H = N // 2
W = 128
MODES = 8
ANGLES = 8
ROWS = 32
HALF = MODES * 2 * W // 2
CHUNK = HALF // 16
F32 = jnp.float32
BF16 = jnp.bfloat16


def split_const(table):
    high = table.astype(BF16)
    low = (table - high.astype(np.float64)).astype(BF16)
    return np.stack([high, low])


def dft_tables():
    k, n = np.arange(H)[:, None], np.arange(N)[None, :]
    turns = 2.0 * np.pi / N * (k * n % N)
    table = np.concatenate([np.cos(turns), -np.sin(turns)], 0)
    table[H] = 1.0 - 2.0 * (np.arange(N) % 2)
    return split_const(table), split_const(np.ascontiguousarray(table.T))


def window_tables():
    j = np.arange(W)
    turns = 2.0 * np.pi / W * (j[:, None] * j[None, :] % W)
    c, s = np.cos(turns), np.sin(turns)
    return split_const(np.block([[c, s], [-s, c]])), split_const(np.block([[c, -s], [s, c]]))


def shears():
    theta = np.pi * (np.arange(ANGLES) + 0.5) / ANGLES - np.pi / 2
    return -np.tan(theta / 2), np.sin(theta)


def cos_sin(phase):
    return np.stack([np.cos(phase), np.sin(phase)], 1)


def phase_tables():
    shear_x, shear_y = shears()
    cells = np.arange(N) - N / 2
    unit_one = -2.0 * np.pi / N * shear_x
    unit_two = -2.0 * np.pi / N * shear_y
    by_y = unit_one[:, None, None] * cells[None, None, :]
    coarse = cos_sin(by_y * (8 * np.arange(H // 8))[None, :, None]).astype(np.float32)
    fine = cos_sin(by_y * np.arange(8)[None, :, None]).astype(np.float32)
    nyquist = np.ones((ANGLES, 8, N))
    nyquist[:, 0] = 0.5 * np.cos(by_y[:, 0] * H)
    freq = np.arange(H, dtype=np.float64)
    freq[0] = H
    by_k = unit_one[:, None, None] * freq[None, None, :]
    rows_coarse = cos_sin(by_k * cells[::8][None, :, None]).astype(np.float32)
    rows_fine = cos_sin(by_k * np.arange(8)[None, :, None]).astype(np.float32)
    two = unit_two[:, None, None] * np.arange(H)[None, :, None] * cells[None, None, :]
    table = np.concatenate([np.cos(two), np.sin(two)], 1)
    table[:, H] = np.cos(unit_two[:, None] * H * cells[None, :])
    beams = np.moveaxis(split_const(table), 0, 1)
    return coarse, fine, nyquist.astype(np.float32), rows_coarse, rows_fine, np.ascontiguousarray(beams)


def mm(a, b):
    return lax.dot_general(a, b, (((1,), (0,)), ((), ())), preferred_element_type=F32)


def mm_t(a, b):
    return lax.dot_general(a, b, (((1,), (1,)), ((), ())), preferred_element_type=F32)


def split(value):
    high = value.astype(BF16)
    return high, (value - high.astype(F32)).astype(BF16)


def three(dot, a, b):
    return dot(a[0], b[0]) + (dot(a[0], b[1]) + dot(a[1], b[0]))


def forward_kernel(
    sc, volume, dft, dft_t, coarse, fine, nyquist, beams, out, spec, turned_hi, turned_lo, field_hi, field_lo
):
    block = volume[0]
    for part in range(2):
        lanes = pl.ds(part * H, H)
        spec[:, lanes] = mm(dft[0], block[:, part * H : (part + 1) * H]) + mm(
            dft[1], block[:, part * H : (part + 1) * H]
        )
    first = lax.broadcasted_iota(jnp.int32, (8, N), 0) == 0
    half_row = jnp.where(first, 0.5, 1.0)
    for pair in range(H // 16):
        reals, imags = [], []
        for u in (2 * pair, 2 * pair + 1):
            ca, sa = coarse[0, 0, u : u + 1, :], coarse[0, 1, u : u + 1, :]
            cb, sb = fine[0, 0], fine[0, 1]
            c, s = ca * cb - sa * sb, sa * cb + ca * sb
            a, b = spec[8 * u : 8 * u + 8, :], spec[H + 8 * u : H + 8 * u + 8, :]
            real, imag = a * c - b * s, a * s + b * c
            if u == 0:
                real, imag = real * half_row, imag * nyquist[0]
            reals.append(real)
            imags.append(imag)
        for base, parts in ((0, reals), (H, imags)):
            high, low = split(jnp.concatenate(parts, 0))
            turned_hi[base + 16 * pair : base + 16 * pair + 16, :] = high
            turned_lo[base + 16 * pair : base + 16 * pair + 16, :] = low
    for part in range(2):
        lanes = slice(part * H, (part + 1) * H)
        field = three(mm, (dft_t[0], dft_t[1]), (turned_hi[:, lanes], turned_lo[:, lanes]))
        high, low = split(field)
        field_hi[:, lanes] = high
        field_lo[:, lanes] = low
    spec[...] = three(mm_t, (dft[0], dft[1]), (field_hi[...], field_lo[...]))
    total = jnp.zeros((8, N), F32)
    for r in range(0, H, 32):
        a, b = spec[r : r + 32, :], spec[H + r : H + r + 32, :]
        c = beams[0, 0, r : r + 32, :].astype(F32) + beams[0, 1, r : r + 32, :].astype(F32)
        s = beams[0, 0, H + r : H + r + 32, :].astype(F32) + beams[0, 1, H + r : H + r + 32, :].astype(F32)
        c_low = c
        if r == 0:
            top = lax.broadcasted_iota(jnp.int32, (32, N), 0) == 0
            c_low, s = jnp.where(top, s, c), jnp.where(top, 0.0, s)
        real = jnp.sum(a * c - b * s, axis=1, keepdims=True)
        imag = jnp.sum(a * s + b * c_low, axis=1, keepdims=True)
        if r == 0:
            weight = jnp.where(lax.broadcasted_iota(jnp.int32, (32, 1), 0) == 0, 0.5, 1.0)
            real, imag = real * weight, imag * weight
        f_real = dft[0, r : r + 32, :].astype(F32) + dft[1, r : r + 32, :].astype(F32)
        f_imag = dft[0, H + r : H + r + 32, :].astype(F32) + dft[1, H + r : H + r + 32, :].astype(F32)
        terms = real * f_real + imag * f_imag
        total = total + jnp.sum(terms.reshape(4, 8, N), axis=0)
    row = jnp.sum(total, axis=0, keepdims=True) * (4.0 / (N * N))
    for t in range(4):
        out[pl.ds(t, ROWS, stride=4), :] = jnp.broadcast_to(row[:, t * W : (t + 1) * W], (ROWS, W))


def window_kernel(sc, whole, probe, measured, left, right, keep, send, exits, far, pieces):
    row, col, core = sc[0], sc[1], sc[2]
    rows = jnp.concatenate([whole[pl.ds(t, ROWS, stride=4), :] for t in range(4)], axis=1)
    band = pltpu.roll(rows, lax.rem(N - col, N), 1)[:, :W]
    pad = jnp.zeros((W - ROWS, W), F32)
    obj_real = pltpu.roll(jnp.concatenate([jnp.cos(band) - 1.0, pad], 0), -row, 0) + 1.0
    obj_imag = pltpu.roll(jnp.concatenate([jnp.sin(band), pad], 0), -row, 0)
    lefts, rights = (left[0], left[1]), (right[0], right[1])
    intensity = jnp.zeros((W, W), F32)
    for pair in range(MODES // 2):
        for m in (2 * pair, 2 * pair + 1):
            lanes = slice((m % 2) * W, (m % 2 + 1) * W)
            p_real, p_imag = probe[m, 0], probe[m, 1]
            exits[:W, lanes] = p_real * obj_real - p_imag * obj_imag
            exits[W:, lanes] = p_real * obj_imag + p_imag * obj_real
        first = three(mm, lefts, split(exits[...]))
        turned = jnp.concatenate(
            [
                jnp.concatenate([first[:W, :W], first[W:, :W]], 1),
                jnp.concatenate([first[:W, W:], first[W:, W:]], 1),
            ],
            0,
        )
        waves = three(mm, split(turned), rights)
        far[2 * W * pair : 2 * W * (pair + 1), :] = waves
        power = waves * waves
        power = power[:W] + power[W:]
        intensity = intensity + (power[:, :W] + power[:, W:])
    factor = (1.0 - jnp.sqrt(measured[0, 0] + 1.0) / jnp.sqrt(intensity + 1.0)) * (1.0 / W)
    factors = jnp.concatenate([jnp.concatenate([factor, factor], 1)] * 2, 0)
    grad_real, grad_imag = jnp.zeros((W, W), F32), jnp.zeros((W, W), F32)
    for pair in range(MODES // 2):
        scaled = far[2 * W * pair : 2 * W * (pair + 1), :] * factors
        first = three(mm, split(scaled), lefts)
        turned = jnp.concatenate(
            [
                jnp.concatenate([first[:W, :W], first[W:, :W]], 1),
                jnp.concatenate([first[:W, W:], first[W:, W:]], 1),
            ],
            0,
        )
        back = three(mm, rights, split(turned))
        for m in (2 * pair, 2 * pair + 1):
            lanes = slice((m % 2) * W, (m % 2 + 1) * W)
            b_real, b_imag = back[:W, lanes], back[W:, lanes]
            p_real, p_imag = probe[m, 0], probe[m, 1]
            grad_real = grad_real + (p_real * b_real + p_imag * b_imag)
            grad_imag = grad_imag + (p_real * b_imag - p_imag * b_real)
            exits[:W, lanes] = obj_real * b_real + obj_imag * b_imag
            exits[W:, lanes] = obj_real * b_imag - obj_imag * b_real

        def store(target, pair=pair):
            for m in (2 * pair, 2 * pair + 1):
                lanes = slice((m % 2) * W, (m % 2 + 1) * W)
                base = (m % 4) * 2 * W
                target[base : base + 2 * W, :] = exits[:, lanes]

        owner = 2 * pair // 4
        pl.when(core == owner)(lambda: store(keep))
        pl.when(core != owner)(lambda: store(send))
    patch = grad_imag * obj_real - grad_real * obj_imag
    shown = pltpu.roll(patch, W + row, 0)[:ROWS]
    wide = pltpu.roll(jnp.concatenate([shown, jnp.zeros((ROWS, N - W), F32)], 1), col, 1)
    for t in range(4):
        pieces[t] = wide[:, t * W : (t + 1) * W]
    for parity in range(2):

        def place(target, parity=parity):
            for t in range(4):
                target[HALF + 16 * t : HALF + 16 * (t + 1), :] = pieces[t, pl.ds(parity, 16, stride=2), :]

        pl.when(core == parity)(lambda: place(keep))
        pl.when(core != parity)(lambda: place(send))


def pack_kernel(sc, keep, other, out):
    angle = jnp.broadcast_to(sc[0].astype(F32), (8, W))
    for peer in range(16):
        rows = slice(CHUNK * peer, CHUNK * (peer + 1))
        out[peer, :CHUNK, :] = keep[rows, :] + other[rows, :]
        for t in range(4):
            base = HALF + 16 * t + 8 * (peer % 2)
            out[peer, CHUNK + 8 * t : CHUNK + 8 * t + 8, :] = keep[base : base + 8, :] + other[base : base + 8, :]
        out[peer, CHUNK + 32 :, :] = angle


def relay_kernel(received, out, pieces):
    total = received[0, :CHUNK, :]
    for peer in range(1, 16):
        total = total + received[peer, :CHUNK, :]
    for a in range(ANGLES):
        pieces[32 * a : 32 * a + 32, :] = (
            received[2 * a, CHUNK : CHUNK + 32, :] + received[2 * a + 1, CHUNK : CHUNK + 32, :]
        )
    for z in range(8):
        out[z, :CHUNK, :] = total
        out[z, CHUNK:, :] = pieces[pl.ds(z, 32, stride=8), :]


def adjoint_kernel(
    sc, received, dft_t, rows_coarse, rows_fine, beams, out, pieces, cbar, rows_dft, sheared_hi, sheared_lo, chunk
):
    step = pl.program_id(0)
    block = sc[ANGLES]
    lane_first = lax.broadcasted_iota(jnp.int32, (8, H), 1) == 0

    @pl.when(step == 0)
    def start():
        total = received[0]
        for z in range(1, 8):
            total = total + received[z]
        chunk[...] = total[:CHUNK] * (1.0 / 16.0)
        pieces[...] = total[CHUNK:]
        rows = jnp.concatenate([pieces[pl.ds(t, 8, stride=4), :] for t in range(4)], axis=1)
        spectrum = three(mm, split(rows), (dft_t[0], dft_t[1])) * (1.0 / N)
        weight = jnp.where(lax.broadcasted_iota(jnp.int32, (8, N), 1) % H == 0, 0.5, 1.0)
        cbar[...] = spectrum * weight
        at = pl.ds(pl.multiple_of(64 * block, 64), 64)
        rows_dft[...] = dft_t[0, at, :].astype(F32) + dft_t[1, at, :].astype(F32)

    mine = cbar[pl.ds(step, 1), :]
    c_real, c_imag = mine[:, :H], mine[:, H:]
    lane_zero = lax.broadcasted_iota(jnp.int32, (64, H), 1) == 0
    r_cos, r_sin = rows_dft[:, :H], rows_dft[:, H:]
    r_sin_real = jnp.where(lane_zero, 0.0, r_sin)
    r_cos_imag = jnp.where(lane_zero, r_sin, r_cos)
    shifted = jnp.concatenate([c_real * r_cos + c_imag * r_sin_real, c_imag * r_cos_imag - c_real * r_sin_real], 1)
    here = three(mm, split(shifted), (beams[0, 0], beams[0, 1]))
    high, low = split(here)
    at_rows = pl.ds(pl.multiple_of(64 * step, 64), 64)
    sheared_hi[at_rows, :] = high
    sheared_lo[at_rows, :] = low

    @pl.when(step == ANGLES - 1)
    def finish():
        spectrum = three(mm, (sheared_hi[...], sheared_lo[...]), (dft_t[0], dft_t[1]))
        sums = [None] * 8
        for a in range(ANGLES):
            number = sc[a]
            cb, sb = rows_fine[number, 0], rows_fine[number, 1]
            for u in range(8):
                ca, sa = rows_coarse[number, 0, u : u + 1, :], rows_coarse[number, 1, u : u + 1, :]
                c, s = ca * cb - sa * sb, sa * cb + ca * sb
                c_first, s_first = jnp.where(lane_first, 1.0, c), jnp.where(lane_first, 0.0, s)
                base = 64 * a + 8 * u
                real, imag = spectrum[base : base + 8, :H], spectrum[base : base + 8, H:]
                unturned = jnp.concatenate([real * c_first + imag * s_first, imag * c - real * s_first], 1)
                sums[u] = unturned if a == 0 else sums[u] + unturned
        weight = jnp.where(lax.broadcasted_iota(jnp.int32, (64, N), 1) % H == 0, 0.5 / 32.0, 1.0 / 32.0)
        whole = jnp.concatenate(sums, 0) * weight
        zeros = jnp.zeros((64, N), BF16)
        high, low = split(whole)
        result = None
        for side in range(2):
            dft_rows = [
                jnp.concatenate([dft_t[p, 64 * a + 32 * side : 64 * a + 32 * side + 32, :] for a in range(ANGLES)], 0)
                for p in range(2)
            ]
            order = (lambda v: [v, zeros]) if side == 0 else (lambda v: [zeros, v])
            columns = (jnp.concatenate(order(high), 0), jnp.concatenate(order(low), 0))
            part = three(mm_t, dft_rows, columns)
            result = part if result is None else result + part
        for peer in range(16):
            a = peer // 2
            out[peer, :CHUNK, :] = chunk[...]
            out[peer, CHUNK:, :] = result[32 * a : 32 * a + 32, :]


def assemble_kernel(sc, received, out):
    lower = lax.broadcasted_iota(jnp.int32, (32, W), 1) < 64
    for b in range(4):
        even = received[4 * b + sc[0], CHUNK:, :]
        odd = received[4 * b + 2 + sc[0], CHUNK:, :]
        lanes = slice(b * W, (b + 1) * W)
        out[0, :32, lanes] = jnp.where(lower, even, pltpu.roll(odd, 64, 1))
        out[0, 32:, lanes] = jnp.where(lower, pltpu.roll(even, 64, 1), odd)


params = dict(vmem_limit_bytes=48 * 1024 * 1024)


def full(shape):
    zeros = (0,) * len(shape)
    return pl.BlockSpec(shape, lambda *unused: zeros)


def by_angle(shape):
    return pl.BlockSpec((1,) + shape, lambda i, sc: (sc[0],) + (0,) * len(shape))


def forward_call(sc, volume, tables):
    dft, dft_t, coarse, fine, nyquist, beams = tables
    return pl.pallas_call(
        forward_kernel,
        grid_spec=pltpu.PrefetchScalarGridSpec(
            num_scalar_prefetch=1,
            grid=(1,),
            in_specs=[
                full((1, N, N)),
                full((2, N, N)),
                full((2, N, N)),
                by_angle((2, H // 8, N)),
                by_angle((2, 8, N)),
                by_angle((8, N)),
                by_angle((2, N, N)),
            ],
            out_specs=full((W, W)),
            scratch_shapes=[pltpu.VMEM((N, N), F32)] + [pltpu.VMEM((N, N), BF16)] * 4,
        ),
        out_shape=jax.ShapeDtypeStruct((4 * ROWS, W), F32),
        compiler_params=pltpu.CompilerParams(**params),
        name="forward",
    )(sc, volume, dft, dft_t, coarse, fine, nyquist, beams)


def vmem_call(kernel, out_shapes, scratch, name, *args):
    specs = [
        pl.BlockSpec(memory_space=pltpu.SMEM if a.dtype == jnp.int32 else pltpu.VMEM) for a in args
    ]
    single = not isinstance(out_shapes, list)
    shapes = [out_shapes] if single else out_shapes
    outs = pl.pallas_call(
        kernel,
        in_specs=specs,
        out_specs=[pl.BlockSpec(memory_space=pltpu.VMEM)] * len(shapes),
        out_shape=[jax.ShapeDtypeStruct(s, F32) for s in shapes],
        scratch_shapes=scratch,
        compiler_params=pltpu.CompilerParams(**params),
        name=name,
    )(*args)
    return outs[0] if single else outs


def adjoint_call(sc, received, dft_t, rows_coarse, rows_fine, beams):
    return pl.pallas_call(
        adjoint_kernel,
        grid_spec=pltpu.PrefetchScalarGridSpec(
            num_scalar_prefetch=1,
            grid=(ANGLES,),
            in_specs=[
                full((8, CHUNK + 32, W)),
                full((2, N, N)),
                pl.BlockSpec((ANGLES, 2, 8, H), lambda i, sc: (0, 0, sc[ANGLES], 0)),
                full((ANGLES, 2, 8, H)),
                pl.BlockSpec((1, 2, N, N), lambda i, sc: (sc[i], 0, 0, 0)),
            ],
            out_specs=full((16, CHUNK + 32, W)),
            scratch_shapes=[
                pltpu.VMEM((32, W), F32),
                pltpu.VMEM((8, N), F32),
                pltpu.VMEM((64, N), F32),
                pltpu.VMEM((N, N), BF16),
                pltpu.VMEM((N, N), BF16),
                pltpu.VMEM((CHUNK, W), F32),
            ],
        ),
        out_shape=jax.ShapeDtypeStruct((16, CHUNK + 32, W), F32),
        compiler_params=pltpu.CompilerParams(**params),
        name="adjoint",
    )(sc, received, dft_t, rows_coarse, rows_fine, beams)


GZ = ("xl", "z", "core")
PLANE = ("y", "xh", "xl")


def exchange(blocks, axes):
    return lax.all_to_all(blocks, axes, split_axis=0, concat_axis=0, tiled=True)


def swap(rows):
    return lax.ppermute(rows, "core", [(0, 1), (1, 0)])


def local(volume, probe, measured, angle_index, row_offset, col_offset):
    dft, dft_t = (jnp.asarray(t) for t in dft_tables())
    left, right = (jnp.asarray(t) for t in window_tables())
    coarse, fine, nyquist, rows_coarse, rows_fine, beams = (jnp.asarray(t) for t in phase_tables())
    core = lax.axis_index("core")
    block = 2 * lax.axis_index("y") + lax.axis_index("xh")
    row = forward_call(angle_index, volume, (dft, dft_t, coarse, fine, nyquist, beams))
    whole = exchange(row.reshape(ROWS, 4, W), GZ).reshape(4 * ROWS, W)
    places = jnp.stack([row_offset[0, 0], col_offset[0, 0], core.astype(jnp.int32)])
    keep, send = vmem_call(
        window_kernel,
        [(HALF + 64, W)] * 2,
        [pltpu.VMEM((2 * W, 2 * W), F32), pltpu.VMEM((MODES * W, 2 * W), F32), pltpu.VMEM((4, ROWS, W), F32)],
        "window",
        places,
        whole,
        probe,
        measured,
        left,
        right,
    )
    packed = vmem_call(pack_kernel, (16, CHUNK + 40, W), [], "pack", angle_index, keep, swap(send))
    shared = exchange(packed, PLANE)
    angles = shared.reshape(ANGLES, 2, CHUNK + 40, W)[:, 0, CHUNK + 32, 0].astype(jnp.int32)
    relay = vmem_call(relay_kernel, (8, CHUNK + 32, W), [pltpu.VMEM((256, W), F32)], "relay", shared)
    rows = exchange(relay, "z")
    numbers = jnp.concatenate([angles, jnp.stack([block.astype(jnp.int32)])])
    blocks = adjoint_call(numbers, rows, dft_t, rows_coarse, rows_fine, beams)
    final = exchange(blocks, PLANE)
    mine = final[:, :CHUNK, :].reshape(HALF, W)
    other = swap(mine)
    here = jnp.stack([lax.axis_index("xl").astype(jnp.int32)])
    volume_update = vmem_call(assemble_kernel, (1, 64, N), [], "assemble", here, final)
    probe_update = jnp.where(core == 0, jnp.stack([mine, other]), jnp.stack([other, mine]))
    return volume_update, probe_update.reshape(MODES, 2, W, W)


def solution(mesh):
    split_mesh = Mesh(mesh.devices.reshape(4, 2, 2, 8, 2), ("y", "xh", "xl", "z", "core"))
    angle, gz = ("y", "xh"), GZ
    return jax.shard_map(
        local,
        mesh=split_mesh,
        in_specs=(
            P(gz, None, None),
            P(),
            P(angle, gz, None, None),
            P(angle),
            P(angle, gz),
            P(angle, gz),
        ),
        out_specs=(P(gz, angle, None), P()),
        check_vma=False,
    )
```

```python
import math

import jax
import jax.numpy as jnp
import numpy as np
from jax import lax
from jax.experimental import pallas as pl
from jax.experimental.pallas import tpu as pltpu
from jax.sharding import Mesh, PartitionSpec as P

N = 512
H = N // 2
W = 128
MODES = 8
ANGLES = 8
PAIRS = ANGLES // 2
ROWS = 32
HALF = MODES * 2 * W // 2
CHUNK = HALF // 16
F32 = jnp.float32
BF16 = jnp.bfloat16


def split_const(table):
    high = table.astype(BF16)
    low = (table - high.astype(np.float64)).astype(BF16)
    return np.stack([high, low])


def dft_tables():
    k, n = np.arange(H)[:, None], np.arange(N)[None, :]
    turns = 2.0 * np.pi / N * (k * n % N)
    table = np.concatenate([np.cos(turns), -np.sin(turns)], 0)
    table[H] = 1.0 - 2.0 * (np.arange(N) % 2)
    return split_const(table), split_const(np.ascontiguousarray(table.T))


def window_tables():
    j = np.arange(W)
    turns = 2.0 * np.pi / W * (j[:, None] * j[None, :] % W)
    c, s = np.cos(turns), np.sin(turns)
    return np.stack([split_const(np.block([[c, s], [-s, c]])), split_const(np.block([[c, -s], [s, c]]))])


def shears():
    theta = np.pi * (np.arange(ANGLES) + 0.5) / ANGLES - np.pi / 2
    return -np.tan(theta / 2), np.sin(theta)


def cos_sin(phase):
    return np.stack([np.cos(phase), np.sin(phase)], 1)


def phase_tables():
    shear_x, shear_y = shears()
    cells = np.arange(N) - N / 2
    unit_one = -2.0 * np.pi / N * shear_x
    unit_two = -2.0 * np.pi / N * shear_y[:PAIRS]
    by_y = unit_one[:, None, None] * cells[None, None, :]
    nyquist = np.ones((ANGLES, 1, 8, N))
    nyquist[:, 0, 0] = 0.5 * np.cos(by_y[:, 0] * H)
    factors = np.concatenate(
        [
            cos_sin(by_y * (8 * np.arange(H // 8))[None, :, None]).reshape(ANGLES, H // 4, N),
            cos_sin(by_y * np.arange(8)[None, :, None]).reshape(ANGLES, 16, N),
            nyquist[:, 0],
        ],
        1,
    )
    freq = np.arange(H, dtype=np.float64)
    freq[0] = H
    by_k = unit_one[:PAIRS, None, None] * freq[None, None, :]
    rows_coarse = cos_sin(by_k * cells[::8][None, :, None])
    rows_fine = cos_sin(by_k * np.arange(8)[None, :, None])
    two = unit_two[:, None, None] * np.arange(H)[None, :, None] * cells[None, None, :]
    table = np.concatenate([np.cos(two), np.sin(two)], 1)
    table[:, H] = np.cos(unit_two[:, None] * H * cells[None, :])
    beams = np.ascontiguousarray(np.moveaxis(split_const(table), 0, 1))
    rows_tables = np.concatenate([rows_coarse, rows_fine], 2)
    return factors.astype(np.float32), rows_tables.astype(np.float32), beams


def mm(a, b):
    return lax.dot_general(a, b, (((1,), (0,)), ((), ())), preferred_element_type=F32)


def mm_t(a, b):
    return lax.dot_general(a, b, (((1,), (1,)), ((), ())), preferred_element_type=F32)


def split(value):
    high = value.astype(BF16)
    return high, (value - high.astype(F32)).astype(BF16)


def three(dot, a, b):
    return dot(a[0], b[0]) + (dot(a[0], b[1]) + dot(a[1], b[0]))


def forward_kernel(
    sc, volume, dft_hbm, dft_t_hbm, factors_hbm, beams_hbm, out,
    slab, dft, dft_t, factors, beams, spec, turned_hi, turned_lo, field_hi, field_lo, sems,
):
    number = sc[0]
    mirrored = number >= PAIRS
    sign = jnp.where(mirrored, -1.0, 1.0)
    moves = [
        pltpu.make_async_copy(volume.at[0], slab, sems.at[0]),
        pltpu.make_async_copy(dft_hbm, dft, sems.at[1]),
        pltpu.make_async_copy(factors_hbm.at[number], factors, sems.at[2]),
        pltpu.make_async_copy(dft_t_hbm, dft_t, sems.at[3]),
        pltpu.make_async_copy(
            beams_hbm.at[jnp.where(mirrored, ANGLES - 1 - number, number)], beams, sems.at[4]
        ),
    ]
    for move in moves:
        move.start()
    moves[0].wait()
    moves[1].wait()
    for part in range(2):
        lanes = slice(part * H, (part + 1) * H)
        spec[:, lanes] = mm(dft[0], slab[:, lanes]) + mm(dft[1], slab[:, lanes])
    moves[2].wait()
    first = lax.broadcasted_iota(jnp.int32, (8, N), 0) == 0
    half_row = jnp.where(first, 0.5, 1.0)
    for pair in range(H // 16):
        reals, imags = [], []
        for u in (2 * pair, 2 * pair + 1):
            ca, sa = factors[u : u + 1, :], factors[32 + u : 33 + u, :]
            cb, sb = factors[64:72, :], factors[72:80, :]
            c, s = ca * cb - sa * sb, sa * cb + ca * sb
            a, b = spec[8 * u : 8 * u + 8, :], spec[H + 8 * u : H + 8 * u + 8, :]
            real, imag = a * c - b * s, a * s + b * c
            if u == 0:
                real, imag = real * half_row, imag * factors[80:88, :]
            reals.append(real)
            imags.append(imag)
        for base, parts in ((0, reals), (H, imags)):
            high, low = split(jnp.concatenate(parts, 0))
            turned_hi[base + 16 * pair : base + 16 * pair + 16, :] = high
            turned_lo[base + 16 * pair : base + 16 * pair + 16, :] = low
    moves[3].wait()
    for part in range(2):
        lanes = slice(part * H, (part + 1) * H)
        field = three(mm, (dft_t[0], dft_t[1]), (turned_hi[:, lanes], turned_lo[:, lanes]))
        high, low = split(field)
        field_hi[:, lanes] = high
        field_lo[:, lanes] = low
    spec[...] = three(mm_t, (dft[0], dft[1]), (field_hi[...], field_lo[...]))
    moves[4].wait()
    total = jnp.zeros((8, N), F32)
    for r in range(0, H, 32):
        a, b = spec[r : r + 32, :], spec[H + r : H + r + 32, :]
        c = beams[0, r : r + 32, :].astype(F32) + beams[1, r : r + 32, :].astype(F32)
        s = beams[0, H + r : H + r + 32, :].astype(F32) + beams[1, H + r : H + r + 32, :].astype(F32)
        c_low = c
        if r == 0:
            top = lax.broadcasted_iota(jnp.int32, (32, N), 0) == 0
            c_low, s = jnp.where(top, s, c), jnp.where(top, 0.0, s)
        s = s * sign
        real = jnp.sum(a * c - b * s, axis=1, keepdims=True)
        imag = jnp.sum(a * s + b * c_low, axis=1, keepdims=True)
        if r == 0:
            weight = jnp.where(lax.broadcasted_iota(jnp.int32, (32, 1), 0) == 0, 0.5, 1.0)
            real, imag = real * weight, imag * weight
        f_real = dft[0, r : r + 32, :].astype(F32) + dft[1, r : r + 32, :].astype(F32)
        f_imag = dft[0, H + r : H + r + 32, :].astype(F32) + dft[1, H + r : H + r + 32, :].astype(F32)
        terms = real * f_real + imag * f_imag
        total = total + jnp.sum(terms.reshape(4, 8, N), axis=0)
    row = jnp.sum(total, axis=0, keepdims=True) * (4.0 / (N * N))
    for t in range(4):
        out[pl.ds(t, ROWS, stride=4), :] = jnp.broadcast_to(row[:, t * W : (t + 1) * W], (ROWS, W))


def window_kernel(row_ref, col_ref, whole, probe, measured, dfts, keep, send, exits, far, pieces):
    row, col, core = row_ref[0, 0], col_ref[0, 0], lax.axis_index("core")
    rows = jnp.concatenate([whole[pl.ds(t, ROWS, stride=4), :] for t in range(4)], axis=1)
    band = pltpu.roll(rows, lax.rem(N - col, N), 1)[:, :W]
    pad = jnp.zeros((W - ROWS, W), F32)
    obj_real = pltpu.roll(jnp.concatenate([jnp.cos(band) - 1.0, pad], 0), -row, 0) + 1.0
    obj_imag = pltpu.roll(jnp.concatenate([jnp.sin(band), pad], 0), -row, 0)
    lefts, rights = (dfts[0, 0], dfts[0, 1]), (dfts[1, 0], dfts[1, 1])
    intensity = jnp.zeros((W, W), F32)
    for pair in range(MODES // 2):
        for m in (2 * pair, 2 * pair + 1):
            lanes = slice((m % 2) * W, (m % 2 + 1) * W)
            p_real, p_imag = probe[m, 0], probe[m, 1]
            exits[pair, :W, lanes] = p_real * obj_real - p_imag * obj_imag
            exits[pair, W:, lanes] = p_real * obj_imag + p_imag * obj_real
        first = three(mm, lefts, split(exits[pair]))
        turned = jnp.concatenate(
            [
                jnp.concatenate([first[:W, :W], first[W:, :W]], 1),
                jnp.concatenate([first[:W, W:], first[W:, W:]], 1),
            ],
            0,
        )
        waves = three(mm, split(turned), rights)
        far[2 * W * pair : 2 * W * (pair + 1), :] = waves
        power = waves * waves
        power = power[:W] + power[W:]
        intensity = intensity + (power[:, :W] + power[:, W:])
    factor = (1.0 - jnp.sqrt(measured[0, 0] + 1.0) / jnp.sqrt(intensity + 1.0)) * (1.0 / W)
    factors = jnp.concatenate([jnp.concatenate([factor, factor], 1)] * 2, 0)
    grad_real, grad_imag = jnp.zeros((W, W), F32), jnp.zeros((W, W), F32)
    for pair in range(MODES // 2):
        scaled = far[2 * W * pair : 2 * W * (pair + 1), :] * factors
        first = three(mm, split(scaled), lefts)
        turned = jnp.concatenate(
            [
                jnp.concatenate([first[:W, :W], first[W:, :W]], 1),
                jnp.concatenate([first[:W, W:], first[W:, W:]], 1),
            ],
            0,
        )
        back = three(mm, rights, split(turned))
        for m in (2 * pair, 2 * pair + 1):
            lanes = slice((m % 2) * W, (m % 2 + 1) * W)
            b_real, b_imag = back[:W, lanes], back[W:, lanes]
            p_real, p_imag = probe[m, 0], probe[m, 1]
            grad_real = grad_real + (p_real * b_real + p_imag * b_imag)
            grad_imag = grad_imag + (p_real * b_imag - p_imag * b_real)
            exits[pair, :W, lanes] = obj_real * b_real + obj_imag * b_imag
            exits[pair, W:, lanes] = obj_real * b_imag - obj_imag * b_real

        def store(target, pair=pair):
            for m in (2 * pair, 2 * pair + 1):
                lanes = slice((m % 2) * W, (m % 2 + 1) * W)
                base = (m % 4) * 2 * W
                target[base : base + 2 * W, :] = exits[pair, :, lanes]

        owner = 2 * pair // 4
        pl.when(core == owner)(lambda: store(keep))
        pl.when(core != owner)(lambda: store(send))
    patch = grad_imag * obj_real - grad_real * obj_imag
    shown = pltpu.roll(patch, W + row, 0)[:ROWS]
    wide = pltpu.roll(jnp.concatenate([shown, jnp.zeros((ROWS, N - W), F32)], 1), col, 1)
    for t in range(4):
        pieces[t] = wide[:, t * W : (t + 1) * W]
    for parity in range(2):

        def place(target, parity=parity):
            for t in range(4):
                target[HALF + 16 * t : HALF + 16 * (t + 1), :] = pieces[t, pl.ds(parity, 16, stride=2), :]

        pl.when(core == parity)(lambda: place(keep))
        pl.when(core != parity)(lambda: place(send))


def pack_kernel(sc, keep, other, out):
    angle = jnp.broadcast_to(sc[0].astype(F32), (8, W))
    for peer in range(16):
        rows = slice(CHUNK * peer, CHUNK * (peer + 1))
        out[peer, :CHUNK, :] = keep[rows, :] + other[rows, :]
        for t in range(4):
            base = HALF + 16 * t + 8 * (peer % 2)
            out[peer, CHUNK + 8 * t : CHUNK + 8 * t + 8, :] = keep[base : base + 8, :] + other[base : base + 8, :]
        out[peer, CHUNK + 32 :, :] = angle


def relay_kernel(received, out, pieces):
    total = received[0, :CHUNK, :]
    for peer in range(1, 16):
        total = total + received[peer, :CHUNK, :]
    for a in range(ANGLES):
        number = jnp.max(received[2 * a, CHUNK + 32 :, :]).astype(jnp.int32)
        slot = jnp.where(number >= PAIRS, 2 * (ANGLES - 1 - number) + 1, 2 * number)
        pieces[pl.ds(pl.multiple_of(32 * slot, 32), 32), :] = (
            received[2 * a, CHUNK : CHUNK + 32, :] + received[2 * a + 1, CHUNK : CHUNK + 32, :]
        )
    for z in range(8):
        out[z, :CHUNK, :] = total
        out[z, CHUNK:, :] = pieces[pl.ds(z, 32, stride=8), :]


def adjoint_kernel(received, dft_t, rows_tables, *refs):
    beams, (out, pieces, shifted, sheared) = refs[:PAIRS], refs[PAIRS:]
    block = 2 * lax.axis_index("y") + lax.axis_index("xh")
    total = received[0]
    for z in range(1, 8):
        total = total + received[z]
    chunk = total[:CHUNK] * (1.0 / 16.0)
    pieces[...] = total[CHUNK:]
    rows = jnp.concatenate([pieces[pl.ds(t, 8, stride=4), :] for t in range(4)], axis=1)
    spectrum = three(mm, split(rows), (dft_t[0], dft_t[1]))
    weight = jnp.where(lax.broadcasted_iota(jnp.int32, (8, N), 1) % H == 0, 0.5 / N, 1.0 / N)
    cbar = spectrum * weight
    at = pl.ds(pl.multiple_of(64 * block, 64), 64)
    rows_dft = dft_t[0, at, :].astype(F32) + dft_t[1, at, :].astype(F32)
    lane_zero = lax.broadcasted_iota(jnp.int32, (64, H), 1) == 0
    r_cos, r_sin = rows_dft[:, :H], rows_dft[:, H:]
    r_sin_real = jnp.where(lane_zero, 0.0, r_sin)
    r_cos_imag = jnp.where(lane_zero, r_sin, r_cos)
    mirror = jnp.where(lane_zero, 1.0, -1.0)
    for slot in range(ANGLES):
        c_real, c_imag = cbar[slot : slot + 1, :H], cbar[slot : slot + 1, H:]
        cosines = c_real * r_cos + c_imag * r_sin_real
        sines = c_imag * r_cos_imag - c_real * r_sin_real
        if slot % 2:
            sines = sines * mirror
        high, low = split(jnp.concatenate([cosines, sines], 1))
        shifted[0, 64 * slot : 64 * slot + 64, :] = high
        shifted[1, 64 * slot : 64 * slot + 64, :] = low
    for q in range(PAIRS):
        at = slice(2 * 64 * q, 2 * 64 * (q + 1))
        here = three(mm, (shifted[0, at, :], shifted[1, at, :]), (beams[q][0], beams[q][1]))
        high, low = split(here)
        sheared[0, at, :] = high
        sheared[1, at, :] = low
    spectrum = three(mm, (sheared[0], sheared[1]), (dft_t[0], dft_t[1]))
    lane_first = lax.broadcasted_iota(jnp.int32, (8, H), 1) == 0
    sums = [None] * 8
    for q in range(PAIRS):
        cb, sb = rows_tables[q, 0, 64:72, :], rows_tables[q, 1, 64:72, :]
        near = rows_tables[q, :, pl.ds(pl.multiple_of(8 * block, 8), 8), :]
        for u in range(8):
            ca, sa = near[0, u : u + 1, :], near[1, u : u + 1, :]
            c, s = ca * cb - sa * sb, sa * cb + ca * sb
            c_first, s_first = jnp.where(lane_first, 1.0, c), jnp.where(lane_first, 0.0, s)
            base = 2 * 64 * q + 8 * u
            one, two = spectrum[base : base + 8, :], spectrum[base + 64 : base + 72, :]
            both, apart = one + two, one - two
            unturned = jnp.concatenate(
                [both[:, :H] * c_first + apart[:, H:] * s_first, both[:, H:] * c - apart[:, :H] * s_first], 1
            )
            sums[u] = unturned if q == 0 else sums[u] + unturned
    weight = jnp.where(lax.broadcasted_iota(jnp.int32, (64, N), 1) % H == 0, 0.5 / 32.0, 1.0 / 32.0)
    whole = jnp.concatenate(sums, 0) * weight
    zeros = jnp.zeros((64, N), BF16)
    high, low = split(whole)
    result = None
    for side in range(2):
        dft_rows = [
            jnp.concatenate([dft_t[p, 64 * a + 32 * side : 64 * a + 32 * side + 32, :] for a in range(ANGLES)], 0)
            for p in range(2)
        ]
        order = (lambda v: [v, zeros]) if side == 0 else (lambda v: [zeros, v])
        columns = (jnp.concatenate(order(high), 0), jnp.concatenate(order(low), 0))
        part = three(mm_t, dft_rows, columns)
        result = part if result is None else result + part
    for peer in range(16):
        a = peer // 2
        out[peer, :CHUNK, :] = chunk
        out[peer, CHUNK:, :] = result[32 * a : 32 * a + 32, :]


def assemble_kernel(received, out):
    xl = lax.axis_index("xl")
    lower = lax.broadcasted_iota(jnp.int32, (32, W), 1) < 64
    for b in range(4):
        even = received[4 * b + xl, CHUNK:, :]
        odd = received[4 * b + 2 + xl, CHUNK:, :]
        lanes = slice(b * W, (b + 1) * W)
        out[0, :32, lanes] = jnp.where(lower, even, pltpu.roll(odd, 64, 1))
        out[0, 32:, lanes] = jnp.where(lower, pltpu.roll(even, 64, 1), odd)


def forward_call(*args):
    return pl.pallas_call(
        forward_kernel,
        in_specs=[pl.BlockSpec(memory_space=pltpu.SMEM)] + [pl.BlockSpec(memory_space=pl.ANY)] * 5,
        out_specs=pl.BlockSpec(memory_space=pltpu.VMEM),
        out_shape=jax.ShapeDtypeStruct((4 * ROWS, W), F32),
        scratch_shapes=[
            pltpu.VMEM((N, N), BF16),
            pltpu.VMEM((2, N, N), BF16),
            pltpu.VMEM((2, N, N), BF16),
            pltpu.VMEM((H // 4 + 24, N), F32),
            pltpu.VMEM((2, N, N), BF16),
            pltpu.VMEM((N, N), F32),
        ]
        + [pltpu.VMEM((N, N), BF16)] * 4
        + [pltpu.SemaphoreType.DMA((5,))],
        compiler_params=pltpu.CompilerParams(vmem_limit_bytes=60 * 1024 * 1024),
        cost_estimate=pl.CostEstimate(flops=4 * 10**9, bytes_accessed=4 * 10**6, transcendentals=0),
        name="forward",
    )(*args)


def vmem_call(kernel, outs, scratch, name, *args):
    result = pl.pallas_call(
        kernel,
        in_specs=[
            pl.BlockSpec(memory_space=pltpu.SMEM if a.dtype == jnp.int32 else pltpu.VMEM) for a in args
        ],
        out_specs=[pl.BlockSpec(memory_space=pltpu.VMEM)] * len(outs),
        out_shape=[jax.ShapeDtypeStruct(o, F32) for o in outs],
        scratch_shapes=scratch,
        compiler_params=pltpu.CompilerParams(vmem_limit_bytes=32 * 1024 * 1024),
        cost_estimate=pl.CostEstimate(flops=3 * 10**9, bytes_accessed=4 * 10**6, transcendentals=0),
        name=name,
    )(*args)
    return result if len(outs) > 1 else result[0]


GZ = ("xl", "z", "core")
PLANE = ("y", "xh", "xl")


def exchange(blocks, axes):
    return lax.all_to_all(blocks, axes, split_axis=0, concat_axis=0, tiled=True)


def swap(rows):
    return lax.ppermute(rows, "core", [(0, 1), (1, 0)])


def local(volume, probe, measured, angle_index, row_offset, col_offset):
    dft, dft_t = (jnp.asarray(t) for t in dft_tables())
    dfts = jnp.asarray(window_tables())
    factors, rows_tables, all_beams = phase_tables()
    factors, rows_tables, all_beams = jnp.asarray(factors), jnp.asarray(rows_tables), jnp.asarray(all_beams)
    beams = [jnp.asarray(b) for b in np.asarray(phase_tables()[2])]
    row = forward_call(angle_index, volume, dft, dft_t, factors, all_beams)
    whole = exchange(row.reshape(ROWS, 4, W), GZ).reshape(4 * ROWS, W)
    keep, send = vmem_call(
        window_kernel,
        [(HALF + 64, W)] * 2,
        [
            pltpu.VMEM((MODES // 2, 2 * W, 2 * W), F32),
            pltpu.VMEM((MODES * W, 2 * W), F32),
            pltpu.VMEM((4, ROWS, W), F32),
        ],
        "window",
        row_offset,
        col_offset,
        whole,
        probe,
        measured,
        dfts,
    )
    packed = vmem_call(pack_kernel, [(16, CHUNK + 40, W)], [], "pack", angle_index, keep, swap(send))
    shared = exchange(packed, PLANE)
    relay = vmem_call(relay_kernel, [(8, CHUNK + 32, W)], [pltpu.VMEM((256, W), F32)], "relay", shared)
    rows = exchange(relay, "z")
    blocks = vmem_call(
        adjoint_kernel,
        [(16, CHUNK + 32, W)],
        [pltpu.VMEM((32, W), F32), pltpu.VMEM((2, N, N), BF16), pltpu.VMEM((2, N, N), BF16)],
        "adjoint",
        rows,
        dft_t,
        rows_tables,
        *beams,
    )
    final = exchange(blocks, PLANE)
    mine = final[:, :CHUNK, :].reshape(HALF, W)
    other = swap(mine)
    volume_update = vmem_call(assemble_kernel, [(1, 64, N)], [], "assemble", final)
    core = lax.axis_index("core")
    probe_update = jnp.where(core == 0, jnp.stack([mine, other]), jnp.stack([other, mine]))
    return volume_update, probe_update.reshape(MODES, 2, W, W)


def solution(mesh):
    split_mesh = Mesh(mesh.devices.reshape(4, 2, 2, 8, 2), ("y", "xh", "xl", "z", "core"))
    angle, gz = ("y", "xh"), GZ
    return jax.shard_map(
        local,
        mesh=split_mesh,
        in_specs=(
            P(gz, None, None),
            P(),
            P(angle, gz, None, None),
            P(angle),
            P(angle, gz),
            P(angle, gz),
        ),
        out_specs=(P(gz, angle, None), P()),
        check_vma=False,
    )
```

```python
import math

import jax
import jax.numpy as jnp
import numpy as np
from jax import lax
from jax.experimental import pallas as pl
from jax.experimental.pallas import tpu as pltpu
from jax.sharding import Mesh, PartitionSpec as P

N = 512
H = N // 2
W = 128
MODES = 8
ANGLES = 8
PAIRS = ANGLES // 2
ROWS = 32
HALF = MODES * 2 * W // 2
CHUNK = HALF // 16
F32 = jnp.float32
BF16 = jnp.bfloat16


def split_const(table):
    high = table.astype(BF16)
    low = (table - high.astype(np.float64)).astype(BF16)
    return np.stack([high, low])


def dft_tables():
    k, n = np.arange(H)[:, None], np.arange(N)[None, :]
    turns = np.pi / N * (k * (2 * n + 1) % (2 * N))
    table = np.concatenate([np.cos(turns), -np.sin(turns)], 0)
    table[H] = 2.0 * (np.arange(N) % 2) - 1.0
    return split_const(table), split_const(np.ascontiguousarray(table.T))


def window_tables():
    j = np.arange(W)
    turns = 2.0 * np.pi / W * (j[:, None] * j[None, :] % W)
    c, s = np.cos(turns), np.sin(turns)
    return np.stack([split_const(np.block([[c, s], [-s, c]])), split_const(np.block([[c, -s], [s, c]]))])


def shears():
    theta = np.pi * (np.arange(ANGLES) + 0.5) / ANGLES - np.pi / 2
    return -np.tan(theta / 2), np.sin(theta)


def cos_sin(phase):
    return np.stack([np.cos(phase), np.sin(phase)], 1)


def phase_tables():
    shear_x, shear_y = shears()
    cells = np.arange(N) - N / 2
    unit_one = -2.0 * np.pi / N * shear_x
    unit_two = -2.0 * np.pi / N * shear_y[:PAIRS]
    by_y = unit_one[:, None, None] * np.concatenate([cells[:H], cells[:H - 1:-1]])[None, None, :]
    nyquist = np.ones((ANGLES, 8, N))
    nyquist[:, 0] = 0.5 * np.cos(by_y[:, 0] * H)
    factors = np.concatenate(
        [
            cos_sin(by_y * (8 * np.arange(H // 8))[None, :, None]).reshape(ANGLES, H // 4, N),
            cos_sin(by_y * np.arange(8)[None, :, None]).reshape(ANGLES, 16, N),
            nyquist,
        ],
        1,
    )
    freq = np.arange(H, dtype=np.float64)
    freq[0] = H
    by_k = unit_one[:PAIRS, None, None] * freq[None, None, :]
    rows_coarse = cos_sin(by_k * cells[::8][None, :, None])
    rows_fine = cos_sin(by_k * np.arange(8)[None, :, None])
    rows_tables = np.concatenate([rows_coarse, rows_fine], 2)
    frequencies = np.arange(H, dtype=np.float64)
    turns = unit_two[:, None, None] * frequencies[None, :, None] * (H - 0.5 - np.arange(H))[None, None, :]
    low = np.cos(unit_two[:, None] * H * cells[None, :H])
    high = np.cos(unit_two[:, None] * H * cells[None, :H - 1:-1])
    table = np.concatenate([np.cos(turns), np.sin(turns)], 1)
    table[:, H] = 0.5 * (low - high)
    beams = np.ascontiguousarray(np.moveaxis(split_const(table), 0, 1))
    edges = np.zeros((PAIRS, 8, H))
    edges[:, 0] = 0.5 * (low + high)
    middle = 0.5 * unit_two[:, None] * frequencies[None, :]
    ordered = np.stack([middle, -middle], 1).reshape(ANGLES, H)
    middles = np.concatenate([np.cos(ordered), np.sin(ordered)], 0)
    return [t if t.dtype == BF16 else t.astype(np.float32) for t in (factors, rows_tables, beams, edges, middles)]


def mm(a, b):
    return lax.dot_general(a, b, (((1,), (0,)), ((), ())), preferred_element_type=F32)


def mm_t(a, b):
    return lax.dot_general(a, b, (((1,), (1,)), ((), ())), preferred_element_type=F32)


def split(value):
    high = value.astype(BF16)
    return high, (value - high.astype(F32)).astype(BF16)


def three(dot, a, b):
    return dot(a[0], b[0]) + (dot(a[0], b[1]) + dot(a[1], b[0]))


def forward_kernel(
    sc, volume, dft_hbm, dft_t_hbm, factors_hbm, beams_hbm, edges_hbm, out,
    slab, dft, dft_t, factors, beams, edges, spec, turned, field, sems,
):
    number = sc[0]
    mirrored = number >= PAIRS
    sign = jnp.where(mirrored, -1.0, 1.0)
    folded = jnp.where(mirrored, ANGLES - 1 - number, number)
    copies = [
        (volume.at[0], slab),
        (dft_hbm, dft),
        (factors_hbm.at[number], factors),
        (dft_t_hbm.at[:, pl.ds(0, H), :], dft_t),
        (beams_hbm.at[folded], beams),
        (edges_hbm.at[folded], edges),
    ]
    moves = [pltpu.make_async_copy(source, target, sems.at[i]) for i, (source, target) in enumerate(copies)]
    for move in moves:
        move.start()
    halves = (slice(0, H), slice(H, N))
    rows, lanes = (lax.broadcasted_iota(jnp.int32, (H, H), axis) for axis in (0, 1))
    reverse = jnp.where(rows + lanes == H - 1, 1.0, 0.0).astype(BF16)
    moves[0].wait()
    backward = mm(slab[:, H:], reverse).astype(BF16)
    moves[1].wait()
    for lanes, columns in zip(halves, (slab[:, :H], backward)):
        spec[:, lanes] = mm(dft[0], columns) + mm(dft[1], columns)
    moves[2].wait()
    half_row = jnp.where(lax.broadcasted_iota(jnp.int32, (8, H), 0) == 0, 0.5, 1.0)
    for lanes in halves:
        cb, sb = factors[64:72, lanes], factors[72:80, lanes]
        for pair in range(H // 16):
            reals, imags = [], []
            for u in (2 * pair, 2 * pair + 1):
                ca, sa = factors[u : u + 1, lanes], factors[32 + u : 33 + u, lanes]
                c, s = ca * cb - sa * sb, sa * cb + ca * sb
                a, b = spec[8 * u : 8 * u + 8, lanes], spec[H + 8 * u : H + 8 * u + 8, lanes]
                real, imag = a * c - b * s, a * s + b * c
                if u == 0:
                    real, imag = real * half_row, imag * factors[80:88, lanes]
                reals.append(real)
                imags.append(imag)
            for base, parts in ((16 * pair, reals), (H + 16 * pair, imags)):
                at = slice(base, base + 16)
                turned[0, at, lanes], turned[1, at, lanes] = split(jnp.concatenate(parts, 0))
    moves[3].wait()
    for part, comps in enumerate(halves):
        both = three(mm, (dft_t[0, :, comps], dft_t[1, :, comps]), (turned[0, comps, :], turned[1, comps, :]))
        field[0, 0, comps, :], field[0, 1, comps, :] = split(both[:, :H] + both[:, H:])
        field[1, 0, comps, :], field[1, 1, comps, :] = split(both[:, :H] - both[:, H:])
    for part, comps in enumerate(halves):
        spec[comps, :] = three(mm_t, (dft[0, comps, :H], dft[1, comps, :H]), (field[part, 0], field[part, 1]))
    moves[4].wait()
    moves[5].wait()
    total = jnp.zeros((8, N), F32)
    for r in range(0, H, 32):
        real_even, real_odd = spec[r : r + 32, :H], spec[r : r + 32, H:]
        imag_even, imag_odd = spec[H + r : H + r + 32, :H], spec[H + r : H + r + 32, H:]
        c = beams[0, r : r + 32, :].astype(F32) + beams[1, r : r + 32, :].astype(F32)
        s = beams[0, H + r : H + r + 32, :].astype(F32) + beams[1, H + r : H + r + 32, :].astype(F32)
        c_imag, s_imag, extra = c, s * sign, None
        if r == 0:
            top = lax.broadcasted_iota(jnp.int32, (32, H), 0) == 0
            extra = jnp.where(top, imag_odd * s, 0.0)
            c_imag = jnp.where(top, edges[0:1, :], c)
            s_imag = jnp.where(top, 0.0, s_imag)
        real_terms = real_even * c + imag_odd * s_imag
        imag_terms = imag_even * c_imag - real_odd * s_imag
        if extra is not None:
            imag_terms = imag_terms + extra
        real = jnp.sum(real_terms, axis=1, keepdims=True)
        imag = jnp.sum(imag_terms, axis=1, keepdims=True)
        if r == 0:
            weight = jnp.where(lax.broadcasted_iota(jnp.int32, (32, 1), 0) == 0, 0.5, 1.0)
            real, imag = real * weight, imag * weight
        c_mid, s_mid = c[:, H - 1 :], s_imag[:, H - 1 :]
        real, imag = real * c_mid + imag * s_mid, imag * c_mid - real * s_mid
        f_real = dft[0, r : r + 32, :].astype(F32) + dft[1, r : r + 32, :].astype(F32)
        f_imag = dft[0, H + r : H + r + 32, :].astype(F32) + dft[1, H + r : H + r + 32, :].astype(F32)
        terms = real * f_real + imag * f_imag
        total = total + jnp.sum(terms.reshape(4, 8, N), axis=0)
    row = jnp.sum(total, axis=0, keepdims=True) * (8.0 / (N * N))
    for t in range(4):
        out[pl.ds(t, ROWS, stride=4), :] = jnp.broadcast_to(row[:, t * W : (t + 1) * W], (ROWS, W))


def turn(block):
    return jnp.concatenate(
        [
            jnp.concatenate([block[:W, :W], block[W:, :W]], 1),
            jnp.concatenate([block[:W, W:], block[W:, W:]], 1),
        ],
        0,
    )


def window_kernel(row_ref, col_ref, whole, probe, measured, dfts, keep, send, stage, far, pieces):
    row, col, core = jnp.max(row_ref[...]), jnp.max(col_ref[...]), lax.axis_index("core")
    rows = jnp.concatenate([whole[pl.ds(t, ROWS, stride=4), :] for t in range(4)], axis=1)
    band = pltpu.roll(rows, lax.rem(N - col, N), 1)[:, :W]
    pad = jnp.zeros((W - ROWS, W), F32)
    obj_real = pltpu.roll(jnp.concatenate([jnp.cos(band) - 1.0, pad], 0), -row, 0) + 1.0
    obj_imag = pltpu.roll(jnp.concatenate([jnp.sin(band), pad], 0), -row, 0)
    lefts, rights = (dfts[0, 0], dfts[0, 1]), (dfts[1, 0], dfts[1, 1])
    pairs = [(j, j + MODES // 2) for j in range(MODES // 2)]
    sides = (slice(0, W), slice(W, 2 * W))

    def put(j, value):
        stage[0, j], stage[1, j] = split(value)

    def get(j):
        return stage[0, j], stage[1, j]

    for j, pair in enumerate(pairs):
        reals = [probe[m, 0] * obj_real - probe[m, 1] * obj_imag for m in pair]
        imags = [probe[m, 0] * obj_imag + probe[m, 1] * obj_real for m in pair]
        put(j, jnp.concatenate([jnp.concatenate(reals, 1), jnp.concatenate(imags, 1)], 0))
    for j in range(MODES // 2):
        put(j, turn(three(mm, lefts, get(j))))
    intensity = jnp.zeros((W, W), F32)
    for j in range(MODES // 2):
        waves = three(mm, get(j), rights)
        far[j] = waves
        power = waves * waves
        power = power[:W] + power[W:]
        intensity = intensity + (power[:, :W] + power[:, W:])
    factor = (1.0 - jnp.sqrt(measured[0, 0] + 1.0) / jnp.sqrt(intensity + 1.0)) * (1.0 / W)
    factors = jnp.concatenate([jnp.concatenate([factor, factor], 1)] * 2, 0)
    for j in range(MODES // 2):
        put(j, far[j] * factors)
    for j in range(MODES // 2):
        put(j, turn(three(mm, get(j), lefts)))
    grad_real, grad_imag = jnp.zeros((W, W), F32), jnp.zeros((W, W), F32)
    for j, pair in enumerate(pairs):
        back = three(mm, rights, get(j))
        grads = []
        for m, lanes in zip(pair, sides):
            b_real, b_imag = back[:W, lanes], back[W:, lanes]
            p_real, p_imag = probe[m, 0], probe[m, 1]
            grad_real = grad_real + (p_real * b_real + p_imag * b_imag)
            grad_imag = grad_imag + (p_real * b_imag - p_imag * b_real)
            grads.append((obj_real * b_real + obj_imag * b_imag, obj_real * b_imag - obj_imag * b_real))
        for part in range(2):
            at = slice((2 * j + part) * W, (2 * j + part + 1) * W)
            keep[at, :] = jnp.where(core == 0, grads[0][part], grads[1][part])
            send[at, :] = jnp.where(core == 0, grads[1][part], grads[0][part])
    patch = grad_imag * obj_real - grad_real * obj_imag
    shown = pltpu.roll(patch, W + row, 0)[:ROWS]
    wide = pltpu.roll(jnp.concatenate([shown, jnp.zeros((ROWS, N - W), F32)], 1), col, 1)
    for t in range(4):
        pieces[t] = wide[:, t * W : (t + 1) * W]
    for t in range(4):
        at = slice(HALF + 16 * t, HALF + 16 * (t + 1))
        even, odd = pieces[t, pl.ds(0, 16, stride=2), :], pieces[t, pl.ds(1, 16, stride=2), :]
        keep[at, :] = jnp.where(core == 0, even, odd)
        send[at, :] = jnp.where(core == 0, odd, even)


def pack_kernel(sc, keep, other, out):
    angle = jnp.broadcast_to(sc[0].astype(F32), (8, W))
    for peer in range(16):
        rows = slice(CHUNK * peer, CHUNK * (peer + 1))
        out[peer, :CHUNK, :] = keep[rows, :] + other[rows, :]
        for t in range(4):
            base = HALF + 16 * t + 8 * (peer % 2)
            out[peer, CHUNK + 8 * t : CHUNK + 8 * t + 8, :] = keep[base : base + 8, :] + other[base : base + 8, :]
        out[peer, CHUNK + 32 :, :] = angle


def relay_kernel(received, out, pieces):
    total = received[0, :CHUNK, :]
    for peer in range(1, 16):
        total = total + received[peer, :CHUNK, :]
    for a in range(ANGLES):
        number = jnp.max(received[2 * a, CHUNK + 32 :, :]).astype(jnp.int32)
        slot = jnp.where(number >= PAIRS, 2 * (ANGLES - 1 - number) + 1, 2 * number)
        pieces[pl.ds(pl.multiple_of(32 * slot, 32), 32), :] = (
            received[2 * a, CHUNK : CHUNK + 32, :] + received[2 * a + 1, CHUNK : CHUNK + 32, :]
        )
    for z in range(8):
        out[z, :CHUNK, :] = total
        out[z, CHUNK:, :] = pieces[pl.ds(z, 32, stride=8), :]


def adjoint_kernel(received, dft_t, rows_tables, edges, middles, *refs):
    beams, (out, pieces, shifted, sheared) = refs[:PAIRS], refs[PAIRS:]
    block = 2 * lax.axis_index("y") + lax.axis_index("xh")
    total = received[0]
    for z in range(1, 8):
        total = total + received[z]
    chunk = total[:CHUNK] * (1.0 / 16.0)
    pieces[...] = total[CHUNK:]
    rows = jnp.concatenate([pieces[pl.ds(t, 8, stride=4), :] for t in range(4)], axis=1)
    spectrum = three(mm, split(rows), (dft_t[0], dft_t[1]))
    weight = jnp.where(lax.broadcasted_iota(jnp.int32, (8, N), 1) % H == 0, 0.5 / N, 1.0 / N)
    cbar = spectrum * weight
    c_mid, s_mid = middles[:ANGLES, :], middles[ANGLES:, :]
    c_reals = cbar[:, :H] * c_mid - cbar[:, H:] * s_mid
    c_imags = cbar[:, H:] * c_mid + cbar[:, :H] * s_mid
    at = pl.ds(pl.multiple_of(64 * block, 64), 64)
    rows_dft = dft_t[0, at, :].astype(F32) + dft_t[1, at, :].astype(F32)
    lane_zero = lax.broadcasted_iota(jnp.int32, (64, H), 1) == 0
    r_cos, r_sin = rows_dft[:, :H], rows_dft[:, H:]
    r_sin_real = jnp.where(lane_zero, 0.0, r_sin)
    r_cos_imag = jnp.where(lane_zero, r_sin, r_cos)
    mirror = jnp.where(lane_zero, 1.0, -1.0)
    nyquist = []
    for slot in range(ANGLES):
        c_real, c_imag = c_reals[slot : slot + 1, :], c_imags[slot : slot + 1, :]
        cosines = c_real * r_cos + c_imag * r_sin_real
        sines = c_imag * r_cos_imag - c_real * r_sin_real
        if slot % 2 == 0:
            sines = sines * mirror
        nyquist.append(sines[:, :1])
        at = slice(64 * slot, 64 * slot + 64)
        shifted[0, at, :H], shifted[1, at, :H] = split(cosines)
        shifted[0, at, H:], shifted[1, at, H:] = split(sines)
    for q in range(PAIRS):
        at = slice(2 * 64 * q, 2 * 64 * (q + 1))
        even = three(mm, (shifted[0, at, :H], shifted[1, at, :H]), (beams[q][0, :H, :], beams[q][1, :H, :]))
        odd = three(mm, (shifted[0, at, H:], shifted[1, at, H:]), (beams[q][0, H:, :], beams[q][1, H:, :]))
        even = even + jnp.concatenate(nyquist[2 * q : 2 * q + 2], 0) * edges[q, 0:1, :]
        sheared[0, at, :H], sheared[1, at, :H] = split(even)
        sheared[0, at, H:], sheared[1, at, H:] = split(odd)
    spectrum = jnp.concatenate(
        [
            three(
                mm, (sheared[0, :, part], sheared[1, :, part]), (dft_t[0, :H, part], dft_t[1, :H, part])
            )
            for part in (slice(0, H), slice(H, N))
        ],
        1,
    )
    lane_first = lax.broadcasted_iota(jnp.int32, (8, H), 1) == 0
    sums = [None] * 8
    for q in range(PAIRS):
        cb, sb = rows_tables[q, 0, 64:72, :], rows_tables[q, 1, 64:72, :]
        near = rows_tables[q, :, pl.ds(pl.multiple_of(8 * block, 8), 8), :]
        for u in range(8):
            ca, sa = near[0, u : u + 1, :], near[1, u : u + 1, :]
            c, s = ca * cb - sa * sb, sa * cb + ca * sb
            c_first, s_first = jnp.where(lane_first, 1.0, c), jnp.where(lane_first, 0.0, s)
            base = 2 * 64 * q + 8 * u
            one, two = spectrum[base : base + 8, :], spectrum[base + 64 : base + 72, :]
            both, apart = one + two, one - two
            unturned = jnp.concatenate(
                [both[:, :H] * c_first + apart[:, H:] * s_first, both[:, H:] * c - apart[:, :H] * s_first], 1
            )
            sums[u] = unturned if q == 0 else sums[u] + unturned
    weight = jnp.where(lax.broadcasted_iota(jnp.int32, (64, N), 1) % H == 0, 1.0 / 32.0, 1.0 / 16.0)
    whole = jnp.concatenate(sums, 0) * weight
    zeros = jnp.zeros((64, N), BF16)
    high, low = split(whole)
    result = None
    for side in range(2):
        dft_rows = [
            jnp.concatenate([dft_t[p, 64 * a + 32 * side : 64 * a + 32 * side + 32, :] for a in range(ANGLES)], 0)
            for p in range(2)
        ]
        order = (lambda v: [v, zeros]) if side == 0 else (lambda v: [zeros, v])
        columns = (jnp.concatenate(order(high), 0), jnp.concatenate(order(low), 0))
        part = three(mm_t, dft_rows, columns)
        result = part if result is None else result + part
    for peer in range(16):
        a = peer // 2
        out[peer, :CHUNK, :] = chunk
        out[peer, CHUNK:, :] = result[32 * a : 32 * a + 32, :]


def assemble_kernel(received, out):
    xl = lax.axis_index("xl")
    lower = lax.broadcasted_iota(jnp.int32, (32, W), 1) < 64
    for b in range(4):
        even = received[4 * b + xl, CHUNK:, :]
        odd = received[4 * b + 2 + xl, CHUNK:, :]
        lanes = slice(b * W, (b + 1) * W)
        out[0, :32, lanes] = jnp.where(lower, even, pltpu.roll(odd, 64, 1))
        out[0, 32:, lanes] = jnp.where(lower, pltpu.roll(even, 64, 1), odd)


def forward_call(*args):
    return pl.pallas_call(
        forward_kernel,
        in_specs=[pl.BlockSpec(memory_space=pltpu.SMEM)] + [pl.BlockSpec(memory_space=pl.ANY)] * 6,
        out_specs=pl.BlockSpec(memory_space=pltpu.VMEM),
        out_shape=jax.ShapeDtypeStruct((4 * ROWS, W), F32),
        scratch_shapes=[
            pltpu.VMEM((N, N), BF16),
            pltpu.VMEM((2, N, N), BF16),
            pltpu.VMEM((2, H, N), BF16),
            pltpu.VMEM((H // 4 + 24, N), F32),
            pltpu.VMEM((2, N, H), BF16),
            pltpu.VMEM((8, H), F32),
            pltpu.VMEM((N, N), F32),
            pltpu.VMEM((2, N, N), BF16),
            pltpu.VMEM((2, 2, N, H), BF16),
            pltpu.SemaphoreType.DMA((6,)),
        ],
        compiler_params=pltpu.CompilerParams(vmem_limit_bytes=60 * 1024 * 1024),
        cost_estimate=pl.CostEstimate(flops=4 * 10**9, bytes_accessed=4 * 10**6, transcendentals=0),
        name="forward",
    )(*args)


def vmem_call(kernel, outs, scratch, name, *args):
    result = pl.pallas_call(
        kernel,
        in_specs=[
            pl.BlockSpec(memory_space=pltpu.SMEM if a.shape == (1,) else pltpu.VMEM) for a in args
        ],
        out_specs=[pl.BlockSpec(memory_space=pltpu.VMEM)] * len(outs),
        out_shape=[jax.ShapeDtypeStruct(o, F32) for o in outs],
        scratch_shapes=scratch,
        compiler_params=pltpu.CompilerParams(vmem_limit_bytes=32 * 1024 * 1024),
        cost_estimate=pl.CostEstimate(flops=3 * 10**9, bytes_accessed=4 * 10**6, transcendentals=0),
        name=name,
    )(*args)
    return result if len(outs) > 1 else result[0]


GZ = ("xl", "z", "core")
PLANE = ("y", "xh", "xl")


def exchange(blocks, axes):
    return lax.all_to_all(blocks, axes, split_axis=0, concat_axis=0, tiled=True)


def swap(rows):
    return lax.ppermute(rows, "core", [(0, 1), (1, 0)])


def local(volume, probe, measured, angle_index, row_offset, col_offset):
    dft, dft_t = (jnp.asarray(t) for t in dft_tables())
    dfts = jnp.asarray(window_tables())
    factors, rows_tables, all_beams, edges, middles = (jnp.asarray(t) for t in phase_tables())
    beams = [jnp.asarray(b) for b in phase_tables()[2]]
    row = forward_call(angle_index, volume, dft, dft_t, factors, all_beams, edges)
    whole = exchange(row.reshape(ROWS, 4, W), GZ).reshape(4 * ROWS, W)
    keep, send = vmem_call(
        window_kernel,
        [(HALF + 64, W)] * 2,
        [
            pltpu.VMEM((2, MODES // 2, 2 * W, 2 * W), BF16),
            pltpu.VMEM((MODES // 2, 2 * W, 2 * W), F32),
            pltpu.VMEM((4, ROWS, W), F32),
        ],
        "window",
        row_offset,
        col_offset,
        whole,
        probe,
        measured,
        dfts,
    )
    packed = vmem_call(pack_kernel, [(16, CHUNK + 40, W)], [], "pack", angle_index, keep, swap(send))
    shared = exchange(packed, PLANE)
    relay = vmem_call(relay_kernel, [(8, CHUNK + 32, W)], [pltpu.VMEM((256, W), F32)], "relay", shared)
    rows = exchange(relay, "z")
    blocks = vmem_call(
        adjoint_kernel,
        [(16, CHUNK + 32, W)],
        [pltpu.VMEM((32, W), F32), pltpu.VMEM((2, N, N), BF16), pltpu.VMEM((2, N, N), BF16)],
        "adjoint",
        rows,
        dft_t,
        rows_tables,
        edges,
        middles,
        *beams,
    )
    final = exchange(blocks, PLANE)
    mine = final[:, :CHUNK, :].reshape(HALF, W)
    other = swap(mine)
    volume_update = vmem_call(assemble_kernel, [(1, 64, N)], [], "assemble", final)
    core = lax.axis_index("core")
    held = lax.optimization_barrier(jnp.stack([mine, mine]))
    probe_update = lax.dynamic_update_slice(held, other[None], (1 - core, 0, 0))
    return volume_update, probe_update.reshape(MODES, 2, W, W)


def solution(mesh):
    split_mesh = Mesh(mesh.devices.reshape(4, 2, 2, 8, 2), ("y", "xh", "xl", "z", "core"))
    angle, gz = ("y", "xh"), GZ
    return jax.shard_map(
        local,
        mesh=split_mesh,
        in_specs=(
            P(gz, None, None),
            P(),
            P(angle, gz, None, None),
            P(angle),
            P(angle, gz),
            P(angle, gz),
        ),
        out_specs=(P(gz, angle, None), P()),
        check_vma=False,
    )
```

```python
import math

import jax
import jax.numpy as jnp
import numpy as np
from jax import lax
from jax.experimental import pallas as pl
from jax.experimental.pallas import tpu as pltpu
from jax.sharding import Mesh, PartitionSpec as P

N = 512
H = N // 2
W = 128
MODES = 8
ANGLES = 8
PAIRS = ANGLES // 2
ROWS = 32
HALF = MODES * 2 * W // 2
CHUNK = HALF // 16
MESSAGE = CHUNK + 17
F32 = jnp.float32
BF16 = jnp.bfloat16


def split_const(table):
    high = table.astype(BF16)
    low = (table - high.astype(np.float64)).astype(BF16)
    return np.stack([high, low])


def dft_tables():
    k, n = np.arange(H)[:, None], np.arange(N)[None, :]
    turns = np.pi / N * (k * (2 * n + 1) % (2 * N))
    table = np.concatenate([np.cos(turns), -np.sin(turns)], 0)
    table[H] = 2.0 * (np.arange(N) % 2) - 1.0
    return split_const(table), split_const(np.ascontiguousarray(table.T))


def window_tables():
    j = np.arange(W)
    turns = 2.0 * np.pi / W * (j[:, None] * j[None, :] % W)
    c, s = np.cos(turns), np.sin(turns)
    return np.stack([split_const(np.block([[c, s], [-s, c]])), split_const(np.block([[c, -s], [s, c]]))])


def shears():
    theta = np.pi * (np.arange(ANGLES) + 0.5) / ANGLES - np.pi / 2
    return -np.tan(theta / 2), np.sin(theta)


def cos_sin(phase):
    return np.stack([np.cos(phase), np.sin(phase)], 1)


def phase_tables():
    shear_x, shear_y = shears()
    cells = np.arange(N) - N / 2
    unit_one = -2.0 * np.pi / N * shear_x
    unit_two = -2.0 * np.pi / N * shear_y[:PAIRS]
    by_y = unit_one[:, None, None] * np.concatenate([cells[:H], cells[:H - 1:-1]])[None, None, :]
    nyquist = np.ones((ANGLES, 8, N))
    nyquist[:, 0] = 0.5 * np.cos(by_y[:, 0] * H)
    factors = np.concatenate(
        [
            cos_sin(by_y * (8 * np.arange(H // 8))[None, :, None]).reshape(ANGLES, H // 4, N),
            cos_sin(by_y * np.arange(8)[None, :, None]).reshape(ANGLES, 16, N),
            nyquist,
        ],
        1,
    )
    freq = np.arange(H, dtype=np.float64)
    freq[0] = H
    by_k = unit_one[:PAIRS, None, None] * freq[None, None, :]
    rows_coarse = cos_sin(by_k * cells[::8][None, :, None])
    rows_fine = cos_sin(by_k * np.arange(8)[None, :, None])
    rows_tables = np.concatenate([rows_coarse, rows_fine], 2)
    frequencies = np.arange(H, dtype=np.float64)
    turns = unit_two[:, None, None] * frequencies[None, :, None] * (H - 0.5 - np.arange(H))[None, None, :]
    low = np.cos(unit_two[:, None] * H * cells[None, :H])
    high = np.cos(unit_two[:, None] * H * cells[None, :H - 1:-1])
    table = np.concatenate([np.cos(turns), np.sin(turns)], 1)
    table[:, H] = 0.5 * (low - high)
    beams = np.ascontiguousarray(np.moveaxis(split_const(table), 0, 1))
    edges = np.zeros((PAIRS, 8, H))
    edges[:, 0] = 0.5 * (low + high)
    middle = 0.5 * unit_two[:, None] * frequencies[None, :]
    ordered = np.stack([middle, -middle], 1).reshape(ANGLES, H)
    middles = np.concatenate([np.cos(ordered), np.sin(ordered)], 0)
    return [t if t.dtype == BF16 else t.astype(np.float32) for t in (factors, rows_tables, beams, edges, middles)]


def mm(a, b):
    return lax.dot_general(a, b, (((1,), (0,)), ((), ())), preferred_element_type=F32)


def mm_t(a, b):
    return lax.dot_general(a, b, (((1,), (1,)), ((), ())), preferred_element_type=F32)


def split(value):
    high = value.astype(BF16)
    return high, (value - high.astype(F32)).astype(BF16)


def three(dot, a, b):
    rows = a[0].shape[0]
    both = dot(jnp.concatenate([a[0], a[1]], 0), b[0])
    return both[:rows] + (both[rows:] + dot(a[0], b[1]))


def forward_kernel(
    sc, volume, dft_hbm, dft_t_hbm, factors_hbm, beams_hbm, edges_hbm, out,
    slab, dft, dft_t, factors, beams, edges, spec, turned, field, sems,
):
    number = sc[0]
    mirrored = number >= PAIRS
    sign = jnp.where(mirrored, -1.0, 1.0)
    folded = jnp.where(mirrored, ANGLES - 1 - number, number)
    copies = [
        (volume.at[0], slab),
        (dft_hbm, dft),
        (factors_hbm.at[number], factors),
        (dft_t_hbm.at[:, pl.ds(0, H), :], dft_t),
        (beams_hbm.at[folded], beams),
        (edges_hbm.at[folded], edges),
    ]
    moves = [pltpu.make_async_copy(source, target, sems.at[i]) for i, (source, target) in enumerate(copies)]
    for move in moves:
        move.start()
    halves = (slice(0, H), slice(H, N))
    rows, lanes = (lax.broadcasted_iota(jnp.int32, (H, H), axis) for axis in (0, 1))
    reverse = jnp.where(rows + lanes == H - 1, 1.0, 0.0).astype(BF16)
    moves[0].wait()
    backward = mm(slab[:, H:], reverse).astype(BF16)
    moves[1].wait()
    moves[2].wait()
    for lanes, columns in zip(halves, (slab[:, :H], backward)):
        spec[:, lanes] = mm(dft[0], columns) + mm(dft[1], columns)
    half_row = jnp.where(lax.broadcasted_iota(jnp.int32, (8, H), 0) == 0, 0.5, 1.0)
    for lanes in halves:
        cb, sb = factors[64:72, lanes], factors[72:80, lanes]
        for pair in range(H // 16):
            reals, imags = [], []
            for u in (2 * pair, 2 * pair + 1):
                ca, sa = factors[u : u + 1, lanes], factors[32 + u : 33 + u, lanes]
                c, s = ca * cb - sa * sb, sa * cb + ca * sb
                a, b = spec[8 * u : 8 * u + 8, lanes], spec[H + 8 * u : H + 8 * u + 8, lanes]
                real, imag = a * c - b * s, a * s + b * c
                if u == 0:
                    real, imag = real * half_row, imag * factors[80:88, lanes]
                reals.append(real)
                imags.append(imag)
            for base, parts in ((16 * pair, reals), (H + 16 * pair, imags)):
                at = slice(base, base + 16)
                turned[0, at, lanes], turned[1, at, lanes] = split(jnp.concatenate(parts, 0))
    moves[3].wait()
    for part, comps in enumerate(halves):
        both = three(mm, (dft_t[0, :, comps], dft_t[1, :, comps]), (turned[0, comps, :], turned[1, comps, :]))
        field[0, 0, comps, :], field[0, 1, comps, :] = split(both[:, :H] + both[:, H:])
        field[1, 0, comps, :], field[1, 1, comps, :] = split(both[:, :H] - both[:, H:])
    for part, comps in enumerate(halves):
        spec[comps, :] = three(mm_t, (dft[0, comps, :H], dft[1, comps, :H]), (field[part, 0], field[part, 1]))
    moves[4].wait()
    moves[5].wait()
    total = jnp.zeros((8, N), F32)
    for r in range(0, H, 32):
        real_even, real_odd = spec[r : r + 32, :H], spec[r : r + 32, H:]
        imag_even, imag_odd = spec[H + r : H + r + 32, :H], spec[H + r : H + r + 32, H:]
        c = beams[0, r : r + 32, :].astype(F32) + beams[1, r : r + 32, :].astype(F32)
        s = beams[0, H + r : H + r + 32, :].astype(F32) + beams[1, H + r : H + r + 32, :].astype(F32)
        c_imag, s_imag, extra = c, s * sign, None
        if r == 0:
            top = lax.broadcasted_iota(jnp.int32, (32, H), 0) == 0
            extra = jnp.where(top, imag_odd * s, 0.0)
            c_imag = jnp.where(top, edges[0:1, :], c)
            s_imag = jnp.where(top, 0.0, s_imag)
        real_terms = real_even * c + imag_odd * s_imag
        imag_terms = imag_even * c_imag - real_odd * s_imag
        if extra is not None:
            imag_terms = imag_terms + extra
        real = jnp.sum(real_terms, axis=1, keepdims=True)
        imag = jnp.sum(imag_terms, axis=1, keepdims=True)
        if r == 0:
            weight = jnp.where(lax.broadcasted_iota(jnp.int32, (32, 1), 0) == 0, 0.5, 1.0)
            real, imag = real * weight, imag * weight
        c_mid, s_mid = c[:, H - 1 :], s_imag[:, H - 1 :]
        real, imag = real * c_mid + imag * s_mid, imag * c_mid - real * s_mid
        f_real = dft[0, r : r + 32, :].astype(F32) + dft[1, r : r + 32, :].astype(F32)
        f_imag = dft[0, H + r : H + r + 32, :].astype(F32) + dft[1, H + r : H + r + 32, :].astype(F32)
        terms = real * f_real + imag * f_imag
        total = total + jnp.sum(terms.reshape(4, 8, N), axis=0)
    row = jnp.sum(total, axis=0, keepdims=True) * (8.0 / (N * N))
    for t in range(4):
        out[pl.ds(t, ROWS, stride=4), :] = jnp.broadcast_to(row[:, t * W : (t + 1) * W], (ROWS, W))


def turn(block):
    return jnp.concatenate(
        [
            jnp.concatenate([block[:W, :W], block[W:, :W]], 1),
            jnp.concatenate([block[:W, W:], block[W:, W:]], 1),
        ],
        0,
    )


def window_kernel(row_ref, col_ref, whole, probe, measured, dfts, keep, send, stage, far, pieces):
    row, col, core = jnp.max(row_ref[...]), jnp.max(col_ref[...]), lax.axis_index("core")
    rows = jnp.concatenate([whole[pl.ds(t, ROWS, stride=4), :] for t in range(4)], axis=1)
    band = pltpu.roll(rows, lax.rem(N - col, N), 1)[:, :W]
    pad = jnp.zeros((W - ROWS, W), F32)
    obj_real = pltpu.roll(jnp.concatenate([jnp.cos(band) - 1.0, pad], 0), -row, 0) + 1.0
    obj_imag = pltpu.roll(jnp.concatenate([jnp.sin(band), pad], 0), -row, 0)
    lefts, rights = (dfts[0, 0], dfts[0, 1]), (dfts[1, 0], dfts[1, 1])
    pairs = [(j, j + MODES // 2) for j in range(MODES // 2)]
    sides = (slice(0, W), slice(W, 2 * W))

    def put(j, value):
        stage[0, j], stage[1, j] = split(value)

    def get(j):
        return stage[0, j], stage[1, j]

    for j, pair in enumerate(pairs):
        reals = [probe[m, 0] * obj_real - probe[m, 1] * obj_imag for m in pair]
        imags = [probe[m, 0] * obj_imag + probe[m, 1] * obj_real for m in pair]
        put(j, jnp.concatenate([jnp.concatenate(reals, 1), jnp.concatenate(imags, 1)], 0))
    for j in range(MODES // 2):
        put(j, turn(three(mm, lefts, get(j))))
    intensity = jnp.zeros((W, W), F32)
    for j in range(MODES // 2):
        waves = three(mm, get(j), rights)
        far[j] = waves
        power = waves * waves
        power = power[:W] + power[W:]
        intensity = intensity + (power[:, :W] + power[:, W:])
    factor = (1.0 - jnp.sqrt(measured[0, 0] + 1.0) / jnp.sqrt(intensity + 1.0)) * (1.0 / W)
    factors = jnp.concatenate([jnp.concatenate([factor, factor], 1)] * 2, 0)
    for j in range(MODES // 2):
        put(j, far[j] * factors)
    for j in range(MODES // 2):
        put(j, turn(three(mm, get(j), lefts)))
    grad_real, grad_imag = jnp.zeros((W, W), F32), jnp.zeros((W, W), F32)
    for j, pair in enumerate(pairs):
        back = three(mm, rights, get(j))
        grads = []
        for m, lanes in zip(pair, sides):
            b_real, b_imag = back[:W, lanes], back[W:, lanes]
            p_real, p_imag = probe[m, 0], probe[m, 1]
            grad_real = grad_real + (p_real * b_real + p_imag * b_imag)
            grad_imag = grad_imag + (p_real * b_imag - p_imag * b_real)
            grads.append((obj_real * b_real + obj_imag * b_imag, obj_real * b_imag - obj_imag * b_real))
        for part in range(2):
            at = slice((2 * j + part) * W, (2 * j + part + 1) * W)
            keep[at, :] = jnp.where(core == 0, grads[0][part], grads[1][part])
            send[at, :] = jnp.where(core == 0, grads[1][part], grads[0][part])
    patch = grad_imag * obj_real - grad_real * obj_imag
    shown = pltpu.roll(patch, W + row, 0)[:ROWS]
    pieces[...] = shown
    even, odd = pieces[pl.ds(0, 16, stride=2), :], pieces[pl.ds(1, 16, stride=2), :]
    keep[HALF : HALF + 16, :] = jnp.where(core == 0, even, odd)
    send[HALF : HALF + 16, :] = jnp.where(core == 0, odd, even)
    column = jnp.full((8, W), col, jnp.int32).astype(F32)
    keep[HALF + 16 :, :] = column
    send[HALF + 16 :, :] = column


def pack_kernel(sc, keep, other, out):
    lane = lax.broadcasted_iota(jnp.int32, (1, W), 1)
    first, second = keep[HALF + 16 : HALF + 17, :], other[HALF + 16 : HALF + 17, :]
    numbers = jnp.where(lane < 32, sc[0].astype(F32), jnp.where(lane < 64, first, second))
    for peer in range(16):
        rows = slice(CHUNK * peer, CHUNK * (peer + 1))
        at = MESSAGE * peer
        out[at : at + CHUNK, :] = keep[rows, :] + other[rows, :]
        rows = slice(HALF + 8 * (peer % 2), HALF + 8 * (peer % 2) + 8)
        out[at + CHUNK : at + CHUNK + 8, :] = keep[rows, :]
        out[at + CHUNK + 8 : at + CHUNK + 16, :] = other[rows, :]
        out[at + CHUNK + 16 : at + MESSAGE, :] = numbers


def relay_kernel(received, out, pieces, numbers):
    total = received[:CHUNK, :]
    for peer in range(1, 16):
        total = total + received[MESSAGE * peer : MESSAGE * peer + CHUNK, :]
    heads = jnp.concatenate([received[pl.ds(MESSAGE * p + MESSAGE - 1, 1), :] for p in range(16)], 0)
    rolls = [heads] + [pltpu.roll(heads, 32 * i, 1) for i in (1, 2, 3)]
    quarter = lax.broadcasted_iota(jnp.int32, (16, W), 1) // 32
    for i in range(3):
        value = rolls[0]
        for shift in (1, 2, 3):
            value = jnp.where(quarter == (i + shift) % 4, rolls[shift], value)
        numbers[i] = value
    windows = [(peer, side) for peer in range(16) for side in range(2)]
    rows = jnp.concatenate(
        [received[MESSAGE * p + CHUNK + 8 * i : MESSAGE * p + CHUNK + 8 * i + 8, :] for p, i in windows], 0
    )
    columns = jnp.concatenate(
        [jnp.broadcast_to(numbers[1 + i, p : p + 1, :], (8, W)) for p, i in windows], 0
    ).astype(jnp.int32)
    for bit in range(7):
        rows = jnp.where(columns & (1 << bit) != 0, pltpu.roll(rows, 1 << bit, 1), rows)
    lane = lax.broadcasted_iota(jnp.int32, rows.shape, 1)
    tiles = (columns >> 7) + jnp.where(lane < (columns & (W - 1)), 1, 0)
    for a in range(ANGLES):
        angle = jnp.max(numbers[0, 2 * a : 2 * a + 1, :]).astype(jnp.int32)
        slot = jnp.where(angle >= PAIRS, 2 * (ANGLES - 1 - angle) + 1, 2 * angle)
        at = pl.multiple_of(32 * slot, 32)
        for t in range(4):
            part = jnp.where(tiles[32 * a : 32 * a + 32] == t, rows[32 * a : 32 * a + 32], 0.0)
            pieces[pl.ds(at + 8 * t, 8), :] = jnp.sum(part.reshape(4, 8, W), axis=0)
    for z in range(8):
        out[z, :CHUNK, :] = total
        out[z, CHUNK:, :] = pieces[pl.ds(z, 32, stride=8), :]


def adjoint_kernel(received, dft_t, rows_tables, edges, middles, *refs):
    beams, (out, pieces, shifted, sheared) = refs[:PAIRS], refs[PAIRS:]
    block = 2 * lax.axis_index("y") + lax.axis_index("xh")
    total = received[0]
    for z in range(1, 8):
        total = total + received[z]
    chunk = total[:CHUNK] * (1.0 / 16.0)
    pieces[...] = total[CHUNK:]
    rows = jnp.concatenate([pieces[pl.ds(t, 8, stride=4), :] for t in range(4)], axis=1)
    spectrum = three(mm, split(rows), (dft_t[0], dft_t[1]))
    weight = jnp.where(lax.broadcasted_iota(jnp.int32, (8, N), 1) % H == 0, 0.5 / N, 1.0 / N)
    cbar = spectrum * weight
    c_mid, s_mid = middles[:ANGLES, :], middles[ANGLES:, :]
    c_reals = cbar[:, :H] * c_mid - cbar[:, H:] * s_mid
    c_imags = cbar[:, H:] * c_mid + cbar[:, :H] * s_mid
    at = pl.ds(pl.multiple_of(64 * block, 64), 64)
    rows_dft = dft_t[0, at, :].astype(F32) + dft_t[1, at, :].astype(F32)
    lane_zero = lax.broadcasted_iota(jnp.int32, (64, H), 1) == 0
    r_cos, r_sin = rows_dft[:, :H], rows_dft[:, H:]
    r_sin_real = jnp.where(lane_zero, 0.0, r_sin)
    r_cos_imag = jnp.where(lane_zero, r_sin, r_cos)
    mirror = jnp.where(lane_zero, 1.0, -1.0)
    nyquist = []
    for slot in range(ANGLES):
        c_real, c_imag = c_reals[slot : slot + 1, :], c_imags[slot : slot + 1, :]
        cosines = c_real * r_cos + c_imag * r_sin_real
        sines = c_imag * r_cos_imag - c_real * r_sin_real
        if slot % 2 == 0:
            sines = sines * mirror
        nyquist.append(sines[:, :1])
        at = slice(64 * slot, 64 * slot + 64)
        shifted[0, at, :H], shifted[1, at, :H] = split(cosines)
        shifted[0, at, H:], shifted[1, at, H:] = split(sines)
    for q in range(PAIRS):
        at = slice(2 * 64 * q, 2 * 64 * (q + 1))
        even = three(mm, (shifted[0, at, :H], shifted[1, at, :H]), (beams[q][0, :H, :], beams[q][1, :H, :]))
        odd = three(mm, (shifted[0, at, H:], shifted[1, at, H:]), (beams[q][0, H:, :], beams[q][1, H:, :]))
        even = even + jnp.concatenate(nyquist[2 * q : 2 * q + 2], 0) * edges[q, 0:1, :]
        sheared[0, at, :H], sheared[1, at, :H] = split(even)
        sheared[0, at, H:], sheared[1, at, H:] = split(odd)
    spectrum = jnp.concatenate(
        [
            three(
                mm, (sheared[0, :, part], sheared[1, :, part]), (dft_t[0, :H, part], dft_t[1, :H, part])
            )
            for part in (slice(0, H), slice(H, N))
        ],
        1,
    )
    lane_first = lax.broadcasted_iota(jnp.int32, (8, H), 1) == 0
    sums = [None] * 8
    for q in range(PAIRS):
        cb, sb = rows_tables[q, 0, 64:72, :], rows_tables[q, 1, 64:72, :]
        near = rows_tables[q, :, pl.ds(pl.multiple_of(8 * block, 8), 8), :]
        for u in range(8):
            ca, sa = near[0, u : u + 1, :], near[1, u : u + 1, :]
            c, s = ca * cb - sa * sb, sa * cb + ca * sb
            c_first, s_first = jnp.where(lane_first, 1.0, c), jnp.where(lane_first, 0.0, s)
            base = 2 * 64 * q + 8 * u
            one, two = spectrum[base : base + 8, :], spectrum[base + 64 : base + 72, :]
            both, apart = one + two, one - two
            unturned = jnp.concatenate(
                [both[:, :H] * c_first + apart[:, H:] * s_first, both[:, H:] * c - apart[:, :H] * s_first], 1
            )
            sums[u] = unturned if q == 0 else sums[u] + unturned
    weight = jnp.where(lax.broadcasted_iota(jnp.int32, (64, N), 1) % H == 0, 1.0 / 32.0, 1.0 / 16.0)
    whole = jnp.concatenate(sums, 0) * weight
    zeros = jnp.zeros((64, N), BF16)
    high, low = split(whole)
    result = None
    for side in range(2):
        dft_rows = [
            jnp.concatenate([dft_t[p, 64 * a + 32 * side : 64 * a + 32 * side + 32, :] for a in range(ANGLES)], 0)
            for p in range(2)
        ]
        order = (lambda v: [v, zeros]) if side == 0 else (lambda v: [zeros, v])
        columns = (jnp.concatenate(order(high), 0), jnp.concatenate(order(low), 0))
        part = three(mm_t, dft_rows, columns)
        result = part if result is None else result + part
    for peer in range(16):
        a = peer // 2
        out[peer, :CHUNK, :] = chunk
        out[peer, CHUNK:, :] = result[32 * a : 32 * a + 32, :]


def assemble_kernel(received, out, probe_out, sem):
    move = pltpu.make_async_copy(received.at[:, pl.ds(0, CHUNK), :], probe_out.at[lax.axis_index("core")], sem)
    move.start()
    xl = lax.axis_index("xl")
    lower = lax.broadcasted_iota(jnp.int32, (32, W), 1) < 64
    for b in range(4):
        even = received[4 * b + xl, CHUNK:, :]
        odd = received[4 * b + 2 + xl, CHUNK:, :]
        lanes = slice(b * W, (b + 1) * W)
        out[0, :32, lanes] = jnp.where(lower, even, pltpu.roll(odd, 64, 1))
        out[0, 32:, lanes] = jnp.where(lower, pltpu.roll(even, 64, 1), odd)
    move.wait()


def forward_call(*args):
    return pl.pallas_call(
        forward_kernel,
        in_specs=[pl.BlockSpec(memory_space=pltpu.SMEM)] + [pl.BlockSpec(memory_space=pl.ANY)] * 6,
        out_specs=pl.BlockSpec(memory_space=pltpu.VMEM),
        out_shape=jax.ShapeDtypeStruct((4 * ROWS, W), F32),
        scratch_shapes=[
            pltpu.VMEM((N, N), BF16),
            pltpu.VMEM((2, N, N), BF16),
            pltpu.VMEM((2, H, N), BF16),
            pltpu.VMEM((H // 4 + 24, N), F32),
            pltpu.VMEM((2, N, H), BF16),
            pltpu.VMEM((8, H), F32),
            pltpu.VMEM((N, N), F32),
            pltpu.VMEM((2, N, N), BF16),
            pltpu.VMEM((2, 2, N, H), BF16),
            pltpu.SemaphoreType.DMA((6,)),
        ],
        compiler_params=pltpu.CompilerParams(vmem_limit_bytes=60 * 1024 * 1024),
        cost_estimate=pl.CostEstimate(flops=4 * 10**9, bytes_accessed=4 * 10**6, transcendentals=0),
        name="forward",
    )(*args)


def vmem_call(kernel, outs, scratch, name, *args, far=0):
    result = pl.pallas_call(
        kernel,
        in_specs=[
            pl.BlockSpec(memory_space=pltpu.SMEM if a.shape == (1,) else pltpu.VMEM) for a in args
        ],
        out_specs=[pl.BlockSpec(memory_space=pltpu.VMEM)] * (len(outs) - far)
        + [pl.BlockSpec(memory_space=pl.ANY)] * far,
        out_shape=[jax.ShapeDtypeStruct(o, F32) for o in outs],
        scratch_shapes=scratch,
        compiler_params=pltpu.CompilerParams(vmem_limit_bytes=32 * 1024 * 1024),
        cost_estimate=pl.CostEstimate(flops=3 * 10**9, bytes_accessed=4 * 10**6, transcendentals=0),
        name=name,
    )(*args)
    return result if len(outs) > 1 else result[0]


GZ = ("xl", "z", "core")
PLANE = ("y", "xh", "xl")


def exchange(blocks, axes):
    return lax.all_to_all(blocks, axes, split_axis=0, concat_axis=0, tiled=True)


def swap(rows):
    return lax.ppermute(rows, "core", [(0, 1), (1, 0)])


def local(volume, probe, measured, angle_index, row_offset, col_offset):
    dft, dft_t = (jnp.asarray(t) for t in dft_tables())
    dfts = jnp.asarray(window_tables())
    factors, rows_tables, all_beams, edges, middles = (jnp.asarray(t) for t in phase_tables())
    beams = [jnp.asarray(b) for b in phase_tables()[2]]
    row = forward_call(angle_index, volume, dft, dft_t, factors, all_beams, edges)
    whole = exchange(row.reshape(ROWS, 4, W), GZ).reshape(4 * ROWS, W)
    keep, send = vmem_call(
        window_kernel,
        [(HALF + 24, W)] * 2,
        [
            pltpu.VMEM((2, MODES // 2, 2 * W, 2 * W), BF16),
            pltpu.VMEM((MODES // 2, 2 * W, 2 * W), F32),
            pltpu.VMEM((ROWS, W), F32),
        ],
        "window",
        row_offset,
        col_offset,
        whole,
        probe,
        measured,
        dfts,
    )
    packed = vmem_call(pack_kernel, [(16 * MESSAGE, W)], [], "pack", angle_index, keep, swap(send))
    shared = exchange(packed.reshape(16, MESSAGE, 1, W), PLANE).reshape(16 * MESSAGE, W)
    relay = vmem_call(relay_kernel, [(8, CHUNK + 32, W)], [pltpu.VMEM((256, W), F32), pltpu.VMEM((3, 16, W), F32)], "relay", shared)
    rows = exchange(relay, "z")
    blocks = vmem_call(
        adjoint_kernel,
        [(16, CHUNK + 32, W)],
        [pltpu.VMEM((32, W), F32), pltpu.VMEM((2, N, N), BF16), pltpu.VMEM((2, N, N), BF16)],
        "adjoint",
        rows,
        dft_t,
        rows_tables,
        edges,
        middles,
        *beams,
    )
    final = exchange(blocks, PLANE)
    other = swap(final[:, :CHUNK, :])
    volume_update, half = vmem_call(
        assemble_kernel,
        [(1, 64, N), (2, 16, CHUNK, W)],
        [pltpu.SemaphoreType.DMA],
        "assemble",
        final,
        far=1,
    )
    core = lax.axis_index("core")
    probe_update = lax.dynamic_update_slice(half, other[None], (1 - core, 0, 0, 0))
    return volume_update, probe_update.reshape(MODES, 2, W, W)


def solution(mesh):
    split_mesh = Mesh(mesh.devices.reshape(4, 2, 2, 8, 2), ("y", "xh", "xl", "z", "core"))
    angle, gz = ("y", "xh"), GZ
    return jax.shard_map(
        local,
        mesh=split_mesh,
        in_specs=(
            P(gz, None, None),
            P(),
            P(angle, gz, None, None),
            P(angle),
            P(angle, gz),
            P(angle, gz),
        ),
        out_specs=(P(gz, angle, None), P()),
        check_vma=False,
    )
```

```python
import math

import jax
import jax.numpy as jnp
import numpy as np
from jax import lax
from jax.experimental import pallas as pl
from jax.experimental.pallas import tpu as pltpu
from jax.sharding import Mesh, PartitionSpec as P

N = 512
H = N // 2
W = 128
MODES = 8
ANGLES = 8
PAIRS = ANGLES // 2
ROWS = 32
HALF = MODES * 2 * W // 2
CHUNK = HALF // 16
MESSAGE = CHUNK + 17
F32 = jnp.float32
BF16 = jnp.bfloat16


def split_const(table):
    high = table.astype(BF16)
    low = (table - high.astype(np.float64)).astype(BF16)
    return np.stack([high, low])


def dft_tables():
    k, n = np.arange(H)[:, None], np.arange(N)[None, :]
    turns = np.pi / N * (k * (2 * n + 1) % (2 * N))
    table = np.concatenate([np.cos(turns), -np.sin(turns)], 0)
    table[H] = 2.0 * (np.arange(N) % 2) - 1.0
    return split_const(table), split_const(np.ascontiguousarray(table.T))


def window_tables():
    j = np.arange(W)
    turns = 2.0 * np.pi / W * (j[:, None] * j[None, :] % W)
    c, s = np.cos(turns), np.sin(turns)
    return np.stack([split_const(np.block([[c, s], [-s, c]])), split_const(np.block([[c, -s], [s, c]]))])


def shears():
    theta = np.pi * (np.arange(ANGLES) + 0.5) / ANGLES - np.pi / 2
    return -np.tan(theta / 2), np.sin(theta)


def cos_sin(phase):
    return np.stack([np.cos(phase), np.sin(phase)], 1)


def phase_tables():
    shear_x, shear_y = shears()
    cells = np.arange(N) - N / 2
    unit_one = -2.0 * np.pi / N * shear_x
    unit_two = -2.0 * np.pi / N * shear_y[:PAIRS]
    by_y = unit_one[:, None, None] * np.concatenate([cells[:H], cells[:H - 1:-1]])[None, None, :]
    nyquist = np.ones((ANGLES, 8, N))
    nyquist[:, 0] = 0.5 * np.cos(by_y[:, 0] * H)
    factors = np.concatenate(
        [
            cos_sin(by_y * (8 * np.arange(H // 8))[None, :, None]).reshape(ANGLES, H // 4, N),
            cos_sin(by_y * np.arange(8)[None, :, None]).reshape(ANGLES, 16, N),
            nyquist,
        ],
        1,
    )
    freq = np.arange(H, dtype=np.float64)
    freq[0] = H
    by_k = unit_one[:PAIRS, None, None] * freq[None, None, :]
    rows_coarse = cos_sin(by_k * cells[::8][None, :, None])
    rows_fine = cos_sin(by_k * np.arange(8)[None, :, None])
    rows_tables = np.concatenate([rows_coarse, rows_fine], 2)
    frequencies = np.arange(H, dtype=np.float64)
    turns = unit_two[:, None, None] * frequencies[None, :, None] * (H - 0.5 - np.arange(H))[None, None, :]
    low = np.cos(unit_two[:, None] * H * cells[None, :H])
    high = np.cos(unit_two[:, None] * H * cells[None, :H - 1:-1])
    table = np.concatenate([np.cos(turns), np.sin(turns)], 1)
    table[:, H] = 0.5 * (low - high)
    beams = np.ascontiguousarray(np.moveaxis(split_const(table), 0, 1))
    edges = np.zeros((PAIRS, 8, H))
    edges[:, 0] = 0.5 * (low + high)
    middle = 0.5 * unit_two[:, None] * frequencies[None, :]
    ordered = np.stack([middle, -middle], 1).reshape(ANGLES, H)
    middles = np.concatenate([np.cos(ordered), np.sin(ordered)], 0)
    return [t if t.dtype == BF16 else t.astype(np.float32) for t in (factors, rows_tables, beams, edges, middles)]


def mm(a, b):
    return lax.dot_general(a, b, (((1,), (0,)), ((), ())), preferred_element_type=F32)


def mm_t(a, b):
    return lax.dot_general(a, b, (((1,), (1,)), ((), ())), preferred_element_type=F32)


def split(value):
    high = value.astype(BF16)
    return high, (value - high.astype(F32)).astype(BF16)


def three(dot, a, b):
    rows = a[0].shape[0]
    both = dot(jnp.concatenate([a[0], a[1]], 0), b[0])
    return both[:rows] + (both[rows:] + dot(a[0], b[1]))


def forward_kernel(
    sc, volume, dft_hbm, dft_t_hbm, factors_hbm, beams_hbm, edges_hbm, out,
    slab, dft, dft_t, factors, beams, edges, spec, turned, field, sems,
):
    number = sc[0]
    mirrored = number >= PAIRS
    sign = jnp.where(mirrored, -1.0, 1.0)
    folded = jnp.where(mirrored, ANGLES - 1 - number, number)
    copies = [
        (volume.at[0], slab),
        (dft_hbm, dft),
        (factors_hbm.at[number], factors),
        (dft_t_hbm.at[:, pl.ds(0, H), :], dft_t),
        (beams_hbm.at[folded], beams),
        (edges_hbm.at[folded], edges),
    ]
    moves = [pltpu.make_async_copy(source, target, sems.at[i]) for i, (source, target) in enumerate(copies)]
    for move in moves:
        move.start()
    halves = (slice(0, H), slice(H, N))
    rows, lanes = (lax.broadcasted_iota(jnp.int32, (H, H), axis) for axis in (0, 1))
    reverse = jnp.where(rows + lanes == H - 1, 1.0, 0.0).astype(BF16)
    moves[0].wait()
    backward = mm(slab[:, H:], reverse).astype(BF16)
    moves[1].wait()
    moves[2].wait()
    for lanes, columns in zip(halves, (slab[:, :H], backward)):
        spec[:, lanes] = mm(dft[0], columns) + mm(dft[1], columns)
    half_row = jnp.where(lax.broadcasted_iota(jnp.int32, (8, H), 0) == 0, 0.5, 1.0)
    for lanes in halves:
        cb, sb = factors[64:72, lanes], factors[72:80, lanes]
        for pair in range(H // 16):
            reals, imags = [], []
            for u in (2 * pair, 2 * pair + 1):
                ca, sa = factors[u : u + 1, lanes], factors[32 + u : 33 + u, lanes]
                c, s = ca * cb - sa * sb, sa * cb + ca * sb
                a, b = spec[8 * u : 8 * u + 8, lanes], spec[H + 8 * u : H + 8 * u + 8, lanes]
                real, imag = a * c - b * s, a * s + b * c
                if u == 0:
                    real, imag = real * half_row, imag * factors[80:88, lanes]
                reals.append(real)
                imags.append(imag)
            for base, parts in ((16 * pair, reals), (H + 16 * pair, imags)):
                at = slice(base, base + 16)
                turned[0, at, lanes], turned[1, at, lanes] = split(jnp.concatenate(parts, 0))
    moves[3].wait()
    for part, comps in enumerate(halves):
        both = three(mm, (dft_t[0, :, comps], dft_t[1, :, comps]), (turned[0, comps, :], turned[1, comps, :]))
        field[0, 0, comps, :], field[0, 1, comps, :] = split(both[:, :H] + both[:, H:])
        field[1, 0, comps, :], field[1, 1, comps, :] = split(both[:, :H] - both[:, H:])
    for part, comps in enumerate(halves):
        spec[comps, :] = three(mm_t, (dft[0, comps, :H], dft[1, comps, :H]), (field[part, 0], field[part, 1]))
    moves[4].wait()
    moves[5].wait()
    total = jnp.zeros((8, N), F32)
    for r in range(0, H, 32):
        real_even, real_odd = spec[r : r + 32, :H], spec[r : r + 32, H:]
        imag_even, imag_odd = spec[H + r : H + r + 32, :H], spec[H + r : H + r + 32, H:]
        c = beams[0, r : r + 32, :].astype(F32) + beams[1, r : r + 32, :].astype(F32)
        s = beams[0, H + r : H + r + 32, :].astype(F32) + beams[1, H + r : H + r + 32, :].astype(F32)
        c_imag, s_imag, extra = c, s * sign, None
        if r == 0:
            top = lax.broadcasted_iota(jnp.int32, (32, H), 0) == 0
            extra = jnp.where(top, imag_odd * s, 0.0)
            c_imag = jnp.where(top, edges[0:1, :], c)
            s_imag = jnp.where(top, 0.0, s_imag)
        real_terms = real_even * c + imag_odd * s_imag
        imag_terms = imag_even * c_imag - real_odd * s_imag
        if extra is not None:
            imag_terms = imag_terms + extra
        real = jnp.sum(real_terms, axis=1, keepdims=True)
        imag = jnp.sum(imag_terms, axis=1, keepdims=True)
        if r == 0:
            weight = jnp.where(lax.broadcasted_iota(jnp.int32, (32, 1), 0) == 0, 0.5, 1.0)
            real, imag = real * weight, imag * weight
        c_mid, s_mid = c[:, H - 1 :], s_imag[:, H - 1 :]
        real, imag = real * c_mid + imag * s_mid, imag * c_mid - real * s_mid
        f_real = dft[0, r : r + 32, :].astype(F32) + dft[1, r : r + 32, :].astype(F32)
        f_imag = dft[0, H + r : H + r + 32, :].astype(F32) + dft[1, H + r : H + r + 32, :].astype(F32)
        terms = real * f_real + imag * f_imag
        total = total + jnp.sum(terms.reshape(4, 8, N), axis=0)
    row = jnp.sum(total, axis=0, keepdims=True) * (8.0 / (N * N))
    for t in range(4):
        out[pl.ds(t, ROWS, stride=4), :] = jnp.broadcast_to(row[:, t * W : (t + 1) * W], (ROWS, W))


def turn(block):
    return jnp.concatenate(
        [
            jnp.concatenate([block[:W, :W], block[W:, :W]], 1),
            jnp.concatenate([block[:W, W:], block[W:, W:]], 1),
        ],
        0,
    )


def pairs_of_modes():
    return [(j, j + MODES // 2) for j in range(MODES // 2)]


def prepare_kernel(row_ref, probe, dfts, waves, band_dft, band_probe, stage):
    start = -row_ref[0, 0]
    lefts, rights = (dfts[0, 0], dfts[0, 1]), (dfts[1, 0], dfts[1, 1])
    for j, pair in enumerate(pairs_of_modes()):
        reals = jnp.concatenate([probe[m, 0] for m in pair], 1)
        imags = jnp.concatenate([probe[m, 1] for m in pair], 1)
        stage[0, j], stage[1, j] = split(jnp.concatenate([reals, imags], 0))
    for j in range(MODES // 2):
        stage[0, j], stage[1, j] = split(turn(three(mm, lefts, (stage[0, j], stage[1, j]))))
    for j in range(MODES // 2):
        waves[j] = three(mm, (stage[0, j], stage[1, j]), rights)
    source = lax.broadcasted_iota(jnp.int32, (2 * W, 2 * W), 0)
    target = lax.broadcasted_iota(jnp.int32, (2 * W, 2 * W), 1)
    wanted = start + (target & (ROWS - 1)) + jnp.where(target & ROWS != 0, W, 0)
    chosen = jnp.where(source == wanted, 1.0, 0.0)
    first = jnp.where(target < 4 * ROWS, chosen, 0.0).astype(BF16)
    second = jnp.where((target >= 4 * ROWS) & (target < 6 * ROWS), chosen, 0.0).astype(BF16)
    band_dft[...] = (mm(lefts[0], first) + mm(lefts[1], second)).astype(BF16)
    for m in range(MODES):
        for part in range(2):
            band_probe[m, part] = probe[m, part, pl.ds(start, ROWS), :]


def window_kernel(
    row_ref, col_ref, whole, probe, measured, dfts, waves, band_dft, band_probe, keep, send, stage, far, pieces
):
    row, col, core = row_ref[0, 0], col_ref[0, 0], lax.axis_index("core")
    rows = jnp.concatenate([whole[pl.ds(t, ROWS, stride=4), :] for t in range(4)], axis=1)
    band = pltpu.roll(rows, lax.rem(N - col, N), 1)[:, :W]
    band_real, band_imag = jnp.cos(band) - 1.0, jnp.sin(band)
    lefts, rights = (dfts[0, 0], dfts[0, 1]), (dfts[1, 0], dfts[1, 1])
    pairs = pairs_of_modes()
    sides = (slice(0, W), slice(W, 2 * W))

    def put(j, value):
        stage[0, j], stage[1, j] = split(value)

    def get(j):
        return stage[0, j], stage[1, j]

    lines = []
    for m in [m for pair in pairs for m in pair]:
        p_real, p_imag = band_probe[m, 0], band_probe[m, 1]
        lines.append(
            jnp.concatenate(
                [p_real * band_real - p_imag * band_imag, p_real * band_imag + p_imag * band_real], 1
            )
        )
    lines = three(mm, split(jnp.concatenate(lines, 0)), rights)
    intensity = jnp.zeros((W, W), F32)
    for j in range(MODES // 2):
        one, two = (lines[2 * ROWS * j + ROWS * i : 2 * ROWS * j + ROWS * (i + 1)] for i in range(2))
        both = jnp.concatenate(
            [jnp.concatenate([one[:, :W], two[:, :W]], 1), jnp.concatenate([one[:, W:], two[:, W:]], 1)], 0
        )
        high, low = split(both)
        blank = jnp.zeros((2 * ROWS, 2 * W), BF16)
        total = waves[j] + turn(mm(band_dft[...], jnp.concatenate([high, low, high, blank], 0)))
        far[j] = total
        power = total * total
        power = power[:W] + power[W:]
        intensity = intensity + (power[:, :W] + power[:, W:])
    pad = jnp.zeros((W - ROWS, W), F32)
    obj_real = pltpu.roll(jnp.concatenate([band_real, pad], 0), -row, 0) + 1.0
    obj_imag = pltpu.roll(jnp.concatenate([band_imag, pad], 0), -row, 0)
    factor = (1.0 - jnp.sqrt(measured[0, 0] + 1.0) / jnp.sqrt(intensity + 1.0)) * (1.0 / W)
    factors = jnp.concatenate([jnp.concatenate([factor, factor], 1)] * 2, 0)
    for j in range(MODES // 2):
        put(j, far[j] * factors)
    for j in range(MODES // 2):
        put(j, turn(three(mm, get(j), lefts)))
    grad_real, grad_imag = jnp.zeros((W, W), F32), jnp.zeros((W, W), F32)
    for j, pair in enumerate(pairs):
        back = three(mm, rights, get(j))
        grads = []
        for m, lanes in zip(pair, sides):
            b_real, b_imag = back[:W, lanes], back[W:, lanes]
            p_real, p_imag = probe[m, 0], probe[m, 1]
            grad_real = grad_real + (p_real * b_real + p_imag * b_imag)
            grad_imag = grad_imag + (p_real * b_imag - p_imag * b_real)
            grads.append((obj_real * b_real + obj_imag * b_imag, obj_real * b_imag - obj_imag * b_real))
        for part in range(2):
            at = slice((2 * j + part) * W, (2 * j + part + 1) * W)
            keep[at, :] = jnp.where(core == 0, grads[0][part], grads[1][part])
            send[at, :] = jnp.where(core == 0, grads[1][part], grads[0][part])
    patch = grad_imag * obj_real - grad_real * obj_imag
    shown = pltpu.roll(patch, W + row, 0)[:ROWS]
    pieces[...] = shown
    even, odd = pieces[pl.ds(0, 16, stride=2), :], pieces[pl.ds(1, 16, stride=2), :]
    keep[HALF : HALF + 16, :] = jnp.where(core == 0, even, odd)
    send[HALF : HALF + 16, :] = jnp.where(core == 0, odd, even)
    column = jnp.full((8, W), col, jnp.int32).astype(F32)
    keep[HALF + 16 :, :] = column
    send[HALF + 16 :, :] = column


def pack_kernel(sc, keep, other, out):
    lane = lax.broadcasted_iota(jnp.int32, (1, W), 1)
    first, second = keep[HALF + 16 : HALF + 17, :], other[HALF + 16 : HALF + 17, :]
    numbers = jnp.where(lane < 32, sc[0].astype(F32), jnp.where(lane < 64, first, second))
    for peer in range(16):
        rows = slice(CHUNK * peer, CHUNK * (peer + 1))
        at = MESSAGE * peer
        out[at : at + CHUNK, :] = keep[rows, :] + other[rows, :]
        rows = slice(HALF + 8 * (peer % 2), HALF + 8 * (peer % 2) + 8)
        out[at + CHUNK : at + CHUNK + 8, :] = keep[rows, :]
        out[at + CHUNK + 8 : at + CHUNK + 16, :] = other[rows, :]
        out[at + CHUNK + 16 : at + MESSAGE, :] = numbers


def relay_kernel(received, out, pieces, numbers):
    total = received[:CHUNK, :]
    for peer in range(1, 16):
        total = total + received[MESSAGE * peer : MESSAGE * peer + CHUNK, :]
    heads = jnp.concatenate([received[pl.ds(MESSAGE * p + MESSAGE - 1, 1), :] for p in range(16)], 0)
    rolls = [heads] + [pltpu.roll(heads, 32 * i, 1) for i in (1, 2, 3)]
    quarter = lax.broadcasted_iota(jnp.int32, (16, W), 1) // 32
    for i in range(3):
        value = rolls[0]
        for shift in (1, 2, 3):
            value = jnp.where(quarter == (i + shift) % 4, rolls[shift], value)
        numbers[i] = value
    windows = [(peer, side) for peer in range(16) for side in range(2)]
    rows = jnp.concatenate(
        [received[MESSAGE * p + CHUNK + 8 * i : MESSAGE * p + CHUNK + 8 * i + 8, :] for p, i in windows], 0
    )
    columns = jnp.concatenate(
        [jnp.broadcast_to(numbers[1 + i, p : p + 1, :], (8, W)) for p, i in windows], 0
    ).astype(jnp.int32)
    for bit in range(7):
        rows = jnp.where(columns & (1 << bit) != 0, pltpu.roll(rows, 1 << bit, 1), rows)
    lane = lax.broadcasted_iota(jnp.int32, rows.shape, 1)
    tiles = (columns >> 7) + jnp.where(lane < (columns & (W - 1)), 1, 0)
    for a in range(ANGLES):
        angle = jnp.max(numbers[0, 2 * a : 2 * a + 1, :]).astype(jnp.int32)
        slot = jnp.where(angle >= PAIRS, 2 * (ANGLES - 1 - angle) + 1, 2 * angle)
        at = pl.multiple_of(32 * slot, 32)
        for t in range(4):
            part = jnp.where(tiles[32 * a : 32 * a + 32] == t, rows[32 * a : 32 * a + 32], 0.0)
            pieces[pl.ds(at + 8 * t, 8), :] = jnp.sum(part.reshape(4, 8, W), axis=0)
    for z in range(8):
        out[z, :CHUNK, :] = total
        out[z, CHUNK:, :] = pieces[pl.ds(z, 32, stride=8), :]


def adjoint_kernel(received, dft_t, rows_tables, edges, middles, *refs):
    beams, (out, pieces, shifted, sheared) = refs[:PAIRS], refs[PAIRS:]
    block = 2 * lax.axis_index("y") + lax.axis_index("xh")
    total = received[0]
    for z in range(1, 8):
        total = total + received[z]
    chunk = total[:CHUNK] * (1.0 / 16.0)
    pieces[...] = total[CHUNK:]
    rows = jnp.concatenate([pieces[pl.ds(t, 8, stride=4), :] for t in range(4)], axis=1)
    spectrum = three(mm, split(rows), (dft_t[0], dft_t[1]))
    weight = jnp.where(lax.broadcasted_iota(jnp.int32, (8, N), 1) % H == 0, 0.5 / N, 1.0 / N)
    cbar = spectrum * weight
    c_mid, s_mid = middles[:ANGLES, :], middles[ANGLES:, :]
    c_reals = cbar[:, :H] * c_mid - cbar[:, H:] * s_mid
    c_imags = cbar[:, H:] * c_mid + cbar[:, :H] * s_mid
    at = pl.ds(pl.multiple_of(64 * block, 64), 64)
    rows_dft = dft_t[0, at, :].astype(F32) + dft_t[1, at, :].astype(F32)
    lane_zero = lax.broadcasted_iota(jnp.int32, (64, H), 1) == 0
    r_cos, r_sin = rows_dft[:, :H], rows_dft[:, H:]
    r_sin_real = jnp.where(lane_zero, 0.0, r_sin)
    r_cos_imag = jnp.where(lane_zero, r_sin, r_cos)
    mirror = jnp.where(lane_zero, 1.0, -1.0)
    nyquist = []
    for slot in range(ANGLES):
        c_real, c_imag = c_reals[slot : slot + 1, :], c_imags[slot : slot + 1, :]
        cosines = c_real * r_cos + c_imag * r_sin_real
        sines = c_imag * r_cos_imag - c_real * r_sin_real
        if slot % 2 == 0:
            sines = sines * mirror
        nyquist.append(sines[:, :1])
        at = slice(64 * slot, 64 * slot + 64)
        shifted[0, at, :H], shifted[1, at, :H] = split(cosines)
        shifted[0, at, H:], shifted[1, at, H:] = split(sines)
    for q in range(PAIRS):
        at = slice(2 * 64 * q, 2 * 64 * (q + 1))
        even = three(mm, (shifted[0, at, :H], shifted[1, at, :H]), (beams[q][0, :H, :], beams[q][1, :H, :]))
        odd = three(mm, (shifted[0, at, H:], shifted[1, at, H:]), (beams[q][0, H:, :], beams[q][1, H:, :]))
        even = even + jnp.concatenate(nyquist[2 * q : 2 * q + 2], 0) * edges[q, 0:1, :]
        sheared[0, at, :H], sheared[1, at, :H] = split(even)
        sheared[0, at, H:], sheared[1, at, H:] = split(odd)
    spectrum = jnp.concatenate(
        [
            three(
                mm, (sheared[0, :, part], sheared[1, :, part]), (dft_t[0, :H, part], dft_t[1, :H, part])
            )
            for part in (slice(0, H), slice(H, N))
        ],
        1,
    )
    lane_first = lax.broadcasted_iota(jnp.int32, (8, H), 1) == 0
    sums = [None] * 8
    for q in range(PAIRS):
        cb, sb = rows_tables[q, 0, 64:72, :], rows_tables[q, 1, 64:72, :]
        near = rows_tables[q, :, pl.ds(pl.multiple_of(8 * block, 8), 8), :]
        for u in range(8):
            ca, sa = near[0, u : u + 1, :], near[1, u : u + 1, :]
            c, s = ca * cb - sa * sb, sa * cb + ca * sb
            c_first, s_first = jnp.where(lane_first, 1.0, c), jnp.where(lane_first, 0.0, s)
            base = 2 * 64 * q + 8 * u
            one, two = spectrum[base : base + 8, :], spectrum[base + 64 : base + 72, :]
            both, apart = one + two, one - two
            unturned = jnp.concatenate(
                [both[:, :H] * c_first + apart[:, H:] * s_first, both[:, H:] * c - apart[:, :H] * s_first], 1
            )
            sums[u] = unturned if q == 0 else sums[u] + unturned
    weight = jnp.where(lax.broadcasted_iota(jnp.int32, (64, N), 1) % H == 0, 1.0 / 32.0, 1.0 / 16.0)
    whole = jnp.concatenate(sums, 0) * weight
    zeros = jnp.zeros((64, N), BF16)
    high, low = split(whole)
    result = None
    for side in range(2):
        dft_rows = [
            jnp.concatenate([dft_t[p, 64 * a + 32 * side : 64 * a + 32 * side + 32, :] for a in range(ANGLES)], 0)
            for p in range(2)
        ]
        order = (lambda v: [v, zeros]) if side == 0 else (lambda v: [zeros, v])
        columns = (jnp.concatenate(order(high), 0), jnp.concatenate(order(low), 0))
        part = three(mm_t, dft_rows, columns)
        result = part if result is None else result + part
    for peer in range(16):
        a = peer // 2
        out[peer, :CHUNK, :] = chunk
        out[peer, CHUNK:, :] = result[32 * a : 32 * a + 32, :]


def assemble_kernel(received, out, probe_out, sem):
    move = pltpu.make_async_copy(received.at[:, pl.ds(0, CHUNK), :], probe_out.at[lax.axis_index("core")], sem)
    move.start()
    xl = lax.axis_index("xl")
    lower = lax.broadcasted_iota(jnp.int32, (32, W), 1) < 64
    for b in range(4):
        even = received[4 * b + xl, CHUNK:, :]
        odd = received[4 * b + 2 + xl, CHUNK:, :]
        lanes = slice(b * W, (b + 1) * W)
        out[0, :32, lanes] = jnp.where(lower, even, pltpu.roll(odd, 64, 1))
        out[0, 32:, lanes] = jnp.where(lower, pltpu.roll(even, 64, 1), odd)
    move.wait()


def forward_call(*args):
    return pl.pallas_call(
        forward_kernel,
        in_specs=[pl.BlockSpec(memory_space=pltpu.SMEM)] + [pl.BlockSpec(memory_space=pl.ANY)] * 6,
        out_specs=pl.BlockSpec(memory_space=pltpu.VMEM),
        out_shape=jax.ShapeDtypeStruct((4 * ROWS, W), F32),
        scratch_shapes=[
            pltpu.VMEM((N, N), BF16),
            pltpu.VMEM((2, N, N), BF16),
            pltpu.VMEM((2, H, N), BF16),
            pltpu.VMEM((H // 4 + 24, N), F32),
            pltpu.VMEM((2, N, H), BF16),
            pltpu.VMEM((8, H), F32),
            pltpu.VMEM((N, N), F32),
            pltpu.VMEM((2, N, N), BF16),
            pltpu.VMEM((2, 2, N, H), BF16),
            pltpu.SemaphoreType.DMA((6,)),
        ],
        compiler_params=pltpu.CompilerParams(vmem_limit_bytes=60 * 1024 * 1024),
        cost_estimate=pl.CostEstimate(flops=4 * 10**9, bytes_accessed=4 * 10**6, transcendentals=0),
        name="forward",
    )(*args)


def vmem_call(kernel, outs, scratch, name, *args, far=0):
    result = pl.pallas_call(
        kernel,
        in_specs=[
            pl.BlockSpec(memory_space=pltpu.SMEM if a.dtype == jnp.int32 else pltpu.VMEM) for a in args
        ],
        out_specs=[pl.BlockSpec(memory_space=pltpu.VMEM)] * (len(outs) - far)
        + [pl.BlockSpec(memory_space=pl.ANY)] * far,
        out_shape=[jax.ShapeDtypeStruct(*o) if o[-1] == BF16 else jax.ShapeDtypeStruct(o, F32) for o in outs],
        scratch_shapes=scratch,
        compiler_params=pltpu.CompilerParams(vmem_limit_bytes=32 * 1024 * 1024),
        cost_estimate=pl.CostEstimate(flops=3 * 10**9, bytes_accessed=4 * 10**6, transcendentals=0),
        name=name,
    )(*args)
    return result if len(outs) > 1 else result[0]


GZ = ("xl", "z", "core")
PLANE = ("y", "xh", "xl")


def exchange(blocks, axes):
    return lax.all_to_all(blocks, axes, split_axis=0, concat_axis=0, tiled=True)


def swap(rows):
    return lax.ppermute(rows, "core", [(0, 1), (1, 0)])


def local(volume, probe, measured, angle_index, row_offset, col_offset):
    dft, dft_t = (jnp.asarray(t) for t in dft_tables())
    dfts = jnp.asarray(window_tables())
    factors, rows_tables, all_beams, edges, middles = (jnp.asarray(t) for t in phase_tables())
    beams = [jnp.asarray(b) for b in phase_tables()[2]]
    row = forward_call(angle_index, volume, dft, dft_t, factors, all_beams, edges)
    whole = exchange(row.reshape(ROWS, 4, W), GZ).reshape(4 * ROWS, W)
    split_modes = pltpu.VMEM((2, MODES // 2, 2 * W, 2 * W), BF16)
    waves, band_dft, band_probe = vmem_call(
        prepare_kernel,
        [(MODES // 2, 2 * W, 2 * W), ((2 * W, 2 * W), BF16), (MODES, 2, ROWS, W)],
        [split_modes],
        "prepare",
        row_offset,
        probe,
        dfts,
    )
    keep, send = vmem_call(
        window_kernel,
        [(HALF + 24, W)] * 2,
        [split_modes, pltpu.VMEM((MODES // 2, 2 * W, 2 * W), F32), pltpu.VMEM((ROWS, W), F32)],
        "window",
        row_offset,
        col_offset,
        whole,
        probe,
        measured,
        dfts,
        waves,
        band_dft,
        band_probe,
    )
    packed = vmem_call(pack_kernel, [(16 * MESSAGE, W)], [], "pack", angle_index, keep, swap(send))
    shared = exchange(packed.reshape(16, MESSAGE, 1, W), PLANE).reshape(16 * MESSAGE, W)
    relay = vmem_call(relay_kernel, [(8, CHUNK + 32, W)], [pltpu.VMEM((256, W), F32), pltpu.VMEM((3, 16, W), F32)], "relay", shared)
    rows = exchange(relay, "z")
    blocks = vmem_call(
        adjoint_kernel,
        [(16, CHUNK + 32, W)],
        [pltpu.VMEM((32, W), F32), pltpu.VMEM((2, N, N), BF16), pltpu.VMEM((2, N, N), BF16)],
        "adjoint",
        rows,
        dft_t,
        rows_tables,
        edges,
        middles,
        *beams,
    )
    final = exchange(blocks, PLANE)
    other = swap(final[:, :CHUNK, :])
    volume_update, half = vmem_call(
        assemble_kernel,
        [(1, 64, N), (2, 16, CHUNK, W)],
        [pltpu.SemaphoreType.DMA],
        "assemble",
        final,
        far=1,
    )
    core = lax.axis_index("core")
    probe_update = lax.dynamic_update_slice(half, other[None], (1 - core, 0, 0, 0))
    return volume_update, probe_update.reshape(MODES, 2, W, W)


def solution(mesh):
    split_mesh = Mesh(mesh.devices.reshape(4, 2, 2, 8, 2), ("y", "xh", "xl", "z", "core"))
    angle, gz = ("y", "xh"), GZ
    return jax.shard_map(
        local,
        mesh=split_mesh,
        in_specs=(
            P(gz, None, None),
            P(),
            P(angle, gz, None, None),
            P(angle),
            P(angle, gz),
            P(angle, gz),
        ),
        out_specs=(P(gz, angle, None), P()),
        check_vma=False,
    )
```

```python
import math

import jax
import jax.numpy as jnp
import numpy as np
from jax import lax
from jax.experimental import pallas as pl
from jax.experimental.pallas import tpu as pltpu
from jax.sharding import Mesh, PartitionSpec as P

N = 512
H = N // 2
W = 128
MODES = 8
ANGLES = 8
PAIRS = ANGLES // 2
ROWS = 32
HALF = MODES * 2 * W // 2
CHUNK = HALF // 16
MESSAGE = CHUNK + 17
F32 = jnp.float32
BF16 = jnp.bfloat16


def split_const(table):
    high = table.astype(BF16)
    low = (table - high.astype(np.float64)).astype(BF16)
    return np.stack([high, low])


def dft_tables():
    k, n = np.arange(H)[:, None], np.arange(N)[None, :]
    turns = np.pi / N * (k * (2 * n + 1) % (2 * N))
    table = np.concatenate([np.cos(turns), -np.sin(turns)], 0)
    table[H] = 2.0 * (np.arange(N) % 2) - 1.0
    order = np.arange(N).reshape(2, 4, 2, 32).transpose(0, 2, 1, 3).reshape(N)
    return [split_const(np.ascontiguousarray(t)) for t in (table, table.T, table[:, order])]


def window_tables():
    j = np.arange(W)
    turns = 2.0 * np.pi / W * (j[:, None] * j[None, :] % W)
    c, s = np.cos(turns), np.sin(turns)
    return np.stack([split_const(np.block([[c, s], [-s, c]])), split_const(np.block([[c, -s], [s, c]]))])


def shears():
    theta = np.pi * (np.arange(ANGLES) + 0.5) / ANGLES - np.pi / 2
    return -np.tan(theta / 2), np.sin(theta)


def cos_sin(phase):
    return np.stack([np.cos(phase), np.sin(phase)], 1)


def phase_tables():
    shear_x, shear_y = shears()
    cells = np.arange(N) - N / 2
    unit_one = -2.0 * np.pi / N * shear_x
    unit_two = -2.0 * np.pi / N * shear_y[:PAIRS]
    by_y = unit_one[:, None, None] * np.concatenate([cells[:H], cells[:H - 1:-1]])[None, None, :]
    nyquist = np.ones((ANGLES, 8, N))
    nyquist[:, 0] = 0.5 * np.cos(by_y[:, 0] * H)
    factors = np.concatenate(
        [
            cos_sin(by_y * (8 * np.arange(H // 8))[None, :, None]).reshape(ANGLES, H // 4, N),
            cos_sin(by_y * np.arange(8)[None, :, None]).reshape(ANGLES, 16, N),
            nyquist,
        ],
        1,
    )
    freq = np.arange(H, dtype=np.float64)
    freq[0] = H
    by_k = unit_one[:PAIRS, None, None] * freq[None, None, :]
    rows_coarse = cos_sin(by_k * cells[::8][None, :, None])
    rows_fine = cos_sin(by_k * np.arange(8)[None, :, None])
    rows_tables = np.concatenate([rows_coarse, rows_fine], 2)
    frequencies = np.arange(H, dtype=np.float64)
    turns = unit_two[:, None, None] * frequencies[None, :, None] * (H - 0.5 - np.arange(H))[None, None, :]
    low = np.cos(unit_two[:, None] * H * cells[None, :H])
    high = np.cos(unit_two[:, None] * H * cells[None, :H - 1:-1])
    table = np.concatenate([np.cos(turns), np.sin(turns)], 1)
    table[:, H] = 0.5 * (low - high)
    beams = np.ascontiguousarray(np.moveaxis(split_const(table), 0, 1))
    edges = np.zeros((PAIRS, 8, H))
    edges[:, 0] = 0.5 * (low + high)
    middle = 0.5 * unit_two[:, None] * frequencies[None, :]
    ordered = np.stack([middle, -middle], 1).reshape(ANGLES, H)
    middles = np.concatenate([np.cos(ordered), np.sin(ordered)], 0)
    return [t if t.dtype == BF16 else t.astype(np.float32) for t in (factors, rows_tables, beams, edges, middles)]


def mm(a, b):
    return lax.dot_general(a, b, (((1,), (0,)), ((), ())), preferred_element_type=F32)


def mm_t(a, b):
    return lax.dot_general(a, b, (((1,), (1,)), ((), ())), preferred_element_type=F32)


def split(value):
    high = value.astype(BF16)
    return high, (value - high.astype(F32)).astype(BF16)


def three(dot, a, b):
    rows = a[0].shape[0]
    both = dot(jnp.concatenate([a[0], a[1]], 0), b[0])
    return both[:rows] + (both[rows:] + dot(a[0], b[1]))


def forward_kernel(
    sc, volume, dft_hbm, dft_t_hbm, factors_hbm, beams_hbm, edges_hbm, out,
    slab, dft, dft_t, factors, beams, edges, spec, turned, field, sems,
):
    number = sc[0]
    mirrored = number >= PAIRS
    sign = jnp.where(mirrored, -1.0, 1.0)
    folded = jnp.where(mirrored, ANGLES - 1 - number, number)
    copies = [
        (volume.at[0], slab),
        (dft_hbm, dft),
        (factors_hbm.at[number], factors),
        (dft_t_hbm.at[:, pl.ds(0, H), :], dft_t),
        (beams_hbm.at[folded], beams),
        (edges_hbm.at[folded], edges),
    ]
    moves = [pltpu.make_async_copy(source, target, sems.at[i]) for i, (source, target) in enumerate(copies)]
    for move in moves:
        move.start()
    halves = (slice(0, H), slice(H, N))
    rows, lanes = (lax.broadcasted_iota(jnp.int32, (H, H), axis) for axis in (0, 1))
    reverse = jnp.where(rows + lanes == H - 1, 1.0, 0.0).astype(BF16)
    moves[0].wait()
    backward = mm(slab[:, H:], reverse).astype(BF16)
    moves[1].wait()
    moves[2].wait()
    for lanes, columns in zip(halves, (slab[:, :H], backward)):
        both = mm(jnp.concatenate([dft[0], dft[1]], 0), columns)
        spec[:, lanes] = both[:N] + both[N:]
    half_row = jnp.where(lax.broadcasted_iota(jnp.int32, (8, H), 0) == 0, 0.5, 1.0)
    for lanes in halves:
        cb, sb = factors[64:72, lanes], factors[72:80, lanes]
        for pair in range(H // 16):
            reals, imags = [], []
            for u in (2 * pair, 2 * pair + 1):
                ca, sa = factors[u : u + 1, lanes], factors[32 + u : 33 + u, lanes]
                c, s = ca * cb - sa * sb, sa * cb + ca * sb
                a, b = spec[8 * u : 8 * u + 8, lanes], spec[H + 8 * u : H + 8 * u + 8, lanes]
                real, imag = a * c - b * s, a * s + b * c
                if u == 0:
                    real, imag = real * half_row, imag * factors[80:88, lanes]
                reals.append(real)
                imags.append(imag)
            for base, parts in ((16 * pair, reals), (H + 16 * pair, imags)):
                at = slice(base, base + 16)
                turned[0, at, lanes], turned[1, at, lanes] = split(jnp.concatenate(parts, 0))
    moves[3].wait()
    for comps in halves:
        for t in range(2):
            near, far = slice(t * W, (t + 1) * W), slice(H + t * W, H + (t + 1) * W)
            both = three(
                mm,
                (dft_t[0, :, comps], dft_t[1, :, comps]),
                [jnp.concatenate([turned[p, comps, near], turned[p, comps, far]], 1) for p in range(2)],
            )
            field[0, 0, comps, near], field[0, 1, comps, near] = split(both[:, :W] + both[:, W:])
            field[1, 0, comps, near], field[1, 1, comps, near] = split(both[:, :W] - both[:, W:])
    moves[4].wait()
    moves[5].wait()
    c = beams[0, :H, :].astype(F32) + beams[1, :H, :].astype(F32)
    s = beams[0, H:, :].astype(F32) + beams[1, H:, :].astype(F32)
    top = lax.broadcasted_iota(jnp.int32, (8, H), 0) == 0
    c_imag = jnp.concatenate([jnp.where(top, edges[:1, :], c[:8]), c[8:]], 0)
    s_imag = jnp.concatenate([jnp.where(top, 0.0, s[:8]), s[8:]], 0) * sign

    def fold(value):
        return value[:, :W] + value[:, W:]

    def beam(part, rows):
        comps = halves[part]
        return three(mm_t, (dft[0, comps, :H], dft[1, comps, :H]), (field[part, 0, rows], field[part, 1, rows]))

    real = fold(beam(0, halves[0]) * c)
    imag = fold(beam(1, halves[0]) * c_imag)
    odd = beam(1, halves[1])
    real = real + fold(odd * s_imag)
    extra = jnp.where(top[:, :W], fold(odd[:8] * s[:8]), 0.0)
    imag = imag - fold(beam(0, halves[1]) * s_imag)
    imag = jnp.concatenate([imag[:8] + extra, imag[8:]], 0)
    real, imag = jnp.sum(real, axis=1, keepdims=True), jnp.sum(imag, axis=1, keepdims=True)
    weight = jnp.where(lax.broadcasted_iota(jnp.int32, (H, 1), 0) == 0, 0.5, 1.0)
    real, imag = real * weight, imag * weight
    c_mid, s_mid = c[:, H - 1 :], s_imag[:, H - 1 :]
    real, imag = real * c_mid + imag * s_mid, imag * c_mid - real * s_mid
    total = jnp.zeros((8, N), F32)
    for r in range(0, H, 32):
        at, below = slice(r, r + 32), slice(H + r, H + r + 32)
        f_real = dft[0, at, :].astype(F32) + dft[1, at, :].astype(F32)
        f_imag = dft[0, below, :].astype(F32) + dft[1, below, :].astype(F32)
        terms = real[at] * f_real + imag[at] * f_imag
        total = total + jnp.sum(terms.reshape(4, 8, N), axis=0)
    row = jnp.sum(total, axis=0, keepdims=True) * (8.0 / (N * N))
    for t in range(4):
        out[pl.ds(t, ROWS, stride=4), :] = jnp.broadcast_to(row[:, t * W : (t + 1) * W], (ROWS, W))


def turn(block):
    return jnp.concatenate(
        [
            jnp.concatenate([block[:W, :W], block[W:, :W]], 1),
            jnp.concatenate([block[:W, W:], block[W:, W:]], 1),
        ],
        0,
    )


def pairs_of_modes():
    return [(j, j + MODES // 2) for j in range(MODES // 2)]


def prepare_kernel(row_ref, probe, dfts, waves, band_dft, band_probe, stage):
    start = -row_ref[0, 0]
    lefts, rights = (dfts[0, 0], dfts[0, 1]), (dfts[1, 0], dfts[1, 1])
    for j, pair in enumerate(pairs_of_modes()):
        reals = jnp.concatenate([probe[m, 0] for m in pair], 1)
        imags = jnp.concatenate([probe[m, 1] for m in pair], 1)
        stage[0, j], stage[1, j] = split(jnp.concatenate([reals, imags], 0))
    for j in range(MODES // 2):
        stage[0, j], stage[1, j] = split(turn(three(mm, lefts, (stage[0, j], stage[1, j]))))
    for j in range(MODES // 2):
        waves[j] = three(mm, (stage[0, j], stage[1, j]), rights)
    source = lax.broadcasted_iota(jnp.int32, (2 * W, 2 * W), 0)
    target = lax.broadcasted_iota(jnp.int32, (2 * W, 2 * W), 1)
    wanted = start + (target & (ROWS - 1)) + jnp.where(target & ROWS != 0, W, 0)
    chosen = jnp.where(source == wanted, 1.0, 0.0)
    first = jnp.where(target < 4 * ROWS, chosen, 0.0).astype(BF16)
    second = jnp.where((target >= 4 * ROWS) & (target < 6 * ROWS), chosen, 0.0).astype(BF16)
    band_dft[...] = (mm(lefts[0], first) + mm(lefts[1], second)).astype(BF16)
    for m in range(MODES):
        for part in range(2):
            band_probe[m, part] = probe[m, part, pl.ds(start, ROWS), :]


def window_kernel(
    row_ref, col_ref, whole, probe, measured, dfts, waves, band_dft, band_probe, keep, send, stage, far, pieces
):
    row, col, core = row_ref[0, 0], col_ref[0, 0], lax.axis_index("core")
    rows = jnp.concatenate([whole[pl.ds(t, ROWS, stride=4), :] for t in range(4)], axis=1)
    band = pltpu.roll(rows, lax.rem(N - col, N), 1)[:, :W]
    band_real, band_imag = jnp.cos(band) - 1.0, jnp.sin(band)
    lefts, rights = (dfts[0, 0], dfts[0, 1]), (dfts[1, 0], dfts[1, 1])
    pairs = pairs_of_modes()
    sides = (slice(0, W), slice(W, 2 * W))

    def put(j, value):
        stage[0, j], stage[1, j] = split(value)

    def get(j):
        return stage[0, j], stage[1, j]

    lines = []
    for m in [m for pair in pairs for m in pair]:
        p_real, p_imag = band_probe[m, 0], band_probe[m, 1]
        lines.append(
            jnp.concatenate(
                [p_real * band_real - p_imag * band_imag, p_real * band_imag + p_imag * band_real], 1
            )
        )
    lines = three(mm, split(jnp.concatenate(lines, 0)), rights)
    intensity = jnp.zeros((W, W), F32)
    for j in range(MODES // 2):
        one, two = (lines[2 * ROWS * j + ROWS * i : 2 * ROWS * j + ROWS * (i + 1)] for i in range(2))
        both = jnp.concatenate(
            [jnp.concatenate([one[:, :W], two[:, :W]], 1), jnp.concatenate([one[:, W:], two[:, W:]], 1)], 0
        )
        high, low = split(both)
        blank = jnp.zeros((2 * ROWS, 2 * W), BF16)
        total = waves[j] + turn(mm(band_dft[...], jnp.concatenate([high, low, high, blank], 0)))
        far[j] = total
        power = total * total
        power = power[:W] + power[W:]
        intensity = intensity + (power[:, :W] + power[:, W:])
    pad = jnp.zeros((W - ROWS, W), F32)
    obj_real = pltpu.roll(jnp.concatenate([band_real, pad], 0), -row, 0) + 1.0
    obj_imag = pltpu.roll(jnp.concatenate([band_imag, pad], 0), -row, 0)
    factor = (1.0 - jnp.sqrt(measured[0, 0] + 1.0) / jnp.sqrt(intensity + 1.0)) * (1.0 / W)
    factors = jnp.concatenate([jnp.concatenate([factor, factor], 1)] * 2, 0)
    for j in range(MODES // 2):
        put(j, far[j] * factors)
    for j in range(MODES // 2):
        put(j, turn(three(mm, get(j), lefts)))
    grad_real, grad_imag = jnp.zeros((W, W), F32), jnp.zeros((W, W), F32)
    for j, pair in enumerate(pairs):
        back = three(mm, rights, get(j))
        grads = []
        for m, lanes in zip(pair, sides):
            b_real, b_imag = back[:W, lanes], back[W:, lanes]
            p_real, p_imag = probe[m, 0], probe[m, 1]
            grad_real = grad_real + (p_real * b_real + p_imag * b_imag)
            grad_imag = grad_imag + (p_real * b_imag - p_imag * b_real)
            grads.append((obj_real * b_real + obj_imag * b_imag, obj_real * b_imag - obj_imag * b_real))
        for part in range(2):
            at = slice((2 * j + part) * W, (2 * j + part + 1) * W)
            keep[at, :] = jnp.where(core == 0, grads[0][part], grads[1][part])
            send[at, :] = jnp.where(core == 0, grads[1][part], grads[0][part])
    patch = grad_imag * obj_real - grad_real * obj_imag
    shown = pltpu.roll(patch, W + row, 0)[:ROWS]
    pieces[...] = pltpu.roll(shown, lax.rem(col, W), 1)
    even, odd = pieces[pl.ds(0, 16, stride=2), :], pieces[pl.ds(1, 16, stride=2), :]
    keep[HALF : HALF + 16, :] = jnp.where(core == 0, even, odd)
    send[HALF : HALF + 16, :] = jnp.where(core == 0, odd, even)
    column = jnp.full((8, W), col, jnp.int32).astype(F32)
    keep[HALF + 16 :, :] = column
    send[HALF + 16 :, :] = column


def pack_kernel(sc, keep, other, out):
    lane = lax.broadcasted_iota(jnp.int32, (1, W), 1)
    first, second = keep[HALF + 16 : HALF + 17, :], other[HALF + 16 : HALF + 17, :]
    numbers = jnp.where(lane < 32, sc[0].astype(F32), jnp.where(lane < 64, first, second))
    for peer in range(16):
        rows = slice(CHUNK * peer, CHUNK * (peer + 1))
        at = MESSAGE * peer
        out[at : at + CHUNK, :] = keep[rows, :] + other[rows, :]
        rows = slice(HALF + 8 * (peer % 2), HALF + 8 * (peer % 2) + 8)
        out[at + CHUNK : at + CHUNK + 8, :] = keep[rows, :]
        out[at + CHUNK + 8 : at + CHUNK + 16, :] = other[rows, :]
        out[at + CHUNK + 16 : at + MESSAGE, :] = numbers


def relay_kernel(received, out, pieces, numbers):
    total = received[:CHUNK, :]
    for peer in range(1, 16):
        total = total + received[MESSAGE * peer : MESSAGE * peer + CHUNK, :]
    heads = jnp.concatenate([received[pl.ds(MESSAGE * p + MESSAGE - 1, 1), :] for p in range(16)], 0)
    rolls = [heads] + [pltpu.roll(heads, 32 * i, 1) for i in (1, 2, 3)]
    quarter = lax.broadcasted_iota(jnp.int32, (16, W), 1) // 32
    for i in range(3):
        value = rolls[0]
        for shift in (1, 2, 3):
            value = jnp.where(quarter == (i + shift) % 4, rolls[shift], value)
        numbers[i] = value
    windows = [(peer, side) for peer in range(16) for side in range(2)]
    rows = jnp.concatenate(
        [received[MESSAGE * p + CHUNK + 8 * i : MESSAGE * p + CHUNK + 8 * i + 8, :] for p, i in windows], 0
    )
    columns = jnp.concatenate(
        [jnp.broadcast_to(numbers[1 + i, p : p + 1, :], (8, W)) for p, i in windows], 0
    ).astype(jnp.int32)
    lane = lax.broadcasted_iota(jnp.int32, rows.shape, 1)
    tiles = (columns >> 7) + jnp.where(lane < (columns & (W - 1)), 1, 0)
    for a in range(ANGLES):
        angle = jnp.max(numbers[0, 2 * a : 2 * a + 1, :]).astype(jnp.int32)
        slot = jnp.where(angle >= PAIRS, 2 * (ANGLES - 1 - angle) + 1, 2 * angle)
        at = pl.multiple_of(32 * slot, 32)
        for t in range(4):
            part = jnp.where(tiles[32 * a : 32 * a + 32] == t, rows[32 * a : 32 * a + 32], 0.0)
            pieces[pl.ds(at + 8 * t, 8), :] = jnp.sum(part.reshape(4, 8, W), axis=0)
    for z in range(8):
        out[z, :CHUNK, :] = total
        out[z, CHUNK:, :] = pieces[pl.ds(z, 32, stride=8), :]


def adjoint_kernel(received, dft_t, leaving, rows_tables, edges, middles, *refs):
    beams, (out, pieces, shifted, sheared) = refs[:PAIRS], refs[PAIRS:]
    block = 2 * lax.axis_index("y") + lax.axis_index("xh")
    total = received[0]
    for z in range(1, 8):
        total = total + received[z]
    chunk = total[:CHUNK] * (1.0 / 16.0)
    pieces[...] = total[CHUNK:]
    rows = jnp.concatenate([pieces[pl.ds(t, 8, stride=4), :] for t in range(4)], axis=1)
    spectrum = three(mm, split(rows), (dft_t[0], dft_t[1]))
    weight = jnp.where(lax.broadcasted_iota(jnp.int32, (8, N), 1) % H == 0, 0.5 / N, 1.0 / N)
    cbar = spectrum * weight
    c_mid, s_mid = middles[:ANGLES, :], middles[ANGLES:, :]
    c_reals = cbar[:, :H] * c_mid - cbar[:, H:] * s_mid
    c_imags = cbar[:, H:] * c_mid + cbar[:, :H] * s_mid
    at = pl.ds(pl.multiple_of(64 * block, 64), 64)
    rows_dft = dft_t[0, at, :].astype(F32) + dft_t[1, at, :].astype(F32)
    lane_zero = lax.broadcasted_iota(jnp.int32, (64, H), 1) == 0
    r_cos, r_sin = rows_dft[:, :H], rows_dft[:, H:]
    r_sin_real = jnp.where(lane_zero, 0.0, r_sin)
    r_cos_imag = jnp.where(lane_zero, r_sin, r_cos)
    mirror = jnp.where(lane_zero, 1.0, -1.0)
    nyquist = []
    for slot in range(ANGLES):
        c_real, c_imag = c_reals[slot : slot + 1, :], c_imags[slot : slot + 1, :]
        cosines = c_real * r_cos + c_imag * r_sin_real
        sines = c_imag * r_cos_imag - c_real * r_sin_real
        if slot % 2 == 0:
            sines = sines * mirror
        nyquist.append(sines[:, :1])
        at = slice(64 * slot, 64 * slot + 64)
        shifted[0, at, :H], shifted[1, at, :H] = split(cosines)
        shifted[0, at, H:], shifted[1, at, H:] = split(sines)
    for q in range(PAIRS):
        at = slice(2 * 64 * q, 2 * 64 * (q + 1))
        even = three(mm, (shifted[0, at, :H], shifted[1, at, :H]), (beams[q][0, :H, :], beams[q][1, :H, :]))
        odd = three(mm, (shifted[0, at, H:], shifted[1, at, H:]), (beams[q][0, H:, :], beams[q][1, H:, :]))
        even = even + jnp.concatenate(nyquist[2 * q : 2 * q + 2], 0) * edges[q, 0:1, :]
        sheared[0, at, :H], sheared[1, at, :H] = split(even)
        sheared[0, at, H:], sheared[1, at, H:] = split(odd)
    lane_first = lax.broadcasted_iota(jnp.int32, (8, H), 1) == 0
    sums = [None] * 8
    for q in range(PAIRS):
        at = slice(2 * 64 * q, 2 * 64 * (q + 1))
        real, imag = (
            three(mm, (sheared[0, at, part], sheared[1, at, part]), (dft_t[0, :H, part], dft_t[1, :H, part]))
            for part in (slice(0, H), slice(H, N))
        )
        cb, sb = rows_tables[q, 0, 64:72, :], rows_tables[q, 1, 64:72, :]
        near = rows_tables[q, :, pl.ds(pl.multiple_of(8 * block, 8), 8), :]
        for u in range(8):
            ca, sa = near[0, u : u + 1, :], near[1, u : u + 1, :]
            c, s = ca * cb - sa * sb, sa * cb + ca * sb
            c_first, s_first = jnp.where(lane_first, 1.0, c), jnp.where(lane_first, 0.0, s)
            one, two = slice(8 * u, 8 * u + 8), slice(64 + 8 * u, 72 + 8 * u)
            unturned = jnp.concatenate(
                [
                    (real[one] + real[two]) * c_first + (imag[one] - imag[two]) * s_first,
                    (imag[one] + imag[two]) * c - (real[one] - real[two]) * s_first,
                ],
                1,
            )
            sums[u] = unturned if q == 0 else sums[u] + unturned
    weight = jnp.where(lax.broadcasted_iota(jnp.int32, (64, N), 1) % H == 0, 1.0 / 32.0, 1.0 / 16.0)
    whole = jnp.concatenate(sums, 0) * weight
    columns = three(mm, split(whole), (leaving[0], leaving[1]))
    for part in range(2):
        first, second = (columns[:, (2 * part + i) * W : (2 * part + i + 1) * W] for i in range(2))
        blocks = jnp.concatenate([first, second], 0).T
        for peer in range(8 * part, 8 * part + 8):
            out[peer, :CHUNK, :] = chunk
            a = peer // 2 - 4 * part
            out[peer, CHUNK:, :] = blocks[32 * a : 32 * a + 32, :]


def assemble_kernel(received, out, probe_out, sem):
    move = pltpu.make_async_copy(received.at[:, pl.ds(0, CHUNK), :], probe_out.at[lax.axis_index("core")], sem)
    move.start()
    xl = lax.axis_index("xl")
    lower = lax.broadcasted_iota(jnp.int32, (32, W), 1) < 64
    for b in range(4):
        even = received[4 * b + xl, CHUNK:, :]
        odd = received[4 * b + 2 + xl, CHUNK:, :]
        lanes = slice(b * W, (b + 1) * W)
        out[0, :32, lanes] = jnp.where(lower, even, pltpu.roll(odd, 64, 1))
        out[0, 32:, lanes] = jnp.where(lower, pltpu.roll(even, 64, 1), odd)
    move.wait()


def forward_call(*args):
    return pl.pallas_call(
        forward_kernel,
        in_specs=[pl.BlockSpec(memory_space=pltpu.SMEM)] + [pl.BlockSpec(memory_space=pl.ANY)] * 6,
        out_specs=pl.BlockSpec(memory_space=pltpu.VMEM),
        out_shape=jax.ShapeDtypeStruct((4 * ROWS, W), F32),
        scratch_shapes=[
            pltpu.VMEM((N, N), BF16),
            pltpu.VMEM((2, N, N), BF16),
            pltpu.VMEM((2, H, N), BF16),
            pltpu.VMEM((H // 4 + 24, N), F32),
            pltpu.VMEM((2, N, H), BF16),
            pltpu.VMEM((8, H), F32),
            pltpu.VMEM((N, N), F32),
            pltpu.VMEM((2, N, N), BF16),
            pltpu.VMEM((2, 2, N, H), BF16),
            pltpu.SemaphoreType.DMA((6,)),
        ],
        compiler_params=pltpu.CompilerParams(vmem_limit_bytes=60 * 1024 * 1024),
        cost_estimate=pl.CostEstimate(flops=4 * 10**9, bytes_accessed=4 * 10**6, transcendentals=0),
        name="forward",
    )(*args)


def vmem_call(kernel, outs, scratch, name, *args, far=0):
    result = pl.pallas_call(
        kernel,
        in_specs=[
            pl.BlockSpec(memory_space=pltpu.SMEM if a.dtype == jnp.int32 else pltpu.VMEM) for a in args
        ],
        out_specs=[pl.BlockSpec(memory_space=pltpu.VMEM)] * (len(outs) - far)
        + [pl.BlockSpec(memory_space=pl.ANY)] * far,
        out_shape=[jax.ShapeDtypeStruct(*o) if o[-1] == BF16 else jax.ShapeDtypeStruct(o, F32) for o in outs],
        scratch_shapes=scratch,
        compiler_params=pltpu.CompilerParams(vmem_limit_bytes=32 * 1024 * 1024),
        cost_estimate=pl.CostEstimate(flops=3 * 10**9, bytes_accessed=4 * 10**6, transcendentals=0),
        name=name,
    )(*args)
    return result if len(outs) > 1 else result[0]


GZ = ("xl", "z", "core")
PLANE = ("y", "xh", "xl")


def exchange(blocks, axes):
    return lax.all_to_all(blocks, axes, split_axis=0, concat_axis=0, tiled=True)


def swap(rows):
    return lax.ppermute(rows, "core", [(0, 1), (1, 0)])


def local(volume, probe, measured, angle_index, row_offset, col_offset):
    dft, dft_t, leaving = (jnp.asarray(t) for t in dft_tables())
    dfts = jnp.asarray(window_tables())
    factors, rows_tables, all_beams, edges, middles = (jnp.asarray(t) for t in phase_tables())
    beams = [jnp.asarray(b) for b in phase_tables()[2]]
    row = forward_call(angle_index, volume, dft, dft_t, factors, all_beams, edges)
    whole = exchange(row.reshape(ROWS, 4, W), GZ).reshape(4 * ROWS, W)
    split_modes = pltpu.VMEM((2, MODES // 2, 2 * W, 2 * W), BF16)
    waves, band_dft, band_probe = vmem_call(
        prepare_kernel,
        [(MODES // 2, 2 * W, 2 * W), ((2 * W, 2 * W), BF16), (MODES, 2, ROWS, W)],
        [split_modes],
        "prepare",
        row_offset,
        probe,
        dfts,
    )
    keep, send = vmem_call(
        window_kernel,
        [(HALF + 24, W)] * 2,
        [split_modes, pltpu.VMEM((MODES // 2, 2 * W, 2 * W), F32), pltpu.VMEM((ROWS, W), F32)],
        "window",
        row_offset,
        col_offset,
        whole,
        probe,
        measured,
        dfts,
        waves,
        band_dft,
        band_probe,
    )
    packed = vmem_call(pack_kernel, [(16 * MESSAGE, W)], [], "pack", angle_index, keep, swap(send))
    shared = exchange(packed.reshape(16, MESSAGE, 1, W), PLANE).reshape(16 * MESSAGE, W)
    relay = vmem_call(relay_kernel, [(8, CHUNK + 32, W)], [pltpu.VMEM((256, W), F32), pltpu.VMEM((3, 16, W), F32)], "relay", shared)
    rows = exchange(relay, "z")
    blocks = vmem_call(
        adjoint_kernel,
        [(16, CHUNK + 32, W)],
        [pltpu.VMEM((32, W), F32), pltpu.VMEM((2, N, N), BF16), pltpu.VMEM((2, N, N), BF16)],
        "adjoint",
        rows,
        dft_t,
        leaving,
        rows_tables,
        edges,
        middles,
        *beams,
    )
    final = exchange(blocks, PLANE)
    other = swap(final[:, :CHUNK, :])
    volume_update, half = vmem_call(
        assemble_kernel,
        [(1, 64, N), (2, 16, CHUNK, W)],
        [pltpu.SemaphoreType.DMA],
        "assemble",
        final,
        far=1,
    )
    core = lax.axis_index("core")
    probe_update = lax.dynamic_update_slice(half, other[None], (1 - core, 0, 0, 0))
    return volume_update, probe_update.reshape(MODES, 2, W, W)


def solution(mesh):
    split_mesh = Mesh(mesh.devices.reshape(4, 2, 2, 8, 2), ("y", "xh", "xl", "z", "core"))
    angle, gz = ("y", "xh"), GZ
    return jax.shard_map(
        local,
        mesh=split_mesh,
        in_specs=(
            P(gz, None, None),
            P(),
            P(angle, gz, None, None),
            P(angle),
            P(angle, gz),
            P(angle, gz),
        ),
        out_specs=(P(gz, angle, None), P()),
        check_vma=False,
    )
```

```python
import math

import jax
import jax.numpy as jnp
import numpy as np
from jax import lax
from jax.experimental import pallas as pl
from jax.experimental.pallas import tpu as pltpu
from jax.sharding import Mesh, PartitionSpec as P

N = 512
H = N // 2
W = 128
MODES = 8
ANGLES = 8
PAIRS = ANGLES // 2
ROWS = 32
HALF = MODES * 2 * W // 2
CHUNK = HALF // 16
PART = CHUNK // 2
MESSAGE = PART + 9
F32 = jnp.float32
BF16 = jnp.bfloat16


def split_const(table):
    high = table.astype(BF16)
    low = (table - high.astype(np.float64)).astype(BF16)
    return np.stack([high, low])


def dft_tables():
    k, n = np.arange(H)[:, None], np.arange(N)[None, :]
    turns = np.pi / N * (k * (2 * n + 1) % (2 * N))
    table = np.concatenate([np.cos(turns), -np.sin(turns)], 0)
    table[H] = 2.0 * (np.arange(N) % 2) - 1.0
    order = np.arange(N).reshape(2, 4, 2, 32).transpose(0, 2, 1, 3).reshape(N)
    return [split_const(np.ascontiguousarray(t)) for t in (table, table.T, table[:, order])]


def window_tables():
    j = np.arange(W)
    turns = 2.0 * np.pi / W * (j[:, None] * j[None, :] % W)
    c, s = np.cos(turns), np.sin(turns)
    return np.stack([split_const(np.block([[c, s], [-s, c]])), split_const(np.block([[c, -s], [s, c]]))])


def shears():
    theta = np.pi * (np.arange(ANGLES) + 0.5) / ANGLES - np.pi / 2
    return -np.tan(theta / 2), np.sin(theta)


def cos_sin(phase):
    return np.stack([np.cos(phase), np.sin(phase)], 1)


def phase_tables():
    shear_x, shear_y = shears()
    cells = np.arange(N) - N / 2
    unit_one = -2.0 * np.pi / N * shear_x
    unit_two = -2.0 * np.pi / N * shear_y[:PAIRS]
    by_y = unit_one[:, None, None] * np.concatenate([cells[:H], cells[:H - 1:-1]])[None, None, :]
    nyquist = np.ones((ANGLES, 8, N))
    nyquist[:, 0] = 0.5 * np.cos(by_y[:, 0] * H)
    factors = np.concatenate(
        [
            cos_sin(by_y * (8 * np.arange(H // 8))[None, :, None]).reshape(ANGLES, H // 4, N),
            cos_sin(by_y * np.arange(8)[None, :, None]).reshape(ANGLES, 16, N),
            nyquist,
        ],
        1,
    )
    freq = np.arange(H, dtype=np.float64)
    freq[0] = H
    by_k = unit_one[:PAIRS, None, None] * freq[None, None, :]
    rows_coarse = cos_sin(by_k * cells[::8][None, :, None])
    rows_fine = cos_sin(by_k * np.arange(8)[None, :, None])
    rows_tables = np.concatenate([rows_coarse, rows_fine], 2)
    frequencies = np.arange(H, dtype=np.float64)
    turns = unit_two[:, None, None] * frequencies[None, :, None] * (H - 0.5 - np.arange(H))[None, None, :]
    low = np.cos(unit_two[:, None] * H * cells[None, :H])
    high = np.cos(unit_two[:, None] * H * cells[None, :H - 1:-1])
    table = np.concatenate([np.cos(turns), np.sin(turns)], 1)
    table[:, H] = 0.5 * (low - high)
    beams = np.ascontiguousarray(np.moveaxis(split_const(table), 0, 1))
    edges = np.zeros((PAIRS, 8, H))
    edges[:, 0] = 0.5 * (low + high)
    middle = 0.5 * unit_two[:, None] * frequencies[None, :]
    ordered = np.stack([middle, -middle], 1).reshape(ANGLES, H)
    middles = np.concatenate([np.cos(ordered), np.sin(ordered)], 0)
    return [t if t.dtype == BF16 else t.astype(np.float32) for t in (factors, rows_tables, beams, edges, middles)]


def mm(a, b):
    return lax.dot_general(a, b, (((1,), (0,)), ((), ())), preferred_element_type=F32)


def mm_t(a, b):
    return lax.dot_general(a, b, (((1,), (1,)), ((), ())), preferred_element_type=F32)


def split(value):
    high = value.astype(BF16)
    return high, (value - high.astype(F32)).astype(BF16)


def three(dot, a, b):
    rows = a[0].shape[0]
    both = dot(jnp.concatenate([a[0], a[1]], 0), b[0])
    return both[:rows] + (both[rows:] + dot(a[0], b[1]))


def forward_kernel(
    sc, volume, dft_hbm, dft_t_hbm, factors_hbm, beams_hbm, edges_hbm, out,
    slab, dft, dft_t, factors, beams, edges, spec, turned, field, sems,
):
    number = sc[0]
    mirrored = number >= PAIRS
    sign = jnp.where(mirrored, -1.0, 1.0)
    folded = jnp.where(mirrored, ANGLES - 1 - number, number)
    copies = [
        (volume.at[0], slab),
        (dft_hbm, dft),
        (factors_hbm.at[number], factors),
        (dft_t_hbm.at[:, pl.ds(0, H), :], dft_t),
        (beams_hbm.at[folded], beams),
        (edges_hbm.at[folded], edges),
    ]
    moves = [pltpu.make_async_copy(source, target, sems.at[i]) for i, (source, target) in enumerate(copies)]
    for move in moves:
        move.start()
    halves = (slice(0, H), slice(H, N))
    rows, lanes = (lax.broadcasted_iota(jnp.int32, (H, H), axis) for axis in (0, 1))
    reverse = jnp.where(rows + lanes == H - 1, 1.0, 0.0).astype(BF16)
    moves[0].wait()
    backward = mm(slab[:, H:], reverse).astype(BF16)
    moves[1].wait()
    moves[2].wait()
    for lanes, columns in zip(halves, (slab[:, :H], backward)):
        both = mm(jnp.concatenate([dft[0], dft[1]], 0), columns)
        spec[:, lanes] = both[:N] + both[N:]
    half_row = jnp.where(lax.broadcasted_iota(jnp.int32, (8, H), 0) == 0, 0.5, 1.0)
    for lanes in halves:
        cb, sb = factors[64:72, lanes], factors[72:80, lanes]
        for pair in range(H // 16):
            reals, imags = [], []
            for u in (2 * pair, 2 * pair + 1):
                ca, sa = factors[u : u + 1, lanes], factors[32 + u : 33 + u, lanes]
                c, s = ca * cb - sa * sb, sa * cb + ca * sb
                a, b = spec[8 * u : 8 * u + 8, lanes], spec[H + 8 * u : H + 8 * u + 8, lanes]
                real, imag = a * c - b * s, a * s + b * c
                if u == 0:
                    real, imag = real * half_row, imag * factors[80:88, lanes]
                reals.append(real)
                imags.append(imag)
            for base, parts in ((16 * pair, reals), (H + 16 * pair, imags)):
                at = slice(base, base + 16)
                turned[0, at, lanes], turned[1, at, lanes] = split(jnp.concatenate(parts, 0))
    moves[3].wait()
    for comps in halves:
        for t in range(2):
            near, far = slice(t * W, (t + 1) * W), slice(H + t * W, H + (t + 1) * W)
            both = three(
                mm,
                (dft_t[0, :, comps], dft_t[1, :, comps]),
                [jnp.concatenate([turned[p, comps, near], turned[p, comps, far]], 1) for p in range(2)],
            )
            field[0, 0, comps, near], field[0, 1, comps, near] = split(both[:, :W] + both[:, W:])
            field[1, 0, comps, near], field[1, 1, comps, near] = split(both[:, :W] - both[:, W:])
    moves[4].wait()
    moves[5].wait()
    c = beams[0, :H, :].astype(F32) + beams[1, :H, :].astype(F32)
    s = beams[0, H:, :].astype(F32) + beams[1, H:, :].astype(F32)
    top = lax.broadcasted_iota(jnp.int32, (8, H), 0) == 0
    c_imag = jnp.concatenate([jnp.where(top, edges[:1, :], c[:8]), c[8:]], 0)
    s_imag = jnp.concatenate([jnp.where(top, 0.0, s[:8]), s[8:]], 0) * sign

    def fold(value):
        return value[:, :W] + value[:, W:]

    def beam(part, rows):
        comps = halves[part]
        return three(mm_t, (dft[0, comps, :H], dft[1, comps, :H]), (field[part, 0, rows], field[part, 1, rows]))

    real = fold(beam(0, halves[0]) * c)
    imag = fold(beam(1, halves[0]) * c_imag)
    odd = beam(1, halves[1])
    real = real + fold(odd * s_imag)
    extra = jnp.where(top[:, :W], fold(odd[:8] * s[:8]), 0.0)
    imag = imag - fold(beam(0, halves[1]) * s_imag)
    imag = jnp.concatenate([imag[:8] + extra, imag[8:]], 0)
    real, imag = jnp.sum(real, axis=1, keepdims=True), jnp.sum(imag, axis=1, keepdims=True)
    weight = jnp.where(lax.broadcasted_iota(jnp.int32, (H, 1), 0) == 0, 0.5, 1.0)
    real, imag = real * weight, imag * weight
    c_mid, s_mid = c[:, H - 1 :], s_imag[:, H - 1 :]
    real, imag = real * c_mid + imag * s_mid, imag * c_mid - real * s_mid
    total = jnp.zeros((8, N), F32)
    for r in range(0, H, 32):
        at, below = slice(r, r + 32), slice(H + r, H + r + 32)
        f_real = dft[0, at, :].astype(F32) + dft[1, at, :].astype(F32)
        f_imag = dft[0, below, :].astype(F32) + dft[1, below, :].astype(F32)
        terms = real[at] * f_real + imag[at] * f_imag
        total = total + jnp.sum(terms.reshape(4, 8, N), axis=0)
    row = jnp.sum(total, axis=0, keepdims=True) * (8.0 / (N * N))
    for t in range(4):
        out[pl.ds(t, ROWS, stride=4), :] = jnp.broadcast_to(row[:, t * W : (t + 1) * W], (ROWS, W))


def turn(block):
    return jnp.concatenate(
        [
            jnp.concatenate([block[:W, :W], block[W:, :W]], 1),
            jnp.concatenate([block[:W, W:], block[W:, W:]], 1),
        ],
        0,
    )


def pairs_of_modes():
    return [(j, j + MODES // 2) for j in range(MODES // 2)]


def prepare_kernel(row_ref, probe, dfts, waves, band_dft, band_probe, stage):
    start = -row_ref[0, 0]
    lefts, rights = (dfts[0, 0], dfts[0, 1]), (dfts[1, 0], dfts[1, 1])
    for j, pair in enumerate(pairs_of_modes()):
        reals = jnp.concatenate([probe[m, 0] for m in pair], 1)
        imags = jnp.concatenate([probe[m, 1] for m in pair], 1)
        stage[0, j], stage[1, j] = split(jnp.concatenate([reals, imags], 0))
    for j in range(MODES // 2):
        stage[0, j], stage[1, j] = split(turn(three(mm, lefts, (stage[0, j], stage[1, j]))))
    for j in range(MODES // 2):
        waves[j] = three(mm, (stage[0, j], stage[1, j]), rights)
    source = lax.broadcasted_iota(jnp.int32, (2 * W, 2 * W), 0)
    target = lax.broadcasted_iota(jnp.int32, (2 * W, 2 * W), 1)
    wanted = start + (target & (ROWS - 1)) + jnp.where(target & ROWS != 0, W, 0)
    chosen = jnp.where(source == wanted, 1.0, 0.0)
    first = jnp.where(target < 4 * ROWS, chosen, 0.0).astype(BF16)
    second = jnp.where((target >= 4 * ROWS) & (target < 6 * ROWS), chosen, 0.0).astype(BF16)
    band_dft[...] = (mm(lefts[0], first) + mm(lefts[1], second)).astype(BF16)
    for m in range(MODES):
        for part in range(2):
            band_probe[m, part] = probe[m, part, pl.ds(start, ROWS), :]


def window_kernel(
    row_ref, col_ref, whole, probe, measured, dfts, waves, band_dft, band_probe, keep, send, stage, far, pieces
):
    row, col, core = row_ref[0, 0], col_ref[0, 0], lax.axis_index("core")
    rows = jnp.concatenate([whole[pl.ds(t, ROWS, stride=4), :] for t in range(4)], axis=1)
    band = pltpu.roll(rows, lax.rem(N - col, N), 1)[:, :W]
    band_real, band_imag = jnp.cos(band) - 1.0, jnp.sin(band)
    lefts, rights = (dfts[0, 0], dfts[0, 1]), (dfts[1, 0], dfts[1, 1])
    pairs = pairs_of_modes()
    sides = (slice(0, W), slice(W, 2 * W))

    def put(j, value):
        stage[0, j], stage[1, j] = split(value)

    def get(j):
        return stage[0, j], stage[1, j]

    lines = []
    for m in [m for pair in pairs for m in pair]:
        p_real, p_imag = band_probe[m, 0], band_probe[m, 1]
        lines.append(
            jnp.concatenate(
                [p_real * band_real - p_imag * band_imag, p_real * band_imag + p_imag * band_real], 1
            )
        )
    lines = three(mm, split(jnp.concatenate(lines, 0)), rights)
    intensity = jnp.zeros((W, W), F32)
    for j in range(MODES // 2):
        one, two = (lines[2 * ROWS * j + ROWS * i : 2 * ROWS * j + ROWS * (i + 1)] for i in range(2))
        both = jnp.concatenate(
            [jnp.concatenate([one[:, :W], two[:, :W]], 1), jnp.concatenate([one[:, W:], two[:, W:]], 1)], 0
        )
        high, low = split(both)
        blank = jnp.zeros((2 * ROWS, 2 * W), BF16)
        total = waves[j] + turn(mm(band_dft[...], jnp.concatenate([high, low, high, blank], 0)))
        far[j] = total
        power = total * total
        power = power[:W] + power[W:]
        intensity = intensity + (power[:, :W] + power[:, W:])
    pad = jnp.zeros((W - ROWS, W), F32)
    obj_real = pltpu.roll(jnp.concatenate([band_real, pad], 0), -row, 0) + 1.0
    obj_imag = pltpu.roll(jnp.concatenate([band_imag, pad], 0), -row, 0)
    factor = (1.0 - jnp.sqrt(measured[0, 0] + 1.0) / jnp.sqrt(intensity + 1.0)) * (1.0 / W)
    factors = jnp.concatenate([jnp.concatenate([factor, factor], 1)] * 2, 0)
    for j in range(MODES // 2):
        put(j, far[j] * factors)
    for j in range(MODES // 2):
        put(j, turn(three(mm, get(j), lefts)))
    grad_real, grad_imag = jnp.zeros((W, W), F32), jnp.zeros((W, W), F32)
    for j, pair in enumerate(pairs):
        back = three(mm, rights, get(j))
        grads = []
        for m, lanes in zip(pair, sides):
            b_real, b_imag = back[:W, lanes], back[W:, lanes]
            p_real, p_imag = probe[m, 0], probe[m, 1]
            grad_real = grad_real + (p_real * b_real + p_imag * b_imag)
            grad_imag = grad_imag + (p_real * b_imag - p_imag * b_real)
            grads.append((obj_real * b_real + obj_imag * b_imag, obj_real * b_imag - obj_imag * b_real))
        for part in range(2):
            at = slice((2 * j + part) * W, (2 * j + part + 1) * W)
            keep[at, :] = jnp.where(core == 0, grads[0][part], grads[1][part])
            send[at, :] = jnp.where(core == 0, grads[1][part], grads[0][part])
    patch = grad_imag * obj_real - grad_real * obj_imag
    shown = pltpu.roll(patch, W + row, 0)[:ROWS]
    pieces[...] = pltpu.roll(shown, lax.rem(col, W), 1)
    even, odd = pieces[pl.ds(0, 16, stride=2), :], pieces[pl.ds(1, 16, stride=2), :]
    keep[HALF : HALF + 16, :] = jnp.where(core == 0, even, odd)
    send[HALF : HALF + 16, :] = jnp.where(core == 0, odd, even)
    column = jnp.full((8, W), col, jnp.int32).astype(F32)
    keep[HALF + 16 :, :] = column
    send[HALF + 16 :, :] = column


def pack_kernel(sc, keep, other, out):
    lane = lax.broadcasted_iota(jnp.int32, (1, W), 1)
    first, second = keep[HALF + 16 : HALF + 17, :], other[HALF + 16 : HALF + 17, :]
    numbers = jnp.where(lane < 32, sc[0].astype(F32), jnp.where(lane < 64, first, second))
    for peer in range(32):
        rows = slice(PART * peer, PART * (peer + 1))
        at = MESSAGE * peer
        out[at : at + PART, :] = keep[rows, :] + other[rows, :]
        rows = pl.ds(HALF + 8 * (peer // 2 % 2) + peer % 2, 4, stride=2)
        out[at + PART : at + PART + 4, :] = keep[rows, :]
        out[at + PART + 4 : at + PART + 8, :] = other[rows, :]
        out[at + PART + 8 : at + MESSAGE, :] = numbers


def relay_kernel(received, out, pieces, numbers):
    total = received[:PART, :]
    for peer in range(1, 32):
        total = total + received[MESSAGE * peer : MESSAGE * peer + PART, :]
    heads = jnp.concatenate([received[pl.ds(MESSAGE * p + MESSAGE - 1, 1), :] for p in range(32)], 0)
    rolls = [heads] + [pltpu.roll(heads, 32 * i, 1) for i in (1, 2, 3)]
    quarter = lax.broadcasted_iota(jnp.int32, (32, W), 1) // 32
    for i in range(3):
        value = rolls[0]
        for shift in (1, 2, 3):
            value = jnp.where(quarter == (i + shift) % 4, rolls[shift], value)
        numbers[i] = value
    rows = jnp.concatenate([received[MESSAGE * p + PART : MESSAGE * p + PART + 8, :] for p in range(32)], 0)
    first, second = (
        jnp.concatenate([jnp.broadcast_to(numbers[1 + i, p : p + 1, :], (8, W)) for p in range(32)], 0)
        for i in range(2)
    )
    row = lax.broadcasted_iota(jnp.int32, rows.shape, 0)
    columns = jnp.where(row % 8 < 4, first, second).astype(jnp.int32)
    lane = lax.broadcasted_iota(jnp.int32, rows.shape, 1)
    tiles = (columns >> 7) + jnp.where(lane < (columns & (W - 1)), 1, 0)
    for a in range(ANGLES):
        angle = jnp.max(numbers[0, 4 * a : 4 * a + 1, :]).astype(jnp.int32)
        slot = jnp.where(angle >= PAIRS, 2 * (ANGLES - 1 - angle) + 1, 2 * angle)
        at = pl.multiple_of(32 * slot, 32)
        for t in range(4):
            part = jnp.where(tiles[32 * a : 32 * a + 32] == t, rows[32 * a : 32 * a + 32], 0.0)
            part = jnp.sum(part.reshape(4, 8, W), axis=0)
            pieces[pl.ds(at + 8 * t, 8), :] = part + pltpu.roll(part, 4, 0)
    for z in range(8):
        out[z, :PART, :] = total
        out[z, PART:, :] = pieces[pl.ds(z // 2, 32, stride=8), :]


def adjoint_kernel(received, dft_t, leaving, rows_tables, edges, middles, *refs):
    beams, (out, pieces, shifted, sheared) = refs[:PAIRS], refs[PAIRS:]
    block = 2 * lax.axis_index("y") + lax.axis_index("xh")
    even, odd = received[0], received[1]
    for z in range(2, 8, 2):
        even, odd = even + received[z], odd + received[z + 1]
    chunk = jnp.concatenate([even[:PART], odd[:PART]], 0) * (1.0 / 16.0)
    pieces[...] = jnp.where(lax.axis_index("zp") == 0, even[PART:], odd[PART:])
    rows = jnp.concatenate([pieces[pl.ds(t, 8, stride=4), :] for t in range(4)], axis=1)
    spectrum = three(mm, split(rows), (dft_t[0], dft_t[1]))
    weight = jnp.where(lax.broadcasted_iota(jnp.int32, (8, N), 1) % H == 0, 0.5 / N, 1.0 / N)
    cbar = spectrum * weight
    c_mid, s_mid = middles[:ANGLES, :], middles[ANGLES:, :]
    c_reals = cbar[:, :H] * c_mid - cbar[:, H:] * s_mid
    c_imags = cbar[:, H:] * c_mid + cbar[:, :H] * s_mid
    at = pl.ds(pl.multiple_of(64 * block, 64), 64)
    rows_dft = dft_t[0, at, :].astype(F32) + dft_t[1, at, :].astype(F32)
    lane_zero = lax.broadcasted_iota(jnp.int32, (64, H), 1) == 0
    r_cos, r_sin = rows_dft[:, :H], rows_dft[:, H:]
    r_sin_real = jnp.where(lane_zero, 0.0, r_sin)
    r_cos_imag = jnp.where(lane_zero, r_sin, r_cos)
    mirror = jnp.where(lane_zero, 1.0, -1.0)
    nyquist = []
    for slot in range(ANGLES):
        c_real, c_imag = c_reals[slot : slot + 1, :], c_imags[slot : slot + 1, :]
        cosines = c_real * r_cos + c_imag * r_sin_real
        sines = c_imag * r_cos_imag - c_real * r_sin_real
        if slot % 2 == 0:
            sines = sines * mirror
        nyquist.append(sines[:, :1])
        at = slice(64 * slot, 64 * slot + 64)
        shifted[0, at, :H], shifted[1, at, :H] = split(cosines)
        shifted[0, at, H:], shifted[1, at, H:] = split(sines)
    for q in range(PAIRS):
        at = slice(2 * 64 * q, 2 * 64 * (q + 1))
        even = three(mm, (shifted[0, at, :H], shifted[1, at, :H]), (beams[q][0, :H, :], beams[q][1, :H, :]))
        odd = three(mm, (shifted[0, at, H:], shifted[1, at, H:]), (beams[q][0, H:, :], beams[q][1, H:, :]))
        even = even + jnp.concatenate(nyquist[2 * q : 2 * q + 2], 0) * edges[q, 0:1, :]
        sheared[0, at, :H], sheared[1, at, :H] = split(even)
        sheared[0, at, H:], sheared[1, at, H:] = split(odd)
    lane_first = lax.broadcasted_iota(jnp.int32, (8, H), 1) == 0
    sums = [None] * 8
    for q in range(PAIRS):
        at = slice(2 * 64 * q, 2 * 64 * (q + 1))
        real, imag = (
            three(mm, (sheared[0, at, part], sheared[1, at, part]), (dft_t[0, :H, part], dft_t[1, :H, part]))
            for part in (slice(0, H), slice(H, N))
        )
        cb, sb = rows_tables[q, 0, 64:72, :], rows_tables[q, 1, 64:72, :]
        near = rows_tables[q, :, pl.ds(pl.multiple_of(8 * block, 8), 8), :]
        for u in range(8):
            ca, sa = near[0, u : u + 1, :], near[1, u : u + 1, :]
            c, s = ca * cb - sa * sb, sa * cb + ca * sb
            c_first, s_first = jnp.where(lane_first, 1.0, c), jnp.where(lane_first, 0.0, s)
            one, two = slice(8 * u, 8 * u + 8), slice(64 + 8 * u, 72 + 8 * u)
            unturned = jnp.concatenate(
                [
                    (real[one] + real[two]) * c_first + (imag[one] - imag[two]) * s_first,
                    (imag[one] + imag[two]) * c - (real[one] - real[two]) * s_first,
                ],
                1,
            )
            sums[u] = unturned if q == 0 else sums[u] + unturned
    weight = jnp.where(lax.broadcasted_iota(jnp.int32, (64, N), 1) % H == 0, 1.0 / 32.0, 1.0 / 16.0)
    whole = jnp.concatenate(sums, 0) * weight
    columns = three(mm, split(whole), (leaving[0], leaving[1]))
    for part in range(2):
        first, second = (columns[:, (2 * part + i) * W : (2 * part + i + 1) * W] for i in range(2))
        blocks = jnp.concatenate([first, second], 0).T
        for peer in range(8 * part, 8 * part + 8):
            out[peer, :CHUNK, :] = chunk
            a = peer // 2 - 4 * part
            out[peer, CHUNK:, :] = blocks[32 * a : 32 * a + 32, :]


def assemble_kernel(received, out, probe_out, sem):
    move = pltpu.make_async_copy(received.at[:, pl.ds(0, CHUNK), :], probe_out.at[lax.axis_index("core")], sem)
    move.start()
    xl = lax.axis_index("xl")
    lower = lax.broadcasted_iota(jnp.int32, (32, W), 1) < 64
    for b in range(4):
        even = received[4 * b + xl, CHUNK:, :]
        odd = received[4 * b + 2 + xl, CHUNK:, :]
        lanes = slice(b * W, (b + 1) * W)
        out[0, :32, lanes] = jnp.where(lower, even, pltpu.roll(odd, 64, 1))
        out[0, 32:, lanes] = jnp.where(lower, pltpu.roll(even, 64, 1), odd)
    move.wait()


def forward_call(*args):
    return pl.pallas_call(
        forward_kernel,
        in_specs=[pl.BlockSpec(memory_space=pltpu.SMEM)] + [pl.BlockSpec(memory_space=pl.ANY)] * 6,
        out_specs=pl.BlockSpec(memory_space=pltpu.VMEM),
        out_shape=jax.ShapeDtypeStruct((4 * ROWS, W), F32),
        scratch_shapes=[
            pltpu.VMEM((N, N), BF16),
            pltpu.VMEM((2, N, N), BF16),
            pltpu.VMEM((2, H, N), BF16),
            pltpu.VMEM((H // 4 + 24, N), F32),
            pltpu.VMEM((2, N, H), BF16),
            pltpu.VMEM((8, H), F32),
            pltpu.VMEM((N, N), F32),
            pltpu.VMEM((2, N, N), BF16),
            pltpu.VMEM((2, 2, N, H), BF16),
            pltpu.SemaphoreType.DMA((6,)),
        ],
        compiler_params=pltpu.CompilerParams(vmem_limit_bytes=60 * 1024 * 1024),
        cost_estimate=pl.CostEstimate(flops=4 * 10**9, bytes_accessed=4 * 10**6, transcendentals=0),
        name="forward",
    )(*args)


def vmem_call(kernel, outs, scratch, name, *args, far=0):
    result = pl.pallas_call(
        kernel,
        in_specs=[
            pl.BlockSpec(memory_space=pltpu.SMEM if a.dtype == jnp.int32 else pltpu.VMEM) for a in args
        ],
        out_specs=[pl.BlockSpec(memory_space=pltpu.VMEM)] * (len(outs) - far)
        + [pl.BlockSpec(memory_space=pl.ANY)] * far,
        out_shape=[jax.ShapeDtypeStruct(*o) if o[-1] == BF16 else jax.ShapeDtypeStruct(o, F32) for o in outs],
        scratch_shapes=scratch,
        compiler_params=pltpu.CompilerParams(vmem_limit_bytes=32 * 1024 * 1024),
        cost_estimate=pl.CostEstimate(flops=3 * 10**9, bytes_accessed=4 * 10**6, transcendentals=0),
        name=name,
    )(*args)
    return result if len(outs) > 1 else result[0]


Z = ("zq", "zp")
GZ = ("xl", "zq", "zp", "core")
PLANE = ("y", "xh", "xl")


def exchange(blocks, axes):
    return lax.all_to_all(blocks, axes, split_axis=0, concat_axis=0, tiled=True)


def swap(rows):
    return lax.ppermute(rows, "core", [(0, 1), (1, 0)])


def local(volume, probe, measured, angle_index, row_offset, col_offset):
    dft, dft_t, leaving = (jnp.asarray(t) for t in dft_tables())
    dfts = jnp.asarray(window_tables())
    factors, rows_tables, all_beams, edges, middles = (jnp.asarray(t) for t in phase_tables())
    beams = [jnp.asarray(b) for b in phase_tables()[2]]
    row = forward_call(angle_index, volume, dft, dft_t, factors, all_beams, edges)
    whole = exchange(row.reshape(ROWS, 4, W), GZ).reshape(4 * ROWS, W)
    split_modes = pltpu.VMEM((2, MODES // 2, 2 * W, 2 * W), BF16)
    waves, band_dft, band_probe = vmem_call(
        prepare_kernel,
        [(MODES // 2, 2 * W, 2 * W), ((2 * W, 2 * W), BF16), (MODES, 2, ROWS, W)],
        [split_modes],
        "prepare",
        row_offset,
        probe,
        dfts,
    )
    keep, send = vmem_call(
        window_kernel,
        [(HALF + 24, W)] * 2,
        [split_modes, pltpu.VMEM((MODES // 2, 2 * W, 2 * W), F32), pltpu.VMEM((ROWS, W), F32)],
        "window",
        row_offset,
        col_offset,
        whole,
        probe,
        measured,
        dfts,
        waves,
        band_dft,
        band_probe,
    )
    packed = vmem_call(pack_kernel, [(32 * MESSAGE, W)], [], "pack", angle_index, keep, swap(send))
    shared = exchange(packed.reshape(32, MESSAGE, 1, W), PLANE + ("zp",)).reshape(32 * MESSAGE, W)
    scratch = [pltpu.VMEM((256, W), F32), pltpu.VMEM((3, 32, W), F32)]
    relay = vmem_call(relay_kernel, [(8, PART + 32, W)], scratch, "relay", shared)
    rows = exchange(relay, Z)
    blocks = vmem_call(
        adjoint_kernel,
        [(16, CHUNK + 32, W)],
        [pltpu.VMEM((32, W), F32), pltpu.VMEM((2, N, N), BF16), pltpu.VMEM((2, N, N), BF16)],
        "adjoint",
        rows,
        dft_t,
        leaving,
        rows_tables,
        edges,
        middles,
        *beams,
    )
    final = exchange(blocks, PLANE)
    other = swap(final[:, :CHUNK, :])
    volume_update, half = vmem_call(
        assemble_kernel,
        [(1, 64, N), (2, 16, CHUNK, W)],
        [pltpu.SemaphoreType.DMA],
        "assemble",
        final,
        far=1,
    )
    core = lax.axis_index("core")
    probe_update = lax.dynamic_update_slice(half, other[None], (1 - core, 0, 0, 0))
    return volume_update, probe_update.reshape(MODES, 2, W, W)


def solution(mesh):
    split_mesh = Mesh(mesh.devices.reshape(4, 2, 2, 4, 2, 2), ("y", "xh", "xl", "zq", "zp", "core"))
    angle, gz = ("y", "xh"), GZ
    return jax.shard_map(
        local,
        mesh=split_mesh,
        in_specs=(
            P(gz, None, None),
            P(),
            P(angle, gz, None, None),
            P(angle),
            P(angle, gz),
            P(angle, gz),
        ),
        out_specs=(P(gz, angle, None), P()),
        check_vma=False,
    )
```

```python
import math

import jax
import jax.numpy as jnp
import numpy as np
from jax import lax
from jax.experimental import pallas as pl
from jax.experimental.pallas import tpu as pltpu
from jax.sharding import Mesh, PartitionSpec as P

N = 512
H = N // 2
W = 128
MODES = 8
ANGLES = 8
PAIRS = ANGLES // 2
ROWS = 32
HALF = MODES * 2 * W // 2
CHUNK = HALF // 16
PART = CHUNK // 2
MESSAGE = PART + 9
F32 = jnp.float32
BF16 = jnp.bfloat16


def split_const(table):
    high = table.astype(BF16)
    low = (table - high.astype(np.float64)).astype(BF16)
    return np.stack([high, low])


def dft_tables():
    k, n = np.arange(H)[:, None], np.arange(N)[None, :]
    turns = np.pi / N * (k * (2 * n + 1) % (2 * N))
    table = np.concatenate([np.cos(turns), -np.sin(turns)], 0)
    table[H] = 2.0 * (np.arange(N) % 2) - 1.0
    order = np.arange(N).reshape(2, 4, 2, 32).transpose(0, 2, 1, 3).reshape(N)
    return [split_const(np.ascontiguousarray(t)) for t in (table, table.T, table[:, order])]


def window_tables():
    j = np.arange(W)
    turns = 2.0 * np.pi / W * (j[:, None] * j[None, :] % W)
    c, s = np.cos(turns), np.sin(turns)
    return np.stack([split_const(np.block([[c, s], [-s, c]])), split_const(np.block([[c, -s], [s, c]]))])


def shears():
    theta = np.pi * (np.arange(ANGLES) + 0.5) / ANGLES - np.pi / 2
    return -np.tan(theta / 2), np.sin(theta)


def cos_sin(phase):
    return np.stack([np.cos(phase), np.sin(phase)], 1)


def phase_tables():
    shear_x, shear_y = shears()
    cells = np.arange(N) - N / 2
    unit_one = -2.0 * np.pi / N * shear_x
    unit_two = -2.0 * np.pi / N * shear_y[:PAIRS]
    by_y = unit_one[:, None, None] * np.concatenate([cells[:H], cells[:H - 1:-1]])[None, None, :]
    nyquist = np.ones((ANGLES, 8, N))
    nyquist[:, 0] = 0.5 * np.cos(by_y[:, 0] * H)
    factors = np.concatenate(
        [
            cos_sin(by_y * (8 * np.arange(H // 8))[None, :, None]).reshape(ANGLES, H // 4, N),
            cos_sin(by_y * np.arange(8)[None, :, None]).reshape(ANGLES, 16, N),
            nyquist,
        ],
        1,
    )
    freq = np.arange(H, dtype=np.float64)
    freq[0] = H
    by_k = unit_one[:PAIRS, None, None] * freq[None, None, :]
    rows_coarse = cos_sin(by_k * cells[::8][None, :, None])
    rows_fine = cos_sin(by_k * np.arange(8)[None, :, None])
    rows_tables = np.concatenate([rows_coarse, rows_fine], 2)
    frequencies = np.arange(H, dtype=np.float64)
    turns = unit_two[:, None, None] * frequencies[None, :, None] * (H - 0.5 - np.arange(H))[None, None, :]
    low = np.cos(unit_two[:, None] * H * cells[None, :H])
    high = np.cos(unit_two[:, None] * H * cells[None, :H - 1:-1])
    table = np.concatenate([np.cos(turns), np.sin(turns)], 1)
    table[:, H] = 0.5 * (low - high)
    beams = np.ascontiguousarray(np.moveaxis(split_const(table), 0, 1))
    edges = np.zeros((PAIRS, 8, H))
    edges[:, 0] = 0.5 * (low + high)
    middle = 0.5 * unit_two[:, None] * frequencies[None, :]
    ordered = np.stack([middle, -middle], 1).reshape(ANGLES, H)
    middles = np.concatenate([np.cos(ordered), np.sin(ordered)], 0)
    return [t if t.dtype == BF16 else t.astype(np.float32) for t in (factors, rows_tables, beams, edges, middles)]


def mm(a, b):
    return lax.dot_general(a, b, (((1,), (0,)), ((), ())), preferred_element_type=F32)


def mm_t(a, b):
    return lax.dot_general(a, b, (((1,), (1,)), ((), ())), preferred_element_type=F32)


def split(value):
    high = value.astype(BF16)
    return high, (value - high.astype(F32)).astype(BF16)


def three(dot, a, b):
    rows = a[0].shape[0]
    both = dot(jnp.concatenate([a[0], a[1]], 0), b[0])
    return both[:rows] + (both[rows:] + dot(a[0], b[1]))


def forward_kernel(
    sc, volume, dft_hbm, dft_t_hbm, factors_hbm, beams_hbm, edges_hbm, out,
    slab, dft, dft_t, factors, beams, edges, spec, turned, field, sems,
):
    number = sc[0]
    mirrored = number >= PAIRS
    sign = jnp.where(mirrored, -1.0, 1.0)
    folded = jnp.where(mirrored, ANGLES - 1 - number, number)
    copies = [
        (volume.at[0], slab),
        (dft_hbm, dft),
        (factors_hbm.at[number], factors),
        (dft_t_hbm.at[:, pl.ds(0, H), :], dft_t),
        (beams_hbm.at[folded], beams),
        (edges_hbm.at[folded], edges),
    ]
    moves = [pltpu.make_async_copy(source, target, sems.at[i]) for i, (source, target) in enumerate(copies)]
    for move in moves:
        move.start()
    halves = (slice(0, H), slice(H, N))
    rows, lanes = (lax.broadcasted_iota(jnp.int32, (H, H), axis) for axis in (0, 1))
    reverse = jnp.where(rows + lanes == H - 1, 1.0, 0.0).astype(BF16)
    moves[0].wait()
    backward = mm(slab[:, H:], reverse).astype(BF16)
    moves[1].wait()
    moves[2].wait()
    for lanes, columns in zip(halves, (slab[:, :H], backward)):
        both = mm(jnp.concatenate([dft[0], dft[1]], 0), columns)
        spec[:, lanes] = both[:N] + both[N:]
    half_row = jnp.where(lax.broadcasted_iota(jnp.int32, (8, H), 0) == 0, 0.5, 1.0)
    for lanes in halves:
        cb, sb = factors[64:72, lanes], factors[72:80, lanes]
        for pair in range(H // 16):
            reals, imags = [], []
            for u in (2 * pair, 2 * pair + 1):
                ca, sa = factors[u : u + 1, lanes], factors[32 + u : 33 + u, lanes]
                c, s = ca * cb - sa * sb, sa * cb + ca * sb
                a, b = spec[8 * u : 8 * u + 8, lanes], spec[H + 8 * u : H + 8 * u + 8, lanes]
                real, imag = a * c - b * s, a * s + b * c
                if u == 0:
                    real, imag = real * half_row, imag * factors[80:88, lanes]
                reals.append(real)
                imags.append(imag)
            for base, parts in ((16 * pair, reals), (H + 16 * pair, imags)):
                at = slice(base, base + 16)
                turned[0, at, lanes], turned[1, at, lanes] = split(jnp.concatenate(parts, 0))
    moves[3].wait()
    for comps in halves:
        for t in range(2):
            near, far = slice(t * W, (t + 1) * W), slice(H + t * W, H + (t + 1) * W)
            both = three(
                mm,
                (dft_t[0, :, comps], dft_t[1, :, comps]),
                [jnp.concatenate([turned[p, comps, near], turned[p, comps, far]], 1) for p in range(2)],
            )
            field[0, 0, comps, near], field[0, 1, comps, near] = split(both[:, :W] + both[:, W:])
            field[1, 0, comps, near], field[1, 1, comps, near] = split(both[:, :W] - both[:, W:])
    moves[4].wait()
    moves[5].wait()
    c = beams[0, :H, :].astype(F32) + beams[1, :H, :].astype(F32)
    s = beams[0, H:, :].astype(F32) + beams[1, H:, :].astype(F32)
    top = lax.broadcasted_iota(jnp.int32, (8, H), 0) == 0
    c_imag = jnp.concatenate([jnp.where(top, edges[:1, :], c[:8]), c[8:]], 0)
    s_imag = jnp.concatenate([jnp.where(top, 0.0, s[:8]), s[8:]], 0) * sign

    def fold(value):
        return value[:, :W] + value[:, W:]

    def beam(part, rows):
        comps = halves[part]
        return three(mm_t, (dft[0, comps, :H], dft[1, comps, :H]), (field[part, 0, rows], field[part, 1, rows]))

    real = fold(beam(0, halves[0]) * c)
    imag = fold(beam(1, halves[0]) * c_imag)
    odd = beam(1, halves[1])
    real = real + fold(odd * s_imag)
    extra = jnp.where(top[:, :W], fold(odd[:8] * s[:8]), 0.0)
    imag = imag - fold(beam(0, halves[1]) * s_imag)
    imag = jnp.concatenate([imag[:8] + extra, imag[8:]], 0)
    real, imag = jnp.sum(real, axis=1, keepdims=True), jnp.sum(imag, axis=1, keepdims=True)
    weight = jnp.where(lax.broadcasted_iota(jnp.int32, (H, 1), 0) == 0, 0.5, 1.0)
    real, imag = real * weight, imag * weight
    c_mid, s_mid = c[:, H - 1 :], s_imag[:, H - 1 :]
    real, imag = real * c_mid + imag * s_mid, imag * c_mid - real * s_mid
    total = jnp.zeros((8, N), F32)
    for r in range(0, H, 32):
        at, below = slice(r, r + 32), slice(H + r, H + r + 32)
        f_real = dft[0, at, :].astype(F32) + dft[1, at, :].astype(F32)
        f_imag = dft[0, below, :].astype(F32) + dft[1, below, :].astype(F32)
        terms = real[at] * f_real + imag[at] * f_imag
        total = total + jnp.sum(terms.reshape(4, 8, N), axis=0)
    row = jnp.sum(total, axis=0, keepdims=True) * (8.0 / (N * N))
    for t in range(4):
        out[pl.ds(t, ROWS, stride=4), :] = jnp.broadcast_to(row[:, t * W : (t + 1) * W], (ROWS, W))


def turn(block):
    return jnp.concatenate(
        [
            jnp.concatenate([block[:W, :W], block[W:, :W]], 1),
            jnp.concatenate([block[:W, W:], block[W:, W:]], 1),
        ],
        0,
    )


def pairs_of_modes():
    return [(j, j + MODES // 2) for j in range(MODES // 2)]


def prepare_kernel(row_ref, probe, dfts, waves, band_dft, band_probe, stage):
    start = -row_ref[0, 0]
    lefts, rights = (dfts[0, 0], dfts[0, 1]), (dfts[1, 0], dfts[1, 1])
    for j, pair in enumerate(pairs_of_modes()):
        reals = jnp.concatenate([probe[m, 0] for m in pair], 1)
        imags = jnp.concatenate([probe[m, 1] for m in pair], 1)
        stage[0, j], stage[1, j] = split(jnp.concatenate([reals, imags], 0))
    for j in range(MODES // 2):
        stage[0, j], stage[1, j] = split(turn(three(mm, lefts, (stage[0, j], stage[1, j]))))
    for j in range(MODES // 2):
        waves[j] = three(mm, (stage[0, j], stage[1, j]), rights)
    source = lax.broadcasted_iota(jnp.int32, (2 * W, 2 * W), 0)
    target = lax.broadcasted_iota(jnp.int32, (2 * W, 2 * W), 1)
    wanted = start + (target & (ROWS - 1)) + jnp.where(target & ROWS != 0, W, 0)
    chosen = jnp.where(source == wanted, 1.0, 0.0)
    first = jnp.where(target < 4 * ROWS, chosen, 0.0).astype(BF16)
    second = jnp.where((target >= 4 * ROWS) & (target < 6 * ROWS), chosen, 0.0).astype(BF16)
    band_dft[...] = (mm(lefts[0], first) + mm(lefts[1], second)).astype(BF16)
    for m in range(MODES):
        for part in range(2):
            band_probe[m, part] = probe[m, part, pl.ds(start, ROWS), :]


def window_kernel(
    row_ref, col_ref, whole, probe, measured, dfts, waves, band_dft, band_probe, keep, send, stage, far, pieces
):
    row, col, core = row_ref[0, 0], col_ref[0, 0], lax.axis_index("core")
    rows = jnp.concatenate([whole[pl.ds(t, ROWS, stride=4), :] for t in range(4)], axis=1)
    band = pltpu.roll(rows, lax.rem(N - col, N), 1)[:, :W]
    band_real, band_imag = jnp.cos(band) - 1.0, jnp.sin(band)
    lefts, rights = (dfts[0, 0], dfts[0, 1]), (dfts[1, 0], dfts[1, 1])
    pairs = pairs_of_modes()
    sides = (slice(0, W), slice(W, 2 * W))

    def put(j, value):
        stage[0, j], stage[1, j] = split(value)

    def get(j):
        return stage[0, j], stage[1, j]

    lines = []
    for m in [m for pair in pairs for m in pair]:
        p_real, p_imag = band_probe[m, 0], band_probe[m, 1]
        lines.append(
            jnp.concatenate(
                [p_real * band_real - p_imag * band_imag, p_real * band_imag + p_imag * band_real], 1
            )
        )
    lines = three(mm, split(jnp.concatenate(lines, 0)), rights)
    intensity = jnp.zeros((W, W), F32)
    for j in range(MODES // 2):
        one, two = (lines[2 * ROWS * j + ROWS * i : 2 * ROWS * j + ROWS * (i + 1)] for i in range(2))
        both = jnp.concatenate(
            [jnp.concatenate([one[:, :W], two[:, :W]], 1), jnp.concatenate([one[:, W:], two[:, W:]], 1)], 0
        )
        high, low = split(both)
        blank = jnp.zeros((2 * ROWS, 2 * W), BF16)
        total = waves[j] + turn(mm(band_dft[...], jnp.concatenate([high, low, high, blank], 0)))
        far[j] = total
        power = total * total
        power = power[:W] + power[W:]
        intensity = intensity + (power[:, :W] + power[:, W:])
    pad = jnp.zeros((W - ROWS, W), F32)
    obj_real = pltpu.roll(jnp.concatenate([band_real, pad], 0), -row, 0) + 1.0
    obj_imag = pltpu.roll(jnp.concatenate([band_imag, pad], 0), -row, 0)
    factor = (1.0 - jnp.sqrt(measured[0, 0] + 1.0) / jnp.sqrt(intensity + 1.0)) * (1.0 / W)
    factors = jnp.concatenate([jnp.concatenate([factor, factor], 1)] * 2, 0)
    for j in range(MODES // 2):
        put(j, far[j] * factors)
    for j in range(MODES // 2):
        put(j, turn(three(mm, get(j), lefts)))
    grad_real, grad_imag = jnp.zeros((W, W), F32), jnp.zeros((W, W), F32)
    for j, pair in enumerate(pairs):
        back = three(mm, rights, get(j))
        grads = []
        for m, lanes in zip(pair, sides):
            b_real, b_imag = back[:W, lanes], back[W:, lanes]
            p_real, p_imag = probe[m, 0], probe[m, 1]
            grad_real = grad_real + (p_real * b_real + p_imag * b_imag)
            grad_imag = grad_imag + (p_real * b_imag - p_imag * b_real)
            grads.append((obj_real * b_real + obj_imag * b_imag, obj_real * b_imag - obj_imag * b_real))
        for part in range(2):
            at = slice((2 * j + part) * W, (2 * j + part + 1) * W)
            keep[at, :] = jnp.where(core == 0, grads[0][part], grads[1][part])
            send[at, :] = jnp.where(core == 0, grads[1][part], grads[0][part])
    patch = grad_imag * obj_real - grad_real * obj_imag
    shown = pltpu.roll(patch, W + row, 0)[:ROWS]
    pieces[...] = pltpu.roll(shown, lax.rem(col, W), 1)
    even, odd = pieces[pl.ds(0, 16, stride=2), :], pieces[pl.ds(1, 16, stride=2), :]
    keep[HALF : HALF + 16, :] = jnp.where(core == 0, even, odd)
    send[HALF : HALF + 16, :] = jnp.where(core == 0, odd, even)
    column = jnp.full((8, W), col, jnp.int32).astype(F32)
    keep[HALF + 16 :, :] = column
    send[HALF + 16 :, :] = column


def pack_kernel(sc, keep, other, out):
    lane = lax.broadcasted_iota(jnp.int32, (1, W), 1)
    first, second = keep[HALF + 16 : HALF + 17, :], other[HALF + 16 : HALF + 17, :]
    numbers = jnp.where(lane < 32, sc[0].astype(F32), jnp.where(lane < 64, first, second))
    for peer in range(32):
        rows = slice(PART * peer, PART * (peer + 1))
        at = MESSAGE * peer
        out[at : at + PART, :] = keep[rows, :] + other[rows, :]
        rows = pl.ds(HALF + 8 * (peer // 2 % 2) + peer % 2, 4, stride=2)
        out[at + PART : at + PART + 4, :] = keep[rows, :]
        out[at + PART + 4 : at + PART + 8, :] = other[rows, :]
        out[at + PART + 8 : at + MESSAGE, :] = numbers


def relay_kernel(received, out, pieces, numbers):
    total = received[:PART, :]
    for peer in range(1, 32):
        total = total + received[MESSAGE * peer : MESSAGE * peer + PART, :]
    heads = jnp.concatenate([received[pl.ds(MESSAGE * p + MESSAGE - 1, 1), :] for p in range(32)], 0)
    rolls = [heads] + [pltpu.roll(heads, 32 * i, 1) for i in (1, 2, 3)]
    quarter = lax.broadcasted_iota(jnp.int32, (32, W), 1) // 32
    for i in range(3):
        value = rolls[0]
        for shift in (1, 2, 3):
            value = jnp.where(quarter == (i + shift) % 4, rolls[shift], value)
        numbers[i] = value
    rows = jnp.concatenate([received[MESSAGE * p + PART : MESSAGE * p + PART + 8, :] for p in range(32)], 0)
    first, second = (
        jnp.concatenate([jnp.broadcast_to(numbers[1 + i, p : p + 1, :], (8, W)) for p in range(32)], 0)
        for i in range(2)
    )
    row = lax.broadcasted_iota(jnp.int32, rows.shape, 0)
    columns = jnp.where(row % 8 < 4, first, second).astype(jnp.int32)
    lane = lax.broadcasted_iota(jnp.int32, rows.shape, 1)
    tiles = (columns >> 7) + jnp.where(lane < (columns & (W - 1)), 1, 0)
    for a in range(ANGLES):
        angle = jnp.max(numbers[0, 4 * a : 4 * a + 1, :]).astype(jnp.int32)
        slot = jnp.where(angle >= PAIRS, 2 * (ANGLES - 1 - angle) + 1, 2 * angle)
        at = pl.multiple_of(32 * slot, 32)
        for t in range(4):
            part = jnp.where(tiles[32 * a : 32 * a + 32] == t, rows[32 * a : 32 * a + 32], 0.0)
            part = jnp.sum(part.reshape(4, 8, W), axis=0)
            pieces[pl.ds(at + 8 * t, 8), :] = part + pltpu.roll(part, 4, 0)
    for z in range(8):
        out[z, :PART, :] = total
        out[z, PART:, :] = pieces[pl.ds(z % 4, 32, stride=8), :]


def adjoint_kernel(received, dft_t, leaving, rows_tables, edges, middles, *refs):
    beams, (out, pieces, shifted, sheared) = refs[:PAIRS], refs[PAIRS:]
    block = 2 * lax.axis_index("y") + lax.axis_index("xh")
    even, odd = received[0], received[4]
    for z in range(1, 4):
        even, odd = even + received[z], odd + received[4 + z]
    chunk = jnp.concatenate([even[:PART], odd[:PART]], 0) * (1.0 / 16.0)
    pieces[...] = jnp.where(lax.axis_index("zp") == 0, even[PART:], odd[PART:])
    rows = jnp.concatenate([pieces[pl.ds(t, 8, stride=4), :] for t in range(4)], axis=1)
    spectrum = three(mm, split(rows), (dft_t[0], dft_t[1]))
    weight = jnp.where(lax.broadcasted_iota(jnp.int32, (8, N), 1) % H == 0, 0.5 / N, 1.0 / N)
    cbar = spectrum * weight
    c_mid, s_mid = middles[:ANGLES, :], middles[ANGLES:, :]
    c_reals = cbar[:, :H] * c_mid - cbar[:, H:] * s_mid
    c_imags = cbar[:, H:] * c_mid + cbar[:, :H] * s_mid
    at = pl.ds(pl.multiple_of(64 * block, 64), 64)
    rows_dft = dft_t[0, at, :].astype(F32) + dft_t[1, at, :].astype(F32)
    lane_zero = lax.broadcasted_iota(jnp.int32, (64, H), 1) == 0
    r_cos, r_sin = rows_dft[:, :H], rows_dft[:, H:]
    r_sin_real = jnp.where(lane_zero, 0.0, r_sin)
    r_cos_imag = jnp.where(lane_zero, r_sin, r_cos)
    mirror = jnp.where(lane_zero, 1.0, -1.0)
    nyquist = []
    for slot in range(ANGLES):
        c_real, c_imag = c_reals[slot : slot + 1, :], c_imags[slot : slot + 1, :]
        cosines = c_real * r_cos + c_imag * r_sin_real
        sines = c_imag * r_cos_imag - c_real * r_sin_real
        if slot % 2 == 0:
            sines = sines * mirror
        nyquist.append(sines[:, :1])
        at = slice(64 * slot, 64 * slot + 64)
        shifted[0, at, :H], shifted[1, at, :H] = split(cosines)
        shifted[0, at, H:], shifted[1, at, H:] = split(sines)
    for q in range(PAIRS):
        at = slice(2 * 64 * q, 2 * 64 * (q + 1))
        even = three(mm, (shifted[0, at, :H], shifted[1, at, :H]), (beams[q][0, :H, :], beams[q][1, :H, :]))
        odd = three(mm, (shifted[0, at, H:], shifted[1, at, H:]), (beams[q][0, H:, :], beams[q][1, H:, :]))
        even = even + jnp.concatenate(nyquist[2 * q : 2 * q + 2], 0) * edges[q, 0:1, :]
        sheared[0, at, :H], sheared[1, at, :H] = split(even)
        sheared[0, at, H:], sheared[1, at, H:] = split(odd)
    lane_first = lax.broadcasted_iota(jnp.int32, (8, H), 1) == 0
    sums = [None] * 8
    for q in range(PAIRS):
        at = slice(2 * 64 * q, 2 * 64 * (q + 1))
        real, imag = (
            three(mm, (sheared[0, at, part], sheared[1, at, part]), (dft_t[0, :H, part], dft_t[1, :H, part]))
            for part in (slice(0, H), slice(H, N))
        )
        cb, sb = rows_tables[q, 0, 64:72, :], rows_tables[q, 1, 64:72, :]
        near = rows_tables[q, :, pl.ds(pl.multiple_of(8 * block, 8), 8), :]
        for u in range(8):
            ca, sa = near[0, u : u + 1, :], near[1, u : u + 1, :]
            c, s = ca * cb - sa * sb, sa * cb + ca * sb
            c_first, s_first = jnp.where(lane_first, 1.0, c), jnp.where(lane_first, 0.0, s)
            one, two = slice(8 * u, 8 * u + 8), slice(64 + 8 * u, 72 + 8 * u)
            unturned = jnp.concatenate(
                [
                    (real[one] + real[two]) * c_first + (imag[one] - imag[two]) * s_first,
                    (imag[one] + imag[two]) * c - (real[one] - real[two]) * s_first,
                ],
                1,
            )
            sums[u] = unturned if q == 0 else sums[u] + unturned
    weight = jnp.where(lax.broadcasted_iota(jnp.int32, (64, N), 1) % H == 0, 1.0 / 32.0, 1.0 / 16.0)
    whole = jnp.concatenate(sums, 0) * weight
    columns = three(mm, split(whole), (leaving[0], leaving[1]))
    for part in range(2):
        first, second = (columns[:, (2 * part + i) * W : (2 * part + i + 1) * W] for i in range(2))
        blocks = jnp.concatenate([first, second], 0).T
        for peer in range(8 * part, 8 * part + 8):
            out[peer, :CHUNK, :] = chunk
            a = peer // 2 - 4 * part
            out[peer, CHUNK:, :] = blocks[32 * a : 32 * a + 32, :]


def assemble_kernel(received, out, probe_out, sem):
    move = pltpu.make_async_copy(received.at[:, pl.ds(0, CHUNK), :], probe_out.at[lax.axis_index("core")], sem)
    move.start()
    xl = lax.axis_index("xl")
    lower = lax.broadcasted_iota(jnp.int32, (32, W), 1) < 64
    for b in range(4):
        even = received[4 * b + xl, CHUNK:, :]
        odd = received[4 * b + 2 + xl, CHUNK:, :]
        lanes = slice(b * W, (b + 1) * W)
        out[0, :32, lanes] = jnp.where(lower, even, pltpu.roll(odd, 64, 1))
        out[0, 32:, lanes] = jnp.where(lower, pltpu.roll(even, 64, 1), odd)
    move.wait()


def forward_call(*args):
    return pl.pallas_call(
        forward_kernel,
        in_specs=[pl.BlockSpec(memory_space=pltpu.SMEM)] + [pl.BlockSpec(memory_space=pl.ANY)] * 6,
        out_specs=pl.BlockSpec(memory_space=pltpu.VMEM),
        out_shape=jax.ShapeDtypeStruct((4 * ROWS, W), F32),
        scratch_shapes=[
            pltpu.VMEM((N, N), BF16),
            pltpu.VMEM((2, N, N), BF16),
            pltpu.VMEM((2, H, N), BF16),
            pltpu.VMEM((H // 4 + 24, N), F32),
            pltpu.VMEM((2, N, H), BF16),
            pltpu.VMEM((8, H), F32),
            pltpu.VMEM((N, N), F32),
            pltpu.VMEM((2, N, N), BF16),
            pltpu.VMEM((2, 2, N, H), BF16),
            pltpu.SemaphoreType.DMA((6,)),
        ],
        compiler_params=pltpu.CompilerParams(vmem_limit_bytes=60 * 1024 * 1024),
        cost_estimate=pl.CostEstimate(flops=4 * 10**9, bytes_accessed=4 * 10**6, transcendentals=0),
        name="forward",
    )(*args)


def vmem_call(kernel, outs, scratch, name, *args, far=0):
    result = pl.pallas_call(
        kernel,
        in_specs=[
            pl.BlockSpec(memory_space=pltpu.SMEM if a.dtype == jnp.int32 else pltpu.VMEM) for a in args
        ],
        out_specs=[pl.BlockSpec(memory_space=pltpu.VMEM)] * (len(outs) - far)
        + [pl.BlockSpec(memory_space=pl.ANY)] * far,
        out_shape=[jax.ShapeDtypeStruct(*o) if o[-1] == BF16 else jax.ShapeDtypeStruct(o, F32) for o in outs],
        scratch_shapes=scratch,
        compiler_params=pltpu.CompilerParams(vmem_limit_bytes=32 * 1024 * 1024),
        cost_estimate=pl.CostEstimate(flops=3 * 10**9, bytes_accessed=4 * 10**6, transcendentals=0),
        name=name,
    )(*args)
    return result if len(outs) > 1 else result[0]


Z = ("zp", "zq")
GZ = ("xl", "zq", "zp", "core")
PLANE = ("y", "xh", "xl")


def exchange(blocks, axes):
    return lax.all_to_all(blocks, axes, split_axis=0, concat_axis=0, tiled=True)


def swap(rows):
    return lax.ppermute(rows, "core", [(0, 1), (1, 0)])


def local(volume, probe, measured, angle_index, row_offset, col_offset):
    dft, dft_t, leaving = (jnp.asarray(t) for t in dft_tables())
    dfts = jnp.asarray(window_tables())
    factors, rows_tables, all_beams, edges, middles = (jnp.asarray(t) for t in phase_tables())
    beams = [jnp.asarray(b) for b in phase_tables()[2]]
    row = forward_call(angle_index, volume, dft, dft_t, factors, all_beams, edges)
    whole = exchange(row.reshape(ROWS, 4, W), GZ).reshape(4 * ROWS, W)
    split_modes = pltpu.VMEM((2, MODES // 2, 2 * W, 2 * W), BF16)
    waves, band_dft, band_probe = vmem_call(
        prepare_kernel,
        [(MODES // 2, 2 * W, 2 * W), ((2 * W, 2 * W), BF16), (MODES, 2, ROWS, W)],
        [split_modes],
        "prepare",
        row_offset,
        probe,
        dfts,
    )
    keep, send = vmem_call(
        window_kernel,
        [(HALF + 24, W)] * 2,
        [split_modes, pltpu.VMEM((MODES // 2, 2 * W, 2 * W), F32), pltpu.VMEM((ROWS, W), F32)],
        "window",
        row_offset,
        col_offset,
        whole,
        probe,
        measured,
        dfts,
        waves,
        band_dft,
        band_probe,
    )
    packed = vmem_call(pack_kernel, [(32 * MESSAGE, W)], [], "pack", angle_index, keep, swap(send))
    shared = exchange(packed.reshape(32, MESSAGE, 1, W), PLANE + ("zp",)).reshape(32 * MESSAGE, W)
    scratch = [pltpu.VMEM((256, W), F32), pltpu.VMEM((3, 32, W), F32)]
    relay = vmem_call(relay_kernel, [(8, PART + 32, W)], scratch, "relay", shared)
    rows = exchange(relay, Z)
    blocks = vmem_call(
        adjoint_kernel,
        [(16, CHUNK + 32, W)],
        [pltpu.VMEM((32, W), F32), pltpu.VMEM((2, N, N), BF16), pltpu.VMEM((2, N, N), BF16)],
        "adjoint",
        rows,
        dft_t,
        leaving,
        rows_tables,
        edges,
        middles,
        *beams,
    )
    final = exchange(blocks, PLANE)
    other = swap(final[:, :CHUNK, :])
    volume_update, half = vmem_call(
        assemble_kernel,
        [(1, 64, N), (2, 16, CHUNK, W)],
        [pltpu.SemaphoreType.DMA],
        "assemble",
        final,
        far=1,
    )
    core = lax.axis_index("core")
    probe_update = lax.dynamic_update_slice(half, other[None], (1 - core, 0, 0, 0))
    return volume_update, probe_update.reshape(MODES, 2, W, W)


def solution(mesh):
    split_mesh = Mesh(mesh.devices.reshape(4, 2, 2, 4, 2, 2), ("y", "xh", "xl", "zq", "zp", "core"))
    angle, gz = ("y", "xh"), GZ
    return jax.shard_map(
        local,
        mesh=split_mesh,
        in_specs=(
            P(gz, None, None),
            P(),
            P(angle, gz, None, None),
            P(angle),
            P(angle, gz),
            P(angle, gz),
        ),
        out_specs=(P(gz, angle, None), P()),
        check_vma=False,
    )
```

```python
import math

import jax
import jax.numpy as jnp
import numpy as np
from jax import lax
from jax.experimental import pallas as pl
from jax.experimental.pallas import tpu as pltpu
from jax.sharding import Mesh, PartitionSpec as P

N = 512
H = N // 2
W = 128
MODES = 8
ANGLES = 8
PAIRS = ANGLES // 2
ROWS = 32
HALF = MODES * 2 * W // 2
CHUNK = HALF // 16
PART = CHUNK // 2
MESSAGE = PART + 9
F32 = jnp.float32
BF16 = jnp.bfloat16


def split_const(table):
    high = table.astype(BF16)
    low = (table - high.astype(np.float64)).astype(BF16)
    return np.stack([high, low])


def dft_tables():
    k, n = np.arange(H)[:, None], np.arange(N)[None, :]
    turns = np.pi / N * (k * (2 * n + 1) % (2 * N))
    table = np.concatenate([np.cos(turns), -np.sin(turns)], 0)
    table[H] = 2.0 * (np.arange(N) % 2) - 1.0
    order = np.arange(N).reshape(2, 4, 2, 32).transpose(0, 2, 1, 3).reshape(N)
    return [split_const(np.ascontiguousarray(t)) for t in (table, table.T, table[:, order])]


def window_tables():
    j = np.arange(W)
    turns = 2.0 * np.pi / W * (j[:, None] * j[None, :] % W)
    c, s = np.cos(turns), np.sin(turns)
    return np.stack([split_const(np.block([[c, s], [-s, c]])), split_const(np.block([[c, -s], [s, c]]))])


def shears():
    theta = np.pi * (np.arange(ANGLES) + 0.5) / ANGLES - np.pi / 2
    return -np.tan(theta / 2), np.sin(theta)


def cos_sin(phase):
    return np.stack([np.cos(phase), np.sin(phase)], 1)


def phase_tables():
    shear_x, shear_y = shears()
    cells = np.arange(N) - N / 2
    unit_one = -2.0 * np.pi / N * shear_x
    unit_two = -2.0 * np.pi / N * shear_y[:PAIRS]
    by_y = unit_one[:, None, None] * np.concatenate([cells[:H], cells[:H - 1:-1]])[None, None, :]
    nyquist = np.ones((ANGLES, 8, N))
    nyquist[:, 0] = 0.5 * np.cos(by_y[:, 0] * H)
    factors = np.concatenate(
        [
            cos_sin(by_y * (8 * np.arange(H // 8))[None, :, None]).reshape(ANGLES, H // 4, N),
            cos_sin(by_y * np.arange(8)[None, :, None]).reshape(ANGLES, 16, N),
            nyquist,
        ],
        1,
    )
    freq = np.arange(H, dtype=np.float64)
    freq[0] = H
    by_k = unit_one[:PAIRS, None, None] * freq[None, None, :]
    rows_coarse = cos_sin(by_k * cells[::8][None, :, None])
    rows_fine = cos_sin(by_k * np.arange(8)[None, :, None])
    rows_tables = np.concatenate([rows_coarse, rows_fine], 2)
    frequencies = np.arange(H, dtype=np.float64)
    turns = unit_two[:, None, None] * frequencies[None, :, None] * (H - 0.5 - np.arange(H))[None, None, :]
    low = np.cos(unit_two[:, None] * H * cells[None, :H])
    high = np.cos(unit_two[:, None] * H * cells[None, :H - 1:-1])
    table = np.concatenate([np.cos(turns), np.sin(turns)], 1)
    table[:, H] = 0.5 * (low - high)
    beams = np.ascontiguousarray(np.moveaxis(split_const(table), 0, 1))
    edges = np.zeros((PAIRS, 8, H))
    edges[:, 0] = 0.5 * (low + high)
    middle = 0.5 * unit_two[:, None] * frequencies[None, :]
    ordered = np.stack([middle, -middle], 1).reshape(ANGLES, H)
    middles = np.concatenate([np.cos(ordered), np.sin(ordered)], 0)
    return [t if t.dtype == BF16 else t.astype(np.float32) for t in (factors, rows_tables, beams, edges, middles)]


def mm(a, b):
    return lax.dot_general(a, b, (((1,), (0,)), ((), ())), preferred_element_type=F32)


def mm_t(a, b):
    return lax.dot_general(a, b, (((1,), (1,)), ((), ())), preferred_element_type=F32)


def split(value):
    high = value.astype(BF16)
    return high, (value - high.astype(F32)).astype(BF16)


def three(dot, a, b):
    rows = a[0].shape[0]
    both = dot(jnp.concatenate([a[0], a[1]], 0), b[0])
    return both[:rows] + (both[rows:] + dot(a[0], b[1]))


def forward_kernel(
    sc, volume, dft_hbm, dft_t_hbm, factors_hbm, beams_hbm, edges_hbm, out,
    slab, dft, dft_t, factors, beams, edges, spec, turned, field, sems,
):
    number = sc[0]
    mirrored = number >= PAIRS
    sign = jnp.where(mirrored, -1.0, 1.0)
    folded = jnp.where(mirrored, ANGLES - 1 - number, number)
    copies = [
        (volume.at[0], slab),
        (dft_hbm, dft),
        (factors_hbm.at[number], factors),
        (dft_t_hbm.at[:, pl.ds(0, H), :], dft_t),
        (beams_hbm.at[folded], beams),
        (edges_hbm.at[folded], edges),
    ]
    moves = [pltpu.make_async_copy(source, target, sems.at[i]) for i, (source, target) in enumerate(copies)]
    for move in moves:
        move.start()
    halves = (slice(0, H), slice(H, N))
    rows, lanes = (lax.broadcasted_iota(jnp.int32, (H, H), axis) for axis in (0, 1))
    reverse = jnp.where(rows + lanes == H - 1, 1.0, 0.0).astype(BF16)
    moves[0].wait()
    backward = mm(slab[:, H:], reverse).astype(BF16)
    moves[1].wait()
    moves[2].wait()
    for lanes, columns in zip(halves, (slab[:, :H], backward)):
        both = mm(jnp.concatenate([dft[0], dft[1]], 0), columns)
        spec[:, lanes] = both[:N] + both[N:]
    half_row = jnp.where(lax.broadcasted_iota(jnp.int32, (8, H), 0) == 0, 0.5, 1.0)
    for lanes in halves:
        cb, sb = factors[64:72, lanes], factors[72:80, lanes]
        for pair in range(H // 16):
            reals, imags = [], []
            for u in (2 * pair, 2 * pair + 1):
                ca, sa = factors[u : u + 1, lanes], factors[32 + u : 33 + u, lanes]
                c, s = ca * cb - sa * sb, sa * cb + ca * sb
                a, b = spec[8 * u : 8 * u + 8, lanes], spec[H + 8 * u : H + 8 * u + 8, lanes]
                real, imag = a * c - b * s, a * s + b * c
                if u == 0:
                    real, imag = real * half_row, imag * factors[80:88, lanes]
                reals.append(real)
                imags.append(imag)
            for base, parts in ((16 * pair, reals), (H + 16 * pair, imags)):
                at = slice(base, base + 16)
                turned[0, at, lanes], turned[1, at, lanes] = split(jnp.concatenate(parts, 0))
    moves[3].wait()
    for comps in halves:
        for t in range(2):
            near, far = slice(t * W, (t + 1) * W), slice(H + t * W, H + (t + 1) * W)
            both = three(
                mm,
                (dft_t[0, :, comps], dft_t[1, :, comps]),
                [jnp.concatenate([turned[p, comps, near], turned[p, comps, far]], 1) for p in range(2)],
            )
            field[0, 0, comps, near], field[0, 1, comps, near] = split(both[:, :W] + both[:, W:])
            field[1, 0, comps, near], field[1, 1, comps, near] = split(both[:, :W] - both[:, W:])
    moves[4].wait()
    moves[5].wait()
    c = beams[0, :H, :].astype(F32) + beams[1, :H, :].astype(F32)
    s = beams[0, H:, :].astype(F32) + beams[1, H:, :].astype(F32)
    top = lax.broadcasted_iota(jnp.int32, (8, H), 0) == 0
    c_imag = jnp.concatenate([jnp.where(top, edges[:1, :], c[:8]), c[8:]], 0)
    s_imag = jnp.concatenate([jnp.where(top, 0.0, s[:8]), s[8:]], 0) * sign

    def fold(value):
        return value[:, :W] + value[:, W:]

    def beam(part, rows):
        comps = halves[part]
        return three(mm_t, (dft[0, comps, :H], dft[1, comps, :H]), (field[part, 0, rows], field[part, 1, rows]))

    real = fold(beam(0, halves[0]) * c)
    imag = fold(beam(1, halves[0]) * c_imag)
    odd = beam(1, halves[1])
    real = real + fold(odd * s_imag)
    extra = jnp.where(top[:, :W], fold(odd[:8] * s[:8]), 0.0)
    imag = imag - fold(beam(0, halves[1]) * s_imag)
    imag = jnp.concatenate([imag[:8] + extra, imag[8:]], 0)
    real, imag = jnp.sum(real, axis=1, keepdims=True), jnp.sum(imag, axis=1, keepdims=True)
    weight = jnp.where(lax.broadcasted_iota(jnp.int32, (H, 1), 0) == 0, 0.5, 1.0)
    real, imag = real * weight, imag * weight
    c_mid, s_mid = c[:, H - 1 :], s_imag[:, H - 1 :]
    real, imag = real * c_mid + imag * s_mid, imag * c_mid - real * s_mid
    total = jnp.zeros((8, N), F32)
    for r in range(0, H, 32):
        at, below = slice(r, r + 32), slice(H + r, H + r + 32)
        f_real = dft[0, at, :].astype(F32) + dft[1, at, :].astype(F32)
        f_imag = dft[0, below, :].astype(F32) + dft[1, below, :].astype(F32)
        terms = real[at] * f_real + imag[at] * f_imag
        total = total + jnp.sum(terms.reshape(4, 8, N), axis=0)
    row = jnp.sum(total, axis=0, keepdims=True) * (8.0 / (N * N))
    for t in range(4):
        out[pl.ds(t, ROWS, stride=4), :] = jnp.broadcast_to(row[:, t * W : (t + 1) * W], (ROWS, W))


def turn(block):
    return jnp.concatenate(
        [
            jnp.concatenate([block[:W, :W], block[W:, :W]], 1),
            jnp.concatenate([block[:W, W:], block[W:, W:]], 1),
        ],
        0,
    )


def pairs_of_modes():
    return [(j, j + MODES // 2) for j in range(MODES // 2)]


def prepare_kernel(row_ref, probe, dfts, waves, band_dft, band_probe, stage):
    start = -row_ref[0, 0]
    lefts, rights = (dfts[0, 0], dfts[0, 1]), (dfts[1, 0], dfts[1, 1])
    for j, pair in enumerate(pairs_of_modes()):
        reals = jnp.concatenate([probe[m, 0] for m in pair], 1)
        imags = jnp.concatenate([probe[m, 1] for m in pair], 1)
        stage[0, j], stage[1, j] = split(jnp.concatenate([reals, imags], 0))
    for j in range(MODES // 2):
        stage[0, j], stage[1, j] = split(turn(three(mm, lefts, (stage[0, j], stage[1, j]))))
    for j in range(MODES // 2):
        waves[j] = three(mm, (stage[0, j], stage[1, j]), rights)
    source = lax.broadcasted_iota(jnp.int32, (2 * W, 2 * W), 0)
    target = lax.broadcasted_iota(jnp.int32, (2 * W, 2 * W), 1)
    wanted = start + (target & (ROWS - 1)) + jnp.where(target & ROWS != 0, W, 0)
    chosen = jnp.where(source == wanted, 1.0, 0.0)
    first = jnp.where(target < 4 * ROWS, chosen, 0.0).astype(BF16)
    second = jnp.where((target >= 4 * ROWS) & (target < 6 * ROWS), chosen, 0.0).astype(BF16)
    band_dft[...] = (mm(lefts[0], first) + mm(lefts[1], second)).astype(BF16)
    for m in range(MODES):
        for part in range(2):
            band_probe[m, part] = probe[m, part, pl.ds(start, ROWS), :]


def window_kernel(
    row_ref, col_ref, whole, probe, measured, dfts, waves, band_dft, band_probe, keep, send, stage, far, pieces
):
    row, col, core = row_ref[0, 0], col_ref[0, 0], lax.axis_index("core")
    rows = jnp.concatenate([whole[pl.ds(t, ROWS, stride=4), :] for t in range(4)], axis=1)
    band = pltpu.roll(rows, lax.rem(N - col, N), 1)[:, :W]
    band_real, band_imag = jnp.cos(band) - 1.0, jnp.sin(band)
    lefts, rights = (dfts[0, 0], dfts[0, 1]), (dfts[1, 0], dfts[1, 1])
    pairs = pairs_of_modes()
    sides = (slice(0, W), slice(W, 2 * W))

    def put(j, value):
        stage[0, j], stage[1, j] = split(value)

    def get(j):
        return stage[0, j], stage[1, j]

    lines = []
    for m in [m for pair in pairs for m in pair]:
        p_real, p_imag = band_probe[m, 0], band_probe[m, 1]
        lines.append(
            jnp.concatenate(
                [p_real * band_real - p_imag * band_imag, p_real * band_imag + p_imag * band_real], 1
            )
        )
    lines = three(mm, split(jnp.concatenate(lines, 0)), rights)
    intensity = jnp.zeros((W, W), F32)
    for j in range(MODES // 2):
        one, two = (lines[2 * ROWS * j + ROWS * i : 2 * ROWS * j + ROWS * (i + 1)] for i in range(2))
        both = jnp.concatenate(
            [jnp.concatenate([one[:, :W], two[:, :W]], 1), jnp.concatenate([one[:, W:], two[:, W:]], 1)], 0
        )
        high, low = split(both)
        blank = jnp.zeros((2 * ROWS, 2 * W), BF16)
        total = waves[j] + turn(mm(band_dft[...], jnp.concatenate([high, low, high, blank], 0)))
        far[j] = total
        power = total * total
        power = power[:W] + power[W:]
        intensity = intensity + (power[:, :W] + power[:, W:])
    pad = jnp.zeros((W - ROWS, W), F32)
    obj_real = pltpu.roll(jnp.concatenate([band_real, pad], 0), -row, 0) + 1.0
    obj_imag = pltpu.roll(jnp.concatenate([band_imag, pad], 0), -row, 0)
    factor = (1.0 - jnp.sqrt(measured[0, 0] + 1.0) / jnp.sqrt(intensity + 1.0)) * (1.0 / W)
    factors = jnp.concatenate([jnp.concatenate([factor, factor], 1)] * 2, 0)
    for j in range(MODES // 2):
        put(j, far[j] * factors)
    for j in range(MODES // 2):
        put(j, turn(three(mm, get(j), lefts)))
    grad_real, grad_imag = jnp.zeros((W, W), F32), jnp.zeros((W, W), F32)
    for j, pair in enumerate(pairs):
        back = three(mm, rights, get(j))
        grads = []
        for m, lanes in zip(pair, sides):
            b_real, b_imag = back[:W, lanes], back[W:, lanes]
            p_real, p_imag = probe[m, 0], probe[m, 1]
            grad_real = grad_real + (p_real * b_real + p_imag * b_imag)
            grad_imag = grad_imag + (p_real * b_imag - p_imag * b_real)
            grads.append((obj_real * b_real + obj_imag * b_imag, obj_real * b_imag - obj_imag * b_real))
        for part in range(2):
            at = slice((2 * j + part) * W, (2 * j + part + 1) * W)
            keep[at, :] = jnp.where(core == 0, grads[0][part], grads[1][part])
            send[at, :] = jnp.where(core == 0, grads[1][part], grads[0][part])
    patch = grad_imag * obj_real - grad_real * obj_imag
    shown = pltpu.roll(patch, W + row, 0)[:ROWS]
    pieces[...] = pltpu.roll(shown, lax.rem(col, W), 1)
    even, odd = pieces[pl.ds(0, 16, stride=2), :], pieces[pl.ds(1, 16, stride=2), :]
    keep[HALF : HALF + 16, :] = jnp.where(core == 0, even, odd)
    send[HALF : HALF + 16, :] = jnp.where(core == 0, odd, even)
    column = jnp.full((8, W), col, jnp.int32).astype(F32)
    keep[HALF + 16 :, :] = column
    send[HALF + 16 :, :] = column


def pack_kernel(sc, keep, other, out):
    lane = lax.broadcasted_iota(jnp.int32, (1, W), 1)
    first, second = keep[HALF + 16 : HALF + 17, :], other[HALF + 16 : HALF + 17, :]
    numbers = jnp.where(lane < 32, sc[0].astype(F32), jnp.where(lane < 64, first, second))
    for peer in range(32):
        rows = slice(PART * peer, PART * (peer + 1))
        at = MESSAGE * peer
        out[at : at + PART, :] = keep[rows, :] + other[rows, :]
        rows = pl.ds(HALF + 8 * BLOCKS[peer // 2][1] + peer % 2, 4, stride=2)
        out[at + PART : at + PART + 4, :] = keep[rows, :]
        out[at + PART + 4 : at + PART + 8, :] = other[rows, :]
        out[at + PART + 8 : at + MESSAGE, :] = numbers


def relay_kernel(received, out, pieces, numbers):
    total = received[:PART, :]
    for peer in range(1, 32):
        total = total + received[MESSAGE * peer : MESSAGE * peer + PART, :]
    heads = jnp.concatenate([received[pl.ds(MESSAGE * p + MESSAGE - 1, 1), :] for p in range(32)], 0)
    rolls = [heads] + [pltpu.roll(heads, 32 * i, 1) for i in (1, 2, 3)]
    quarter = lax.broadcasted_iota(jnp.int32, (32, W), 1) // 32
    for i in range(3):
        value = rolls[0]
        for shift in (1, 2, 3):
            value = jnp.where(quarter == (i + shift) % 4, rolls[shift], value)
        numbers[i] = value
    order = [2 * rank(a, xl) + zp for a in range(ANGLES) for xl in range(2) for zp in range(2)]
    rows = jnp.concatenate([received[MESSAGE * p + PART : MESSAGE * p + PART + 8, :] for p in order], 0)
    first, second = (
        jnp.concatenate([jnp.broadcast_to(numbers[1 + i, p : p + 1, :], (8, W)) for p in order], 0)
        for i in range(2)
    )
    row = lax.broadcasted_iota(jnp.int32, rows.shape, 0)
    columns = jnp.where(row % 8 < 4, first, second).astype(jnp.int32)
    lane = lax.broadcasted_iota(jnp.int32, rows.shape, 1)
    tiles = (columns >> 7) + jnp.where(lane < (columns & (W - 1)), 1, 0)
    for a in range(ANGLES):
        angle = jnp.max(numbers[0, order[4 * a] : order[4 * a] + 1, :]).astype(jnp.int32)
        slot = jnp.where(angle >= PAIRS, 2 * (ANGLES - 1 - angle) + 1, 2 * angle)
        at = pl.multiple_of(32 * slot, 32)
        for t in range(4):
            part = jnp.where(tiles[32 * a : 32 * a + 32] == t, rows[32 * a : 32 * a + 32], 0.0)
            part = jnp.sum(part.reshape(4, 8, W), axis=0)
            pieces[pl.ds(at + 8 * t, 8), :] = part + pltpu.roll(part, 4, 0)
    for z in range(8):
        out[z, :PART, :] = total
        out[z, PART:, :] = pieces[pl.ds(z % 4, 32, stride=8), :]


def adjoint_kernel(received, dft_t, leaving, rows_tables, edges, middles, *refs):
    beams, (out, pieces, shifted, sheared) = refs[:PAIRS], refs[PAIRS:]
    block = 2 * lax.axis_index("y") + lax.axis_index("xh")
    even, odd = received[0], received[4]
    for z in range(1, 4):
        even, odd = even + received[z], odd + received[4 + z]
    chunk = jnp.concatenate([even[:PART], odd[:PART]], 0) * (1.0 / 16.0)
    pieces[...] = jnp.where(lax.axis_index("zp") == 0, even[PART:], odd[PART:])
    rows = jnp.concatenate([pieces[pl.ds(t, 8, stride=4), :] for t in range(4)], axis=1)
    spectrum = three(mm, split(rows), (dft_t[0], dft_t[1]))
    weight = jnp.where(lax.broadcasted_iota(jnp.int32, (8, N), 1) % H == 0, 0.5 / N, 1.0 / N)
    cbar = spectrum * weight
    c_mid, s_mid = middles[:ANGLES, :], middles[ANGLES:, :]
    c_reals = cbar[:, :H] * c_mid - cbar[:, H:] * s_mid
    c_imags = cbar[:, H:] * c_mid + cbar[:, :H] * s_mid
    at = pl.ds(pl.multiple_of(64 * block, 64), 64)
    rows_dft = dft_t[0, at, :].astype(F32) + dft_t[1, at, :].astype(F32)
    lane_zero = lax.broadcasted_iota(jnp.int32, (64, H), 1) == 0
    r_cos, r_sin = rows_dft[:, :H], rows_dft[:, H:]
    r_sin_real = jnp.where(lane_zero, 0.0, r_sin)
    r_cos_imag = jnp.where(lane_zero, r_sin, r_cos)
    mirror = jnp.where(lane_zero, 1.0, -1.0)
    nyquist = []
    for slot in range(ANGLES):
        c_real, c_imag = c_reals[slot : slot + 1, :], c_imags[slot : slot + 1, :]
        cosines = c_real * r_cos + c_imag * r_sin_real
        sines = c_imag * r_cos_imag - c_real * r_sin_real
        if slot % 2 == 0:
            sines = sines * mirror
        nyquist.append(sines[:, :1])
        at = slice(64 * slot, 64 * slot + 64)
        shifted[0, at, :H], shifted[1, at, :H] = split(cosines)
        shifted[0, at, H:], shifted[1, at, H:] = split(sines)
    for q in range(PAIRS):
        at = slice(2 * 64 * q, 2 * 64 * (q + 1))
        even = three(mm, (shifted[0, at, :H], shifted[1, at, :H]), (beams[q][0, :H, :], beams[q][1, :H, :]))
        odd = three(mm, (shifted[0, at, H:], shifted[1, at, H:]), (beams[q][0, H:, :], beams[q][1, H:, :]))
        even = even + jnp.concatenate(nyquist[2 * q : 2 * q + 2], 0) * edges[q, 0:1, :]
        sheared[0, at, :H], sheared[1, at, :H] = split(even)
        sheared[0, at, H:], sheared[1, at, H:] = split(odd)
    lane_first = lax.broadcasted_iota(jnp.int32, (8, H), 1) == 0
    sums = [None] * 8
    for q in range(PAIRS):
        at = slice(2 * 64 * q, 2 * 64 * (q + 1))
        real, imag = (
            three(mm, (sheared[0, at, part], sheared[1, at, part]), (dft_t[0, :H, part], dft_t[1, :H, part]))
            for part in (slice(0, H), slice(H, N))
        )
        cb, sb = rows_tables[q, 0, 64:72, :], rows_tables[q, 1, 64:72, :]
        near = rows_tables[q, :, pl.ds(pl.multiple_of(8 * block, 8), 8), :]
        for u in range(8):
            ca, sa = near[0, u : u + 1, :], near[1, u : u + 1, :]
            c, s = ca * cb - sa * sb, sa * cb + ca * sb
            c_first, s_first = jnp.where(lane_first, 1.0, c), jnp.where(lane_first, 0.0, s)
            one, two = slice(8 * u, 8 * u + 8), slice(64 + 8 * u, 72 + 8 * u)
            unturned = jnp.concatenate(
                [
                    (real[one] + real[two]) * c_first + (imag[one] - imag[two]) * s_first,
                    (imag[one] + imag[two]) * c - (real[one] - real[two]) * s_first,
                ],
                1,
            )
            sums[u] = unturned if q == 0 else sums[u] + unturned
    weight = jnp.where(lax.broadcasted_iota(jnp.int32, (64, N), 1) % H == 0, 1.0 / 32.0, 1.0 / 16.0)
    whole = jnp.concatenate(sums, 0) * weight
    columns = three(mm, split(whole), (leaving[0], leaving[1]))
    for part in range(2):
        first, second = (columns[:, (2 * part + i) * W : (2 * part + i + 1) * W] for i in range(2))
        blocks = jnp.concatenate([first, second], 0).T
        for a in range(4):
            for peer in (rank(4 * part + a, 0), rank(4 * part + a, 1)):
                out[peer, :CHUNK, :] = chunk
                out[peer, CHUNK:, :] = blocks[32 * a : 32 * a + 32, :]


def assemble_kernel(received, out, probe_out, sem):
    move = pltpu.make_async_copy(received.at[:, pl.ds(0, CHUNK), :], probe_out.at[lax.axis_index("core")], sem)
    move.start()
    xl = lax.axis_index("xl")
    lower = lax.broadcasted_iota(jnp.int32, (32, W), 1) < 64
    for b in range(4):
        even = received[rank(2 * b, xl), CHUNK:, :]
        odd = received[rank(2 * b + 1, xl), CHUNK:, :]
        lanes = slice(b * W, (b + 1) * W)
        out[0, :32, lanes] = jnp.where(lower, even, pltpu.roll(odd, 64, 1))
        out[0, 32:, lanes] = jnp.where(lower, pltpu.roll(even, 64, 1), odd)
    move.wait()


def forward_call(*args):
    return pl.pallas_call(
        forward_kernel,
        in_specs=[pl.BlockSpec(memory_space=pltpu.SMEM)] + [pl.BlockSpec(memory_space=pl.ANY)] * 6,
        out_specs=pl.BlockSpec(memory_space=pltpu.VMEM),
        out_shape=jax.ShapeDtypeStruct((4 * ROWS, W), F32),
        scratch_shapes=[
            pltpu.VMEM((N, N), BF16),
            pltpu.VMEM((2, N, N), BF16),
            pltpu.VMEM((2, H, N), BF16),
            pltpu.VMEM((H // 4 + 24, N), F32),
            pltpu.VMEM((2, N, H), BF16),
            pltpu.VMEM((8, H), F32),
            pltpu.VMEM((N, N), F32),
            pltpu.VMEM((2, N, N), BF16),
            pltpu.VMEM((2, 2, N, H), BF16),
            pltpu.SemaphoreType.DMA((6,)),
        ],
        compiler_params=pltpu.CompilerParams(vmem_limit_bytes=60 * 1024 * 1024),
        cost_estimate=pl.CostEstimate(flops=4 * 10**9, bytes_accessed=4 * 10**6, transcendentals=0),
        name="forward",
    )(*args)


def vmem_call(kernel, outs, scratch, name, *args, far=0):
    result = pl.pallas_call(
        kernel,
        in_specs=[
            pl.BlockSpec(memory_space=pltpu.SMEM if a.dtype == jnp.int32 else pltpu.VMEM) for a in args
        ],
        out_specs=[pl.BlockSpec(memory_space=pltpu.VMEM)] * (len(outs) - far)
        + [pl.BlockSpec(memory_space=pl.ANY)] * far,
        out_shape=[jax.ShapeDtypeStruct(*o) if o[-1] == BF16 else jax.ShapeDtypeStruct(o, F32) for o in outs],
        scratch_shapes=scratch,
        compiler_params=pltpu.CompilerParams(vmem_limit_bytes=32 * 1024 * 1024),
        cost_estimate=pl.CostEstimate(flops=3 * 10**9, bytes_accessed=4 * 10**6, transcendentals=0),
        name=name,
    )(*args)
    return result if len(outs) > 1 else result[0]


Z = ("zp", "zq")
GZ = ("xl", "zq", "zp", "core")
PLANE = ("xl", "xh", "y")


def rank(block, xl):
    return 8 * xl + 4 * (block % 2) + block // 2


BLOCKS = {rank(block, xl): (block, xl) for block in range(ANGLES) for xl in range(2)}


def exchange(blocks, axes):
    return lax.all_to_all(blocks, axes, split_axis=0, concat_axis=0, tiled=True)


def swap(rows):
    return lax.ppermute(rows, "core", [(0, 1), (1, 0)])


def local(volume, probe, measured, angle_index, row_offset, col_offset):
    dft, dft_t, leaving = (jnp.asarray(t) for t in dft_tables())
    dfts = jnp.asarray(window_tables())
    factors, rows_tables, all_beams, edges, middles = (jnp.asarray(t) for t in phase_tables())
    beams = [jnp.asarray(b) for b in phase_tables()[2]]
    row = forward_call(angle_index, volume, dft, dft_t, factors, all_beams, edges)
    whole = exchange(row.reshape(ROWS, 4, W), GZ).reshape(4 * ROWS, W)
    split_modes = pltpu.VMEM((2, MODES // 2, 2 * W, 2 * W), BF16)
    waves, band_dft, band_probe = vmem_call(
        prepare_kernel,
        [(MODES // 2, 2 * W, 2 * W), ((2 * W, 2 * W), BF16), (MODES, 2, ROWS, W)],
        [split_modes],
        "prepare",
        row_offset,
        probe,
        dfts,
    )
    keep, send = vmem_call(
        window_kernel,
        [(HALF + 24, W)] * 2,
        [split_modes, pltpu.VMEM((MODES // 2, 2 * W, 2 * W), F32), pltpu.VMEM((ROWS, W), F32)],
        "window",
        row_offset,
        col_offset,
        whole,
        probe,
        measured,
        dfts,
        waves,
        band_dft,
        band_probe,
    )
    packed = vmem_call(pack_kernel, [(32 * MESSAGE, W)], [], "pack", angle_index, keep, swap(send))
    shared = exchange(packed.reshape(32, MESSAGE, 1, W), PLANE + ("zp",)).reshape(32 * MESSAGE, W)
    scratch = [pltpu.VMEM((256, W), F32), pltpu.VMEM((3, 32, W), F32)]
    relay = vmem_call(relay_kernel, [(8, PART + 32, W)], scratch, "relay", shared)
    rows = exchange(relay, Z)
    blocks = vmem_call(
        adjoint_kernel,
        [(16, CHUNK + 32, W)],
        [pltpu.VMEM((32, W), F32), pltpu.VMEM((2, N, N), BF16), pltpu.VMEM((2, N, N), BF16)],
        "adjoint",
        rows,
        dft_t,
        leaving,
        rows_tables,
        edges,
        middles,
        *beams,
    )
    final = exchange(blocks, PLANE)
    other = swap(final[:, :CHUNK, :])
    volume_update, half = vmem_call(
        assemble_kernel,
        [(1, 64, N), (2, 16, CHUNK, W)],
        [pltpu.SemaphoreType.DMA],
        "assemble",
        final,
        far=1,
    )
    core = lax.axis_index("core")
    probe_update = lax.dynamic_update_slice(half, other[None], (1 - core, 0, 0, 0))
    return volume_update, probe_update.reshape(MODES, 2, W, W)


def solution(mesh):
    split_mesh = Mesh(mesh.devices.reshape(4, 2, 2, 4, 2, 2), ("y", "xh", "xl", "zq", "zp", "core"))
    angle, gz = ("y", "xh"), GZ
    return jax.shard_map(
        local,
        mesh=split_mesh,
        in_specs=(
            P(gz, None, None),
            P(),
            P(angle, gz, None, None),
            P(angle),
            P(angle, gz),
            P(angle, gz),
        ),
        out_specs=(P(gz, angle, None), P()),
        check_vma=False,
    )
```

```python
import math

import jax
import jax.numpy as jnp
import numpy as np
from jax import lax
from jax.experimental import pallas as pl
from jax.experimental.pallas import tpu as pltpu
from jax.sharding import Mesh, PartitionSpec as P

N = 512
H = N // 2
W = 128
MODES = 8
ANGLES = 8
PAIRS = ANGLES // 2
ROWS = 32
HALF = MODES * 2 * W // 2
CHUNK = HALF // 16
PART = CHUNK // 2
MESSAGE = PART + 9
F32 = jnp.float32
BF16 = jnp.bfloat16


def split_const(table):
    high = table.astype(BF16)
    low = (table - high.astype(np.float64)).astype(BF16)
    return np.stack([high, low])


def dft_tables():
    k, n = np.arange(H)[:, None], np.arange(N)[None, :]
    turns = np.pi / N * (k * (2 * n + 1) % (2 * N))
    table = np.concatenate([np.cos(turns), -np.sin(turns)], 0)
    table[H] = 2.0 * (np.arange(N) % 2) - 1.0
    order = np.arange(N).reshape(2, 4, 2, 32).transpose(0, 2, 1, 3).reshape(N)
    return [split_const(np.ascontiguousarray(t)) for t in (table, table.T, table[:, order])]


def window_tables():
    j = np.arange(W)
    turns = 2.0 * np.pi / W * (j[:, None] * j[None, :] % W)
    c, s = np.cos(turns), np.sin(turns)
    return np.stack([split_const(np.block([[c, s], [-s, c]])), split_const(np.block([[c, -s], [s, c]]))])


def shears():
    theta = np.pi * (np.arange(ANGLES) + 0.5) / ANGLES - np.pi / 2
    return -np.tan(theta / 2), np.sin(theta)


def cos_sin(phase):
    return np.stack([np.cos(phase), np.sin(phase)], 1)


def phase_tables():
    shear_x, shear_y = shears()
    cells = np.arange(N) - N / 2
    unit_one = -2.0 * np.pi / N * shear_x
    unit_two = -2.0 * np.pi / N * shear_y[:PAIRS]
    by_y = unit_one[:, None, None] * np.concatenate([cells[:H], cells[:H - 1:-1]])[None, None, :]
    nyquist = np.ones((ANGLES, 8, N))
    nyquist[:, 0] = 0.5 * np.cos(by_y[:, 0] * H)
    factors = np.concatenate(
        [
            cos_sin(by_y * (8 * np.arange(H // 8))[None, :, None]).reshape(ANGLES, H // 4, N),
            cos_sin(by_y * np.arange(8)[None, :, None]).reshape(ANGLES, 16, N),
            nyquist,
        ],
        1,
    )
    freq = np.arange(H, dtype=np.float64)
    freq[0] = H
    by_k = unit_one[:PAIRS, None, None] * freq[None, None, :]
    rows_coarse = cos_sin(by_k * cells[::8][None, :, None])
    rows_fine = cos_sin(by_k * np.arange(8)[None, :, None])
    rows_tables = np.concatenate([rows_coarse, rows_fine], 2)
    frequencies = np.arange(H, dtype=np.float64)
    turns = unit_two[:, None, None] * frequencies[None, :, None] * (H - 0.5 - np.arange(H))[None, None, :]
    low = np.cos(unit_two[:, None] * H * cells[None, :H])
    high = np.cos(unit_two[:, None] * H * cells[None, :H - 1:-1])
    table = np.concatenate([np.cos(turns), np.sin(turns)], 1)
    table[:, H] = 0.5 * (low - high)
    beams = np.ascontiguousarray(np.moveaxis(split_const(table), 0, 1))
    edges = np.zeros((PAIRS, 8, H))
    edges[:, 0] = 0.5 * (low + high)
    middle = 0.5 * unit_two[:, None] * frequencies[None, :]
    ordered = np.stack([middle, -middle], 1).reshape(ANGLES, H)
    middles = np.concatenate([np.cos(ordered), np.sin(ordered)], 0)
    return [t if t.dtype == BF16 else t.astype(np.float32) for t in (factors, rows_tables, beams, edges, middles)]


def mm(a, b):
    return lax.dot_general(a, b, (((1,), (0,)), ((), ())), preferred_element_type=F32)


def mm_t(a, b):
    return lax.dot_general(a, b, (((1,), (1,)), ((), ())), preferred_element_type=F32)


def split(value):
    high = value.astype(BF16)
    return high, (value - high.astype(F32)).astype(BF16)


def three(dot, a, b):
    rows = a[0].shape[0]
    both = dot(jnp.concatenate([a[0], a[1]], 0), b[0])
    return both[:rows] + (both[rows:] + dot(a[0], b[1]))


def forward_kernel(
    sc, volume, dft_hbm, dft_t_hbm, factors_hbm, beams_hbm, edges_hbm, out,
    slab, dft, dft_t, factors, beams, edges, spec, turned, field, sems,
):
    number = sc[0]
    mirrored = number >= PAIRS
    sign = jnp.where(mirrored, -1.0, 1.0)
    folded = jnp.where(mirrored, ANGLES - 1 - number, number)
    copies = [
        (volume.at[0], slab),
        (dft_hbm, dft),
        (factors_hbm.at[number], factors),
        (dft_t_hbm.at[:, pl.ds(0, H), :], dft_t),
        (beams_hbm.at[folded], beams),
        (edges_hbm.at[folded], edges),
    ]
    moves = [pltpu.make_async_copy(source, target, sems.at[i]) for i, (source, target) in enumerate(copies)]
    for move in moves:
        move.start()
    halves = (slice(0, H), slice(H, N))
    rows, lanes = (lax.broadcasted_iota(jnp.int32, (H, H), axis) for axis in (0, 1))
    reverse = jnp.where(rows + lanes == H - 1, 1.0, 0.0).astype(BF16)
    moves[0].wait()
    backward = mm(slab[:, H:], reverse).astype(BF16)
    moves[1].wait()
    moves[2].wait()
    for lanes, columns in zip(halves, (slab[:, :H], backward)):
        both = mm(jnp.concatenate([dft[0], dft[1]], 0), columns)
        spec[:, lanes] = both[:N] + both[N:]
    half_row = jnp.where(lax.broadcasted_iota(jnp.int32, (8, H), 0) == 0, 0.5, 1.0)
    for lanes in halves:
        cb, sb = factors[64:72, lanes], factors[72:80, lanes]
        for pair in range(H // 16):
            reals, imags = [], []
            for u in (2 * pair, 2 * pair + 1):
                ca, sa = factors[u : u + 1, lanes], factors[32 + u : 33 + u, lanes]
                c, s = ca * cb - sa * sb, sa * cb + ca * sb
                a, b = spec[8 * u : 8 * u + 8, lanes], spec[H + 8 * u : H + 8 * u + 8, lanes]
                real, imag = a * c - b * s, a * s + b * c
                if u == 0:
                    real, imag = real * half_row, imag * factors[80:88, lanes]
                reals.append(real)
                imags.append(imag)
            for base, parts in ((16 * pair, reals), (H + 16 * pair, imags)):
                at = slice(base, base + 16)
                turned[0, at, lanes], turned[1, at, lanes] = split(jnp.concatenate(parts, 0))
    moves[3].wait()
    for comps in halves:
        for t in range(2):
            near, far = slice(t * W, (t + 1) * W), slice(H + t * W, H + (t + 1) * W)
            both = three(
                mm,
                (dft_t[0, :, comps], dft_t[1, :, comps]),
                [jnp.concatenate([turned[p, comps, near], turned[p, comps, far]], 1) for p in range(2)],
            )
            field[0, 0, comps, near], field[0, 1, comps, near] = split(both[:, :W] + both[:, W:])
            field[1, 0, comps, near], field[1, 1, comps, near] = split(both[:, :W] - both[:, W:])
    moves[4].wait()
    moves[5].wait()
    c = beams[0, :H, :].astype(F32) + beams[1, :H, :].astype(F32)
    s = beams[0, H:, :].astype(F32) + beams[1, H:, :].astype(F32)
    top = lax.broadcasted_iota(jnp.int32, (8, H), 0) == 0
    c_imag = jnp.concatenate([jnp.where(top, edges[:1, :], c[:8]), c[8:]], 0)
    s_imag = jnp.concatenate([jnp.where(top, 0.0, s[:8]), s[8:]], 0) * sign

    def fold(value):
        return value[:, :W] + value[:, W:]

    def beam(part, rows):
        comps = halves[part]
        return three(mm_t, (dft[0, comps, :H], dft[1, comps, :H]), (field[part, 0, rows], field[part, 1, rows]))

    real = fold(beam(0, halves[0]) * c)
    imag = fold(beam(1, halves[0]) * c_imag)
    odd = beam(1, halves[1])
    real = real + fold(odd * s_imag)
    extra = jnp.where(top[:, :W], fold(odd[:8] * s[:8]), 0.0)
    imag = imag - fold(beam(0, halves[1]) * s_imag)
    imag = jnp.concatenate([imag[:8] + extra, imag[8:]], 0)
    real, imag = jnp.sum(real, axis=1, keepdims=True), jnp.sum(imag, axis=1, keepdims=True)
    weight = jnp.where(lax.broadcasted_iota(jnp.int32, (H, 1), 0) == 0, 0.5, 1.0)
    real, imag = real * weight, imag * weight
    c_mid, s_mid = c[:, H - 1 :], s_imag[:, H - 1 :]
    real, imag = real * c_mid + imag * s_mid, imag * c_mid - real * s_mid
    total = jnp.zeros((8, N), F32)
    for r in range(0, H, 32):
        at, below = slice(r, r + 32), slice(H + r, H + r + 32)
        f_real = dft[0, at, :].astype(F32) + dft[1, at, :].astype(F32)
        f_imag = dft[0, below, :].astype(F32) + dft[1, below, :].astype(F32)
        terms = real[at] * f_real + imag[at] * f_imag
        total = total + jnp.sum(terms.reshape(4, 8, N), axis=0)
    row = jnp.sum(total, axis=0, keepdims=True) * (8.0 / (N * N))
    for t in range(4):
        out[pl.ds(t, ROWS, stride=4), :] = jnp.broadcast_to(row[:, t * W : (t + 1) * W], (ROWS, W))


def turn(block):
    return jnp.concatenate(
        [
            jnp.concatenate([block[:W, :W], block[W:, :W]], 1),
            jnp.concatenate([block[:W, W:], block[W:, W:]], 1),
        ],
        0,
    )


def pairs_of_modes():
    return [(j, j + MODES // 2) for j in range(MODES // 2)]


def prepare_kernel(row_ref, probe, dfts, waves, band_dft, band_probe, stage):
    start = -row_ref[0, 0]
    lefts, rights = (dfts[0, 0], dfts[0, 1]), (dfts[1, 0], dfts[1, 1])
    for j, pair in enumerate(pairs_of_modes()):
        reals = jnp.concatenate([probe[m, 0] for m in pair], 1)
        imags = jnp.concatenate([probe[m, 1] for m in pair], 1)
        stage[0, j], stage[1, j] = split(jnp.concatenate([reals, imags], 0))
    for j in range(MODES // 2):
        stage[0, j], stage[1, j] = split(turn(three(mm, lefts, (stage[0, j], stage[1, j]))))
    for j in range(MODES // 2):
        waves[j] = three(mm, (stage[0, j], stage[1, j]), rights)
    source = lax.broadcasted_iota(jnp.int32, (2 * W, 2 * W), 0)
    target = lax.broadcasted_iota(jnp.int32, (2 * W, 2 * W), 1)
    wanted = start + (target & (ROWS - 1)) + jnp.where(target & ROWS != 0, W, 0)
    chosen = jnp.where(source == wanted, 1.0, 0.0)
    first = jnp.where(target < 4 * ROWS, chosen, 0.0).astype(BF16)
    second = jnp.where((target >= 4 * ROWS) & (target < 6 * ROWS), chosen, 0.0).astype(BF16)
    band_dft[...] = (mm(lefts[0], first) + mm(lefts[1], second)).astype(BF16)
    for m in range(MODES):
        for part in range(2):
            band_probe[m, part] = probe[m, part, pl.ds(start, ROWS), :]


def window_kernel(
    row_ref, col_ref, whole, probe, measured, dfts, waves, band_dft, band_probe, keep, send, stage, far, pieces
):
    row, col, core = row_ref[0, 0], col_ref[0, 0], lax.axis_index("core")
    rows = jnp.concatenate([whole[pl.ds(t, ROWS, stride=4), :] for t in range(4)], axis=1)
    band = pltpu.roll(rows, lax.rem(N - col, N), 1)[:, :W]
    band_real, band_imag = jnp.cos(band) - 1.0, jnp.sin(band)
    lefts, rights = (dfts[0, 0], dfts[0, 1]), (dfts[1, 0], dfts[1, 1])
    pairs = pairs_of_modes()
    sides = (slice(0, W), slice(W, 2 * W))

    def put(j, value):
        stage[0, j], stage[1, j] = split(value)

    def get(j):
        return stage[0, j], stage[1, j]

    lines = []
    for m in [m for pair in pairs for m in pair]:
        p_real, p_imag = band_probe[m, 0], band_probe[m, 1]
        lines.append(
            jnp.concatenate(
                [p_real * band_real - p_imag * band_imag, p_real * band_imag + p_imag * band_real], 1
            )
        )
    lines = three(mm, split(jnp.concatenate(lines, 0)), rights)
    intensity = jnp.zeros((W, W), F32)
    for j in range(MODES // 2):
        one, two = (lines[2 * ROWS * j + ROWS * i : 2 * ROWS * j + ROWS * (i + 1)] for i in range(2))
        both = jnp.concatenate(
            [jnp.concatenate([one[:, :W], two[:, :W]], 1), jnp.concatenate([one[:, W:], two[:, W:]], 1)], 0
        )
        high, low = split(both)
        blank = jnp.zeros((2 * ROWS, 2 * W), BF16)
        total = waves[j] + turn(mm(band_dft[...], jnp.concatenate([high, low, high, blank], 0)))
        far[j] = total
        power = total * total
        power = power[:W] + power[W:]
        intensity = intensity + (power[:, :W] + power[:, W:])
    pad = jnp.zeros((W - ROWS, W), F32)
    obj_real = pltpu.roll(jnp.concatenate([band_real, pad], 0), -row, 0) + 1.0
    obj_imag = pltpu.roll(jnp.concatenate([band_imag, pad], 0), -row, 0)
    factor = (1.0 - jnp.sqrt(measured[0, 0] + 1.0) / jnp.sqrt(intensity + 1.0)) * (1.0 / W)
    factors = jnp.concatenate([jnp.concatenate([factor, factor], 1)] * 2, 0)
    for j in range(MODES // 2):
        put(j, far[j] * factors)
    for j in range(MODES // 2):
        put(j, turn(three(mm, get(j), lefts)))
    grad_real, grad_imag = jnp.zeros((W, W), F32), jnp.zeros((W, W), F32)
    for j, pair in enumerate(pairs):
        back = three(mm, rights, get(j))
        grads = []
        for m, lanes in zip(pair, sides):
            b_real, b_imag = back[:W, lanes], back[W:, lanes]
            p_real, p_imag = probe[m, 0], probe[m, 1]
            grad_real = grad_real + (p_real * b_real + p_imag * b_imag)
            grad_imag = grad_imag + (p_real * b_imag - p_imag * b_real)
            grads.append((obj_real * b_real + obj_imag * b_imag, obj_real * b_imag - obj_imag * b_real))
        for part in range(2):
            at = slice((2 * j + part) * W, (2 * j + part + 1) * W)
            keep[at, :] = jnp.where(core == 0, grads[0][part], grads[1][part])
            send[at, :] = jnp.where(core == 0, grads[1][part], grads[0][part])
    patch = grad_imag * obj_real - grad_real * obj_imag
    shown = pltpu.roll(patch, W + row, 0)[:ROWS]
    pieces[...] = pltpu.roll(shown, lax.rem(col, W), 1)
    even, odd = pieces[pl.ds(0, 16, stride=2), :], pieces[pl.ds(1, 16, stride=2), :]
    keep[HALF : HALF + 16, :] = jnp.where(core == 0, even, odd)
    send[HALF : HALF + 16, :] = jnp.where(core == 0, odd, even)
    column = jnp.full((8, W), col, jnp.int32).astype(F32)
    keep[HALF + 16 :, :] = column
    send[HALF + 16 :, :] = column


def pack_kernel(sc, keep, other, out):
    lane = lax.broadcasted_iota(jnp.int32, (1, W), 1)
    first, second = keep[HALF + 16 : HALF + 17, :], other[HALF + 16 : HALF + 17, :]
    numbers = jnp.where(lane < 32, sc[0].astype(F32), jnp.where(lane < 64, first, second))
    for peer in range(32):
        place, zp = peer % 16, peer // 16
        rows = slice(PART * (2 * place + zp), PART * (2 * place + zp + 1))
        at = MESSAGE * peer
        out[at : at + PART, :] = keep[rows, :] + other[rows, :]
        rows = pl.ds(HALF + 8 * BLOCKS[place][1] + zp, 4, stride=2)
        out[at + PART : at + PART + 4, :] = keep[rows, :]
        out[at + PART + 4 : at + PART + 8, :] = other[rows, :]
        out[at + PART + 8 : at + MESSAGE, :] = numbers


def relay_kernel(received, out, pieces, numbers):
    total = received[:PART, :]
    for peer in range(1, 32):
        total = total + received[MESSAGE * peer : MESSAGE * peer + PART, :]
    heads = jnp.concatenate([received[pl.ds(MESSAGE * p + MESSAGE - 1, 1), :] for p in range(32)], 0)
    rolls = [heads] + [pltpu.roll(heads, 32 * i, 1) for i in (1, 2, 3)]
    quarter = lax.broadcasted_iota(jnp.int32, (32, W), 1) // 32
    for i in range(3):
        value = rolls[0]
        for shift in (1, 2, 3):
            value = jnp.where(quarter == (i + shift) % 4, rolls[shift], value)
        numbers[i] = value
    order = [16 * zp + rank(a, xl) for a in range(ANGLES) for xl in range(2) for zp in range(2)]
    rows = jnp.concatenate([received[MESSAGE * p + PART : MESSAGE * p + PART + 8, :] for p in order], 0)
    first, second = (
        jnp.concatenate([jnp.broadcast_to(numbers[1 + i, p : p + 1, :], (8, W)) for p in order], 0)
        for i in range(2)
    )
    row = lax.broadcasted_iota(jnp.int32, rows.shape, 0)
    columns = jnp.where(row % 8 < 4, first, second).astype(jnp.int32)
    lane = lax.broadcasted_iota(jnp.int32, rows.shape, 1)
    tiles = (columns >> 7) + jnp.where(lane < (columns & (W - 1)), 1, 0)
    for a in range(ANGLES):
        angle = jnp.max(numbers[0, order[4 * a] : order[4 * a] + 1, :]).astype(jnp.int32)
        slot = jnp.where(angle >= PAIRS, 2 * (ANGLES - 1 - angle) + 1, 2 * angle)
        at = pl.multiple_of(32 * slot, 32)
        for t in range(4):
            part = jnp.where(tiles[32 * a : 32 * a + 32] == t, rows[32 * a : 32 * a + 32], 0.0)
            part = jnp.sum(part.reshape(4, 8, W), axis=0)
            pieces[pl.ds(at + 8 * t, 8), :] = part + pltpu.roll(part, 4, 0)
    for z in range(8):
        out[z, :PART, :] = total
        out[z, PART:, :] = pieces[pl.ds(z % 4, 32, stride=8), :]


def adjoint_kernel(received, dft_t, leaving, rows_tables, edges, middles, *refs):
    beams, (out, pieces, shifted, sheared) = refs[:PAIRS], refs[PAIRS:]
    block = 2 * lax.axis_index("y") + lax.axis_index("xh")
    even, odd = received[0], received[4]
    for z in range(1, 4):
        even, odd = even + received[z], odd + received[4 + z]
    chunk = jnp.concatenate([even[:PART], odd[:PART]], 0) * (1.0 / 16.0)
    pieces[...] = jnp.where(lax.axis_index("zp") == 0, even[PART:], odd[PART:])
    rows = jnp.concatenate([pieces[pl.ds(t, 8, stride=4), :] for t in range(4)], axis=1)
    spectrum = three(mm, split(rows), (dft_t[0], dft_t[1]))
    weight = jnp.where(lax.broadcasted_iota(jnp.int32, (8, N), 1) % H == 0, 0.5 / N, 1.0 / N)
    cbar = spectrum * weight
    c_mid, s_mid = middles[:ANGLES, :], middles[ANGLES:, :]
    c_reals = cbar[:, :H] * c_mid - cbar[:, H:] * s_mid
    c_imags = cbar[:, H:] * c_mid + cbar[:, :H] * s_mid
    at = pl.ds(pl.multiple_of(64 * block, 64), 64)
    rows_dft = dft_t[0, at, :].astype(F32) + dft_t[1, at, :].astype(F32)
    lane_zero = lax.broadcasted_iota(jnp.int32, (64, H), 1) == 0
    r_cos, r_sin = rows_dft[:, :H], rows_dft[:, H:]
    r_sin_real = jnp.where(lane_zero, 0.0, r_sin)
    r_cos_imag = jnp.where(lane_zero, r_sin, r_cos)
    mirror = jnp.where(lane_zero, 1.0, -1.0)
    nyquist = []
    for slot in range(ANGLES):
        c_real, c_imag = c_reals[slot : slot + 1, :], c_imags[slot : slot + 1, :]
        cosines = c_real * r_cos + c_imag * r_sin_real
        sines = c_imag * r_cos_imag - c_real * r_sin_real
        if slot % 2 == 0:
            sines = sines * mirror
        nyquist.append(sines[:, :1])
        at = slice(64 * slot, 64 * slot + 64)
        shifted[0, at, :H], shifted[1, at, :H] = split(cosines)
        shifted[0, at, H:], shifted[1, at, H:] = split(sines)
    for q in range(PAIRS):
        at = slice(2 * 64 * q, 2 * 64 * (q + 1))
        even = three(mm, (shifted[0, at, :H], shifted[1, at, :H]), (beams[q][0, :H, :], beams[q][1, :H, :]))
        odd = three(mm, (shifted[0, at, H:], shifted[1, at, H:]), (beams[q][0, H:, :], beams[q][1, H:, :]))
        even = even + jnp.concatenate(nyquist[2 * q : 2 * q + 2], 0) * edges[q, 0:1, :]
        sheared[0, at, :H], sheared[1, at, :H] = split(even)
        sheared[0, at, H:], sheared[1, at, H:] = split(odd)
    lane_first = lax.broadcasted_iota(jnp.int32, (8, H), 1) == 0
    sums = [None] * 8
    for q in range(PAIRS):
        at = slice(2 * 64 * q, 2 * 64 * (q + 1))
        real, imag = (
            three(mm, (sheared[0, at, part], sheared[1, at, part]), (dft_t[0, :H, part], dft_t[1, :H, part]))
            for part in (slice(0, H), slice(H, N))
        )
        cb, sb = rows_tables[q, 0, 64:72, :], rows_tables[q, 1, 64:72, :]
        near = rows_tables[q, :, pl.ds(pl.multiple_of(8 * block, 8), 8), :]
        for u in range(8):
            ca, sa = near[0, u : u + 1, :], near[1, u : u + 1, :]
            c, s = ca * cb - sa * sb, sa * cb + ca * sb
            c_first, s_first = jnp.where(lane_first, 1.0, c), jnp.where(lane_first, 0.0, s)
            one, two = slice(8 * u, 8 * u + 8), slice(64 + 8 * u, 72 + 8 * u)
            unturned = jnp.concatenate(
                [
                    (real[one] + real[two]) * c_first + (imag[one] - imag[two]) * s_first,
                    (imag[one] + imag[two]) * c - (real[one] - real[two]) * s_first,
                ],
                1,
            )
            sums[u] = unturned if q == 0 else sums[u] + unturned
    weight = jnp.where(lax.broadcasted_iota(jnp.int32, (64, N), 1) % H == 0, 1.0 / 32.0, 1.0 / 16.0)
    whole = jnp.concatenate(sums, 0) * weight
    columns = three(mm, split(whole), (leaving[0], leaving[1]))
    for part in range(2):
        first, second = (columns[:, (2 * part + i) * W : (2 * part + i + 1) * W] for i in range(2))
        blocks = jnp.concatenate([first, second], 0).T
        for a in range(4):
            for peer in (rank(4 * part + a, 0), rank(4 * part + a, 1)):
                out[peer, :CHUNK, :] = chunk
                out[peer, CHUNK:, :] = blocks[32 * a : 32 * a + 32, :]


def assemble_kernel(received, out, probe_out, sem):
    move = pltpu.make_async_copy(received.at[:, pl.ds(0, CHUNK), :], probe_out.at[lax.axis_index("core")], sem)
    move.start()
    xl = lax.axis_index("xl")
    lower = lax.broadcasted_iota(jnp.int32, (32, W), 1) < 64
    for b in range(4):
        even = received[rank(2 * b, xl), CHUNK:, :]
        odd = received[rank(2 * b + 1, xl), CHUNK:, :]
        lanes = slice(b * W, (b + 1) * W)
        out[0, :32, lanes] = jnp.where(lower, even, pltpu.roll(odd, 64, 1))
        out[0, 32:, lanes] = jnp.where(lower, pltpu.roll(even, 64, 1), odd)
    move.wait()


def forward_call(*args):
    return pl.pallas_call(
        forward_kernel,
        in_specs=[pl.BlockSpec(memory_space=pltpu.SMEM)] + [pl.BlockSpec(memory_space=pl.ANY)] * 6,
        out_specs=pl.BlockSpec(memory_space=pltpu.VMEM),
        out_shape=jax.ShapeDtypeStruct((4 * ROWS, W), F32),
        scratch_shapes=[
            pltpu.VMEM((N, N), BF16),
            pltpu.VMEM((2, N, N), BF16),
            pltpu.VMEM((2, H, N), BF16),
            pltpu.VMEM((H // 4 + 24, N), F32),
            pltpu.VMEM((2, N, H), BF16),
            pltpu.VMEM((8, H), F32),
            pltpu.VMEM((N, N), F32),
            pltpu.VMEM((2, N, N), BF16),
            pltpu.VMEM((2, 2, N, H), BF16),
            pltpu.SemaphoreType.DMA((6,)),
        ],
        compiler_params=pltpu.CompilerParams(vmem_limit_bytes=60 * 1024 * 1024),
        cost_estimate=pl.CostEstimate(flops=4 * 10**9, bytes_accessed=4 * 10**6, transcendentals=0),
        name="forward",
    )(*args)


def vmem_call(kernel, outs, scratch, name, *args, far=0):
    result = pl.pallas_call(
        kernel,
        in_specs=[
            pl.BlockSpec(memory_space=pltpu.SMEM if a.dtype == jnp.int32 else pltpu.VMEM) for a in args
        ],
        out_specs=[pl.BlockSpec(memory_space=pltpu.VMEM)] * (len(outs) - far)
        + [pl.BlockSpec(memory_space=pl.ANY)] * far,
        out_shape=[jax.ShapeDtypeStruct(*o) if o[-1] == BF16 else jax.ShapeDtypeStruct(o, F32) for o in outs],
        scratch_shapes=scratch,
        compiler_params=pltpu.CompilerParams(vmem_limit_bytes=32 * 1024 * 1024),
        cost_estimate=pl.CostEstimate(flops=3 * 10**9, bytes_accessed=4 * 10**6, transcendentals=0),
        name=name,
    )(*args)
    return result if len(outs) > 1 else result[0]


Z = ("zp", "zq")
GZ = ("xl", "zq", "zp", "core")
PLANE = ("xl", "xh", "y")


def rank(block, xl):
    return 8 * xl + 4 * (block % 2) + block // 2


BLOCKS = {rank(block, xl): (block, xl) for block in range(ANGLES) for xl in range(2)}


def exchange(blocks, axes):
    return lax.all_to_all(blocks, axes, split_axis=0, concat_axis=0, tiled=True)


def swap(rows):
    return lax.ppermute(rows, "core", [(0, 1), (1, 0)])


def local(volume, probe, measured, angle_index, row_offset, col_offset):
    dft, dft_t, leaving = (jnp.asarray(t) for t in dft_tables())
    dfts = jnp.asarray(window_tables())
    factors, rows_tables, all_beams, edges, middles = (jnp.asarray(t) for t in phase_tables())
    beams = [jnp.asarray(b) for b in phase_tables()[2]]
    row = forward_call(angle_index, volume, dft, dft_t, factors, all_beams, edges)
    whole = exchange(row.reshape(ROWS, 4, W), GZ).reshape(4 * ROWS, W)
    split_modes = pltpu.VMEM((2, MODES // 2, 2 * W, 2 * W), BF16)
    waves, band_dft, band_probe = vmem_call(
        prepare_kernel,
        [(MODES // 2, 2 * W, 2 * W), ((2 * W, 2 * W), BF16), (MODES, 2, ROWS, W)],
        [split_modes],
        "prepare",
        row_offset,
        probe,
        dfts,
    )
    keep, send = vmem_call(
        window_kernel,
        [(HALF + 24, W)] * 2,
        [split_modes, pltpu.VMEM((MODES // 2, 2 * W, 2 * W), F32), pltpu.VMEM((ROWS, W), F32)],
        "window",
        row_offset,
        col_offset,
        whole,
        probe,
        measured,
        dfts,
        waves,
        band_dft,
        band_probe,
    )
    packed = vmem_call(pack_kernel, [(32 * MESSAGE, W)], [], "pack", angle_index, keep, swap(send))
    shared = exchange(packed.reshape(32, MESSAGE, 1, W), ("zp",) + PLANE).reshape(32 * MESSAGE, W)
    scratch = [pltpu.VMEM((256, W), F32), pltpu.VMEM((3, 32, W), F32)]
    relay = vmem_call(relay_kernel, [(8, PART + 32, W)], scratch, "relay", shared)
    rows = exchange(relay, Z)
    blocks = vmem_call(
        adjoint_kernel,
        [(16, CHUNK + 32, W)],
        [pltpu.VMEM((32, W), F32), pltpu.VMEM((2, N, N), BF16), pltpu.VMEM((2, N, N), BF16)],
        "adjoint",
        rows,
        dft_t,
        leaving,
        rows_tables,
        edges,
        middles,
        *beams,
    )
    final = exchange(blocks, PLANE)
    other = swap(final[:, :CHUNK, :])
    volume_update, half = vmem_call(
        assemble_kernel,
        [(1, 64, N), (2, 16, CHUNK, W)],
        [pltpu.SemaphoreType.DMA],
        "assemble",
        final,
        far=1,
    )
    core = lax.axis_index("core")
    probe_update = lax.dynamic_update_slice(half, other[None], (1 - core, 0, 0, 0))
    return volume_update, probe_update.reshape(MODES, 2, W, W)


def solution(mesh):
    split_mesh = Mesh(mesh.devices.reshape(4, 2, 2, 4, 2, 2), ("y", "xh", "xl", "zq", "zp", "core"))
    angle, gz = ("y", "xh"), GZ
    return jax.shard_map(
        local,
        mesh=split_mesh,
        in_specs=(
            P(gz, None, None),
            P(),
            P(angle, gz, None, None),
            P(angle),
            P(angle, gz),
            P(angle, gz),
        ),
        out_specs=(P(gz, angle, None), P()),
        check_vma=False,
    )
```
